32 devices in a mesh: pb: 4 (over y, core), ka: 8 (over z, x).
Axes of the slice: x: 2, y: 2, z: 4, core: 2. Of those that a mesh axis runs over, the one named last changes fastest.
Arguments:
- teacher_q: float32 [2, 3072, 256], P(None, 'ka')
- student_q: float32 [2, 3072, 128], P(None, 'ka')
Outputs:
- query_grad: float32 [2, 3072, 128], P(None, 'ka')
- loss: float32 [], replicated
All inputs are finite; a program needn't handle non-finite values.
Results may differ from the reference program's by a relative error of at most 0.00029.
Values sent between devices are 32-bit elements; how exact they have to be, the bound alone decides.
A program may use at most 64 MiB of HBM per device.

```python
import math
import jax
import jax.numpy as jnp
from jax import lax

BATCH = 2
HEADS = 1
DT = 256
DS = 128
SEQ = 3072


def draw_queries(key, columns, base):
    keys = jax.random.split(key, 3)
    position = jnp.arange(SEQ)
    normal_part = jax.random.truncated_normal(keys[0], -6.0, 6.0, (BATCH, SEQ, columns), jnp.float32)
    token_scale = jnp.exp(jax.random.uniform(keys[2], (BATCH, SEQ, 1), jnp.float32, math.log(0.3), math.log(3.0)))
    rising = 1.0 + 0.8 * position.astype(jnp.float32)[None, :, None] / SEQ
    queries = base * normal_part * token_scale * rising
    return queries


def draw_teacher_q(key, part):
    return draw_queries(jax.random.fold_in(key, 11), HEADS * DT, 0.25)


def draw_student_q(key, part):
    return draw_queries(jax.random.fold_in(key, 23), HEADS * DS, 0.3)


def setup_inputs(seed: int = 0) -> dict:
    streams_of = jax.random.split(jax.random.key(seed), 3)
    return {
        "teacher_q": draw_teacher_q(jax.random.fold_in(streams_of[2], 71), 0),
        "student_q": draw_student_q(jax.random.fold_in(streams_of[2], 71), 0),
    }


precise = lax.Precision.HIGHEST

def relation_head(teacher_head, student_head):
    row_block = math.gcd(SEQ, 512)
    number = SEQ // row_block
    teacher_factor = 1.0 / math.sqrt(DT)
    student_factor = 1.0 / math.sqrt(DS)
    teacher_blocks = teacher_head.reshape(number, row_block, DT)
    student_blocks = student_head.reshape(number, row_block, DS)

    def advance(column_grad, blocks):
        teacher_rows, student_rows = blocks
        teacher_tile = jnp.dot(teacher_rows, teacher_head.T, precision=precise, preferred_element_type=jnp.float32) * teacher_factor
        student_tile = jnp.dot(student_rows, student_head.T, precision=precise, preferred_element_type=jnp.float32) * student_factor
        teacher_max = lax.optimization_barrier(jnp.max(teacher_tile, axis=1))
        student_max = lax.optimization_barrier(jnp.max(student_tile, axis=1))
        teacher_exp = jnp.exp(teacher_tile - teacher_max[:, None])
        student_exp = jnp.exp(student_tile - student_max[:, None])
        teacher_sum = lax.optimization_barrier(jnp.sum(teacher_exp, axis=1))
        student_sum = lax.optimization_barrier(jnp.sum(student_exp, axis=1))
        cross = lax.optimization_barrier(jnp.sum(teacher_exp * (teacher_tile - student_tile), axis=1))
        divergence = cross / teacher_sum - teacher_max - jnp.log(teacher_sum) + student_max + jnp.log(student_sum)
        grad_scores = (student_exp / student_sum[:, None] - teacher_exp / teacher_sum[:, None]) / HEADS
        row_grad = jnp.dot(grad_scores, student_head, precision=precise, preferred_element_type=jnp.float32) * student_factor
        column_grad = column_grad + jnp.dot(grad_scores.T, student_rows, precision=precise, preferred_element_type=jnp.float32) * student_factor
        return (column_grad, (divergence, row_grad))
    column_grad, (divergence, row_grad) = lax.scan(advance, jnp.zeros((SEQ, DS), jnp.float32), (teacher_blocks, student_blocks))
    return (jnp.sum(divergence), row_grad.reshape(SEQ, DS) + column_grad)

def reference(teacher_q, student_q):
    sequences = []
    summed = []
    for seq_index in range(BATCH):
        gradients = []
        for head_index in range(HEADS):
            head_sum, head_grad = relation_head(teacher_q[seq_index, :, head_index * DT:(head_index + 1) * DT], student_q[seq_index, :, head_index * DS:(head_index + 1) * DS])
            gradients.append(head_grad)
            summed.append(head_sum)
        sequences.append(jnp.concatenate(gradients, axis=1))
    loss = sum(summed) / (BATCH * HEADS * SEQ)
    return (jnp.stack(sequences, axis=0), loss)
```

```python
import functools
import math

import jax
import jax.numpy as jnp
from jax import lax
from jax.experimental import pallas as pl
from jax.experimental.pallas import tpu as pltpu
from jax.sharding import PartitionSpec as P

HEADS = 1
DT = 256
DS = 128
CHUNK = 64
MESH = pl.DeviceIdType.MESH
LOG2E = 1.4426950408889634
LN2 = 0.6931471805599453


def split(values):
    high = values.astype(jnp.bfloat16)
    low = (values - high.astype(jnp.float32)).astype(jnp.bfloat16)
    return high, low


def nt(left, right):
    return lax.dot_general(
        left, right, (((1,), (1,)), ((), ())), preferred_element_type=jnp.float32
    )


def nn(left, right):
    return jnp.dot(left, right, preferred_element_type=jnp.float32)


def kernel(
    groups, levels, rows, batches,
    t_hbm, s_hbm, out_ref, loss_ref,
    own_t, own_s, nbr_t, nbr_s, col_t, col_s, row_t, row_s, t_sc, s_sc, acc,
    stat_in, level_in, wide, q_tr, w_high, w_low, part, part_in, total_in,
    load_sem, slot_sem, x_send, x_recv, z_send, z_recv,
    stat_send, stat_recv, level_send, level_recv, part_send, part_recv,
    out_send, out_recv,
):
    chunks = rows // CHUNK
    pb = lax.axis_index("pb")
    ka = lax.axis_index("ka")
    seq = pb % batches
    y = pb // batches
    z = ka // 2
    x = ka % 2
    place = x * groups + y
    low = jnp.where(seq == 0, y, groups - 1 - y)
    high = levels - 1 - low
    sources = (low, high)
    mate = y * batches + (1 - seq)
    x_device = (pb, z * 2 + (1 - x))

    planes = []
    for step in range(1, 2 * groups):
        other = (place + step) % (2 * groups)
        planes.append(((other % groups) * batches + seq, z * 2 + other // groups))
    line = [(pb, ((z + step) % levels) * 2 + x) for step in range(1, levels)]
    everyone = planes + line + [(mate, ka)]
    barrier = pltpu.get_barrier_semaphore()
    for device in everyone:
        pl.semaphore_signal(barrier, inc=1, device_id=device, device_id_type=MESH)

    loads = [
        pltpu.make_async_copy(t_hbm.at[seq], own_t, load_sem.at[0]),
        pltpu.make_async_copy(s_hbm.at[seq], own_s, load_sem.at[1]),
    ]
    for slot in range(2):
        @pl.when(z == sources[slot])
        def _():
            pltpu.make_async_copy(t_hbm.at[seq], col_t.at[slot], slot_sem.at[slot, 0]).start()
            pltpu.make_async_copy(s_hbm.at[seq], col_s.at[slot], slot_sem.at[slot, 1]).start()
    for load in loads:
        load.start()
    pl.semaphore_wait(barrier, len(everyone))

    x_copies = [
        pltpu.make_async_remote_copy(
            src_ref=src.at[seq], dst_ref=dst, send_sem=x_send.at[i], recv_sem=x_recv.at[i],
            device_id=x_device, device_id_type=MESH,
        )
        for i, (src, dst) in enumerate(((t_hbm, nbr_t), (s_hbm, nbr_s)))
    ]

    def z_copies(slot, j, way):
        step = 1 if way == 0 else -1
        span = pl.ds(pl.multiple_of(j * CHUNK, CHUNK), CHUNK)
        return [
            pltpu.make_async_remote_copy(
                src_ref=buf.at[slot, span, :], dst_ref=buf.at[slot, span, :],
                send_sem=z_send.at[way, slot, j, i], recv_sem=z_recv.at[slot, j, i],
                device_id=(pb, (z + step) * 2 + x), device_id_type=MESH,
            )
            for i, buf in enumerate((col_t, col_s))
        ]

    for slot in range(2):
        @pl.when(z == sources[slot])
        def _():
            pltpu.make_async_copy(t_hbm.at[seq], col_t.at[slot], slot_sem.at[slot, 0]).wait()
            pltpu.make_async_copy(s_hbm.at[seq], col_s.at[slot], slot_sem.at[slot, 1]).wait()

    def going(slot):
        up = jnp.logical_and(z >= sources[slot], z < levels - 1)
        down = jnp.logical_and(z <= sources[slot], z > 0)
        return ((0, up), (1, down))

    def put_rows(xb, teacher, student):
        t_high, t_low = split(teacher * (LOG2E / math.sqrt(DT)))
        s_high, s_low = split(student * (LOG2E / math.sqrt(DS)))
        row_t[xb] = jnp.concatenate([t_high, t_low, t_high], axis=1)
        row_s[xb] = jnp.concatenate([s_high, s_low, s_high], axis=1)

    def fold(values, how):
        return how(values.reshape(CHUNK // 8, 8, rows), axis=0)

    def relate(xb, slot, j):
        span = pl.ds(pl.multiple_of(j * CHUNK, CHUNK), CHUNK)
        t_high, t_low = split(col_t[slot, span, :])
        s_high, s_low = split(col_s[slot, span, :])
        teacher = nt(jnp.concatenate([t_high, t_high, t_low], axis=1), row_t[xb])
        student = nt(jnp.concatenate([s_high, s_high, s_low], axis=1), row_s[xb])
        at = pl.ds(pl.multiple_of(slot * rows + j * CHUNK, CHUNK), CHUNK)
        t_sc[xb, at, :] = teacher
        s_sc[xb, at, :] = student
        t_old, s_old = acc[xb, 0], acc[xb, 3]
        t_max = jnp.maximum(t_old, fold(teacher, jnp.max))
        s_max = jnp.maximum(s_old, fold(student, jnp.max))
        t_scale = jnp.exp2(t_old - t_max)
        s_scale = jnp.exp2(s_old - s_max)
        t_three = teacher.reshape(CHUNK // 8, 8, rows)
        s_three = student.reshape(CHUNK // 8, 8, rows)
        t_exp = jnp.exp2(t_three - t_max[None])
        s_exp = jnp.exp2(s_three - s_max[None])
        acc[xb, 0] = t_max
        acc[xb, 1] = acc[xb, 1] * t_scale + jnp.sum(t_exp, axis=0)
        acc[xb, 2] = acc[xb, 2] * t_scale + jnp.sum(t_exp * (t_three - s_three), axis=0)
        acc[xb, 3] = s_max
        acc[xb, 4] = acc[xb, 4] * s_scale + jnp.sum(s_exp, axis=0)

    for xb in range(2):
        for kind in range(5):
            start = -jnp.inf if kind in (0, 3) else 0.0
            acc[xb, kind] = jnp.full((8, rows), start, jnp.float32)

    def first_send():
        for slot in range(2):
            for way, goes in going(slot):
                @pl.when(jnp.logical_and(goes, z == sources[slot]))
                def _():
                    def send(j, carry):
                        for copy in z_copies(slot, j, way):
                            copy.start()
                        return carry
                    lax.fori_loop(0, chunks, send, 0)

    first_send()
    for copy in x_copies:
        copy.start()
    for load in loads:
        load.wait()
    put_rows(x, own_t[...], own_s[...])

    def gather(j, carry):
        for slot in range(2):
            @pl.when(z != sources[slot])
            def _():
                for copy in z_copies(slot, j, 0):
                    copy.wait_recv()
                for way, goes in going(slot):
                    @pl.when(goes)
                    def _():
                        for copy in z_copies(slot, j, way):
                            copy.start()
        for slot in range(2):
            relate(x, slot, j)
        return carry

    lax.fori_loop(0, chunks, gather, 0)
    for copy in x_copies:
        copy.wait_recv()
    put_rows(1 - x, nbr_t[...], nbr_s[...])

    def second(j, carry):
        for slot in range(2):
            relate(1 - x, slot, j)
        return carry

    lax.fori_loop(0, chunks, second, 0)

    for xb in range(2):
        t_max, s_max = acc[xb, 0], acc[xb, 3]
        t_top = jnp.max(t_max, axis=0, keepdims=True)
        s_top = jnp.max(s_max, axis=0, keepdims=True)
        t_scale = jnp.exp2(t_max - t_top)
        s_scale = jnp.exp2(s_max - s_top)
        t_sum = jnp.sum(acc[xb, 1] * t_scale, axis=0, keepdims=True)
        cross = jnp.sum(acc[xb, 2] * t_scale, axis=0, keepdims=True)
        s_sum = jnp.sum(acc[xb, 4] * s_scale, axis=0, keepdims=True)
        stat_in[place, xb] = jnp.concatenate(
            [t_top, t_sum, cross, s_top, s_sum, jnp.zeros((3, rows), jnp.float32)], axis=0
        )

    def stat_copy(step):
        return pltpu.make_async_remote_copy(
            src_ref=stat_in.at[place], dst_ref=stat_in.at[place],
            send_sem=stat_send.at[step], recv_sem=stat_recv.at[step],
            device_id=planes[step - 1], device_id_type=MESH,
        )

    def stat_wait(step):
        return pltpu.make_async_remote_copy(
            src_ref=stat_in.at[(place - step + 2 * groups) % (2 * groups)],
            dst_ref=stat_in.at[(place - step + 2 * groups) % (2 * groups)],
            send_sem=stat_send.at[step], recv_sem=stat_recv.at[step],
            device_id=planes[step - 1], device_id_type=MESH,
        )

    for step in range(1, 2 * groups):
        stat_copy(step).start()
    for slot in range(2):
        high_part, low_part = split((col_s[slot] * (1.0 / math.sqrt(DS))).T)
        q_tr[0:DS, slot * rows:(slot + 1) * rows] = high_part
        q_tr[DS:2 * DS, slot * rows:(slot + 1) * rows] = low_part
    for step in range(1, 2 * groups):
        stat_wait(step).wait_recv()

    t_max = stat_in[0, :, 0:1, :]
    s_max = stat_in[0, :, 3:4, :]
    for other in range(1, 2 * groups):
        t_max = jnp.maximum(t_max, stat_in[other, :, 0:1, :])
        s_max = jnp.maximum(s_max, stat_in[other, :, 3:4, :])
    t_sum = cross = s_sum = jnp.zeros((2, 1, rows), jnp.float32)
    for other in range(2 * groups):
        t_scale = jnp.exp2(stat_in[other, :, 0:1, :] - t_max)
        s_scale = jnp.exp2(stat_in[other, :, 3:4, :] - s_max)
        t_sum = t_sum + stat_in[other, :, 1:2, :] * t_scale
        cross = cross + stat_in[other, :, 2:3, :] * t_scale
        s_sum = s_sum + stat_in[other, :, 4:5, :] * s_scale
    t_level = t_max + jnp.log2(t_sum)
    s_level = s_max + jnp.log2(s_sum)
    divergence = LN2 * (cross / t_sum - t_level + s_level)
    both = jnp.broadcast_to(jnp.sum(divergence, axis=0), (6, rows))
    wide[...] = jnp.concatenate([t_level, s_level], axis=1)
    level_in[z] = jnp.concatenate([wide[x], both], axis=0)

    def level_copy(step, slot):
        return pltpu.make_async_remote_copy(
            src_ref=level_in.at[slot], dst_ref=level_in.at[slot],
            send_sem=level_send.at[step], recv_sem=level_recv.at[step],
            device_id=line[step - 1], device_id_type=MESH,
        )

    for step in range(1, levels):
        level_copy(step, z).start()
    for step in range(1, levels):
        level_copy(step, (z - step + levels) % levels).wait_recv()
    columns = [level_in[source].T for source in sources]

    def part_copy(step):
        other = (place + step) % (2 * groups)
        return pltpu.make_async_remote_copy(
            src_ref=part.at[other // groups], dst_ref=part_in.at[step],
            send_sem=part_send.at[step], recv_sem=part_recv.at[step],
            device_id=planes[step - 1], device_id_type=MESH,
        )

    def gradient(xb):
        rows_t = wide[xb, 0:1, :]
        rows_s = wide[xb, 1:2, :]
        for slot in range(2):
            for j in range(chunks):
                at = slice(slot * rows + j * CHUNK, slot * rows + (j + 1) * CHUNK)
                col = columns[slot][j * CHUNK:(j + 1) * CHUNK]
                teacher = t_sc[xb, at, :]
                student = s_sc[xb, at, :]
                weight = (
                    jnp.exp2(student - rows_s) + jnp.exp2(student - col[:, 1:2])
                    - jnp.exp2(teacher - rows_t) - jnp.exp2(teacher - col[:, 0:1])
                )
                high_part, low_part = split(weight)
                w_high[at, :] = high_part
                w_low[at, :] = low_part
        first = nn(q_tr[...], w_high[...])
        part[xb] = first[:DS] + first[DS:] + nn(q_tr[0:DS, :], w_low[...])

    gradient(1 - x)
    for step in range(1, 2 * groups):
        other = (place + step) % (2 * groups)
        @pl.when(other // groups != x)
        def _():
            part_copy(step).start()
    gradient(x)
    for step in range(1, 2 * groups):
        other = (place + step) % (2 * groups)
        @pl.when(other // groups == x)
        def _():
            part_copy(step).start()
    total = level_in[0, 2:3, :]
    for level in range(1, levels):
        total = total + level_in[level, 2:3, :]
    total_in[seq] = jnp.broadcast_to(total, (8, rows))
    total_copy = pltpu.make_async_remote_copy(
        src_ref=total_in.at[seq], dst_ref=total_in.at[seq],
        send_sem=out_send.at[1], recv_sem=out_recv.at[1],
        device_id=(mate, ka), device_id_type=MESH,
    )
    total_copy.start()
    result = part[x]
    for step in range(1, 2 * groups):
        part_copy(step).wait_recv()
        result = result + part_in[step]
    out_ref[seq] = result.T
    out_copy = pltpu.make_async_remote_copy(
        src_ref=out_ref.at[seq], dst_ref=out_ref.at[seq],
        send_sem=out_send.at[0], recv_sem=out_recv.at[0],
        device_id=(mate, ka), device_id_type=MESH,
    )
    out_copy.start()
    total_copy.wait_send()
    pltpu.make_async_remote_copy(
        src_ref=total_in.at[1 - seq], dst_ref=total_in.at[1 - seq],
        send_sem=out_send.at[1], recv_sem=out_recv.at[1],
        device_id=(mate, ka), device_id_type=MESH,
    ).wait_recv()
    loss_ref[0, 0] = jnp.sum(total_in[0, 0:1, :] + total_in[1, 0:1, :]) / (
        batches * HEADS * rows * 2 * levels
    )
    for copy in x_copies:
        copy.wait_send()
    for slot in range(2):
        for way, goes in going(slot):
            @pl.when(goes)
            def _():
                def done(j, carry):
                    for copy in z_copies(slot, j, way):
                        copy.wait_send()
                    return carry
                lax.fori_loop(0, chunks, done, 0)
    for step in range(1, 2 * groups):
        stat_copy(step).wait_send()
        part_copy(step).wait_send()
    for step in range(1, levels):
        level_copy(step, z).wait_send()
    out_copy.wait_send()
    pltpu.make_async_remote_copy(
        src_ref=out_ref.at[1 - seq], dst_ref=out_ref.at[1 - seq],
        send_sem=out_send.at[0], recv_sem=out_recv.at[0],
        device_id=(mate, ka), device_id_type=MESH,
    ).wait_recv()


def solution(mesh):
    def shards(teacher_q, student_q):
        batches, rows = teacher_q.shape[0], teacher_q.shape[1]
        groups = mesh.shape["pb"] // batches
        levels = mesh.shape["ka"] // 2
        chunks = rows // CHUNK
        f32, bf16 = jnp.float32, jnp.bfloat16
        dma = pltpu.SemaphoreType.DMA
        grad, loss = pl.pallas_call(
            functools.partial(kernel, groups, levels, rows, batches),
            out_shape=(
                jax.ShapeDtypeStruct((batches, rows, DS), f32),
                jax.ShapeDtypeStruct((1, 1), f32),
            ),
            in_specs=[pl.BlockSpec(memory_space=pl.ANY)] * 2,
            out_specs=(
                pl.BlockSpec(memory_space=pltpu.VMEM),
                pl.BlockSpec(memory_space=pltpu.SMEM),
            ),
            scratch_shapes=[
                pltpu.VMEM((rows, DT), f32),
                pltpu.VMEM((rows, DS), f32),
                pltpu.VMEM((rows, DT), f32),
                pltpu.VMEM((rows, DS), f32),
                pltpu.VMEM((2, rows, DT), f32),
                pltpu.VMEM((2, rows, DS), f32),
                pltpu.VMEM((2, rows, 3 * DT), bf16),
                pltpu.VMEM((2, rows, 3 * DS), bf16),
                pltpu.VMEM((2, 2 * rows, rows), f32),
                pltpu.VMEM((2, 2 * rows, rows), f32),
                pltpu.VMEM((2, 5, 8, rows), f32),
                pltpu.VMEM((2 * groups, 2, 8, rows), f32),
                pltpu.VMEM((levels, 8, rows), f32),
                pltpu.VMEM((2, 2, rows), f32),
                pltpu.VMEM((2 * DS, 2 * rows), bf16),
                pltpu.VMEM((2 * rows, rows), bf16),
                pltpu.VMEM((2 * rows, rows), bf16),
                pltpu.VMEM((2, DS, rows), f32),
                pltpu.VMEM((2 * groups, DS, rows), f32),
                pltpu.VMEM((batches, 8, rows), f32),
                dma((2,)),
                dma((2, 2)),
                dma((2,)),
                dma((2,)),
                dma((2, 2, chunks, 2)),
                dma((2, chunks, 2)),
                dma((2 * groups,)),
                dma((2 * groups,)),
                dma((levels,)),
                dma((levels,)),
                dma((2 * groups,)),
                dma((2 * groups,)),
                dma((2,)),
                dma((2,)),
            ],
            compiler_params=pltpu.CompilerParams(
                collective_id=0, has_side_effects=True, vmem_limit_bytes=48 * 1024 * 1024
            ),
        )(teacher_q, student_q)
        return grad, loss.reshape(())

    in_specs = (P(None, "ka", None), P(None, "ka", None))
    out_specs = (P(None, "ka", None), P())
    return jax.shard_map(shards, mesh=mesh, in_specs=in_specs, out_specs=out_specs, check_vma=False)
```

```python
import functools
import math

import jax
import jax.numpy as jnp
from jax import lax
from jax.experimental import pallas as pl
from jax.experimental.pallas import tpu as pltpu
from jax.sharding import PartitionSpec as P

HEADS = 1
DT = 256
DS = 128
CHUNK = 96
TILE = 64
MESH = pl.DeviceIdType.MESH
LOG2E = 1.4426950408889634
LN2 = 0.6931471805599453


def split(values):
    high = values.astype(jnp.bfloat16)
    low = (values - high.astype(jnp.float32)).astype(jnp.bfloat16)
    return high, low


def nt(left, right):
    return lax.dot_general(
        left, right, (((1,), (1,)), ((), ())), preferred_element_type=jnp.float32
    )


def nn(left, right):
    return jnp.dot(left, right, preferred_element_type=jnp.float32)


def kernel(
    groups, levels, rows, batches,
    t_hbm, s_hbm, out_ref, loss_ref,
    own_t, own_s, nbr_t, nbr_s, col_t, col_s, row_t, row_s, t_sc, s_sc, acc,
    stat_in, level_in, wide, col_level, w_row, q_tr, w_high, w_low, part, part_in, total_in,
    load_sem, slot_sem, x_send, x_recv, z_send, z_recv,
    stat_send, stat_recv, level_send, level_recv, part_send, part_recv,
    out_send, out_recv,
):
    chunks = rows // CHUNK
    pb = lax.axis_index("pb")
    ka = lax.axis_index("ka")
    seq = pb % batches
    y = pb // batches
    z = ka // 2
    x = ka % 2
    place = x * groups + y
    low = jnp.where(seq == 0, y, groups - 1 - y)
    high = levels - 1 - low
    sources = (low, high)
    mate = y * batches + (1 - seq)
    x_device = (pb, z * 2 + (1 - x))

    planes = []
    for step in range(1, 2 * groups):
        other = (place + step) % (2 * groups)
        planes.append(((other % groups) * batches + seq, z * 2 + other // groups))
    line = [(pb, ((z + step) % levels) * 2 + x) for step in range(1, levels)]
    everyone = planes + line + [(mate, ka)]
    barrier = pltpu.get_barrier_semaphore()
    for device in everyone:
        pl.semaphore_signal(barrier, inc=1, device_id=device, device_id_type=MESH)

    loads = [
        pltpu.make_async_copy(t_hbm.at[seq], own_t, load_sem.at[0]),
        pltpu.make_async_copy(s_hbm.at[seq], own_s, load_sem.at[1]),
    ]
    for slot in range(2):
        @pl.when(z == sources[slot])
        def _():
            pltpu.make_async_copy(t_hbm.at[seq], col_t.at[slot], slot_sem.at[slot, 0]).start()
            pltpu.make_async_copy(s_hbm.at[seq], col_s.at[slot], slot_sem.at[slot, 1]).start()
    for load in loads:
        load.start()
    pl.semaphore_wait(barrier, len(everyone))

    x_copies = [
        pltpu.make_async_remote_copy(
            src_ref=src.at[seq], dst_ref=dst, send_sem=x_send.at[i], recv_sem=x_recv.at[i],
            device_id=x_device, device_id_type=MESH,
        )
        for i, (src, dst) in enumerate(((t_hbm, nbr_t), (s_hbm, nbr_s)))
    ]

    def z_copies(slot, j, to):
        span = pl.ds(pl.multiple_of(j * CHUNK, CHUNK), CHUNK)
        return [
            pltpu.make_async_remote_copy(
                src_ref=buf.at[slot, span, :], dst_ref=buf.at[slot, span, :],
                send_sem=z_send.at[to, slot, j, i], recv_sem=z_recv.at[slot, j, i],
                device_id=(pb, to * 2 + x), device_id_type=MESH,
            )
            for i, buf in enumerate((col_t, col_s))
        ]

    for slot in range(2):
        @pl.when(z == sources[slot])
        def _():
            pltpu.make_async_copy(t_hbm.at[seq], col_t.at[slot], slot_sem.at[slot, 0]).wait()
            pltpu.make_async_copy(s_hbm.at[seq], col_s.at[slot], slot_sem.at[slot, 1]).wait()

    last = levels - 1

    def source_sends(slot, to):
        near = abs(z - to) == 1
        reach = (to != z) if 0 < to < last else near
        return jnp.logical_and(z == sources[slot], reach)

    def forwards(slot, to):
        beside = 1 if to == 0 else last - 1
        waits = jnp.logical_and(sources[slot] != z, sources[slot] != to)
        return jnp.logical_and(z == beside, waits)

    def put_rows(xb, teacher, student):
        t_high, t_low = split(teacher * (LOG2E / math.sqrt(DT)))
        s_high, s_low = split(student * (LOG2E / math.sqrt(DS)))
        row_t[xb] = jnp.concatenate([t_high, t_low, t_high], axis=1)
        row_s[xb] = jnp.concatenate([s_high, s_low, s_high], axis=1)

    def relate(xb, j):
        span = pl.ds(pl.multiple_of(j * CHUNK, CHUNK), CHUNK)
        t_high, t_low = split(col_t[:, span, :].reshape(2 * CHUNK, DT))
        s_high, s_low = split(col_s[:, span, :].reshape(2 * CHUNK, DS))
        teacher = nt(jnp.concatenate([t_high, t_high, t_low], axis=1), row_t[xb])
        student = nt(jnp.concatenate([s_high, s_high, s_low], axis=1), row_s[xb])
        for slot in range(2):
            at = pl.ds(pl.multiple_of(slot * rows + j * CHUNK, CHUNK), CHUNK)
            t_sc[xb, at, :] = teacher[slot * CHUNK:(slot + 1) * CHUNK]
            s_sc[xb, at, :] = student[slot * CHUNK:(slot + 1) * CHUNK]
        t_three = teacher.reshape(2 * CHUNK // 8, 8, rows)
        s_three = student.reshape(2 * CHUNK // 8, 8, rows)
        t_old, s_old = acc[xb, 0], acc[xb, 3]
        t_max = jnp.maximum(t_old, jnp.max(t_three, axis=0))
        s_max = jnp.maximum(s_old, jnp.max(s_three, axis=0))
        t_scale = jnp.exp2(t_old - t_max)
        s_scale = jnp.exp2(s_old - s_max)
        t_exp = jnp.exp2(t_three - t_max[None])
        s_exp = jnp.exp2(s_three - s_max[None])
        acc[xb, 0] = t_max
        acc[xb, 1] = acc[xb, 1] * t_scale + jnp.sum(t_exp, axis=0)
        acc[xb, 2] = acc[xb, 2] * t_scale + jnp.sum(t_exp * (t_three - s_three), axis=0)
        acc[xb, 3] = s_max
        acc[xb, 4] = acc[xb, 4] * s_scale + jnp.sum(s_exp, axis=0)

    for xb in range(2):
        for kind in range(5):
            start = -jnp.inf if kind in (0, 3) else 0.0
            acc[xb, kind] = jnp.full((8, rows), start, jnp.float32)

    for copy in x_copies:
        copy.start()

    def first_send(j, carry):
        for slot in range(2):
            for to in range(levels):
                @pl.when(source_sends(slot, to))
                def _():
                    for copy in z_copies(slot, j, to):
                        copy.start()
        return carry

    lax.fori_loop(0, chunks, first_send, 0)
    for load in loads:
        load.wait()
    put_rows(x, own_t[...], own_s[...])
    half = chunks // 2

    def gather(j, carry):
        for slot in range(2):
            @pl.when(z != sources[slot])
            def _():
                for copy in z_copies(slot, j, 1):
                    copy.wait_recv()
                for to in (0, last):
                    @pl.when(forwards(slot, to))
                    def _():
                        for copy in z_copies(slot, j, to):
                            copy.start()

        relate(x, j)

        @pl.when(j == half)
        def _():
            for copy in x_copies:
                copy.wait_recv()
            put_rows(1 - x, nbr_t[...], nbr_s[...])

        @pl.when(j >= half)
        def _():
            relate(1 - x, j - half)
            relate(1 - x, j)
        return carry

    lax.fori_loop(0, chunks, gather, 0)

    for xb in range(2):
        t_max, s_max = acc[xb, 0], acc[xb, 3]
        t_top = jnp.max(t_max, axis=0, keepdims=True)
        s_top = jnp.max(s_max, axis=0, keepdims=True)
        t_scale = jnp.exp2(t_max - t_top)
        s_scale = jnp.exp2(s_max - s_top)
        t_sum = jnp.sum(acc[xb, 1] * t_scale, axis=0, keepdims=True)
        cross = jnp.sum(acc[xb, 2] * t_scale, axis=0, keepdims=True)
        s_sum = jnp.sum(acc[xb, 4] * s_scale, axis=0, keepdims=True)
        stat_in[place, xb] = jnp.concatenate(
            [t_top, t_sum, cross, s_top, s_sum, jnp.zeros((3, rows), jnp.float32)], axis=0
        )

    def stat_copy(step):
        return pltpu.make_async_remote_copy(
            src_ref=stat_in.at[place], dst_ref=stat_in.at[place],
            send_sem=stat_send.at[step], recv_sem=stat_recv.at[step],
            device_id=planes[step - 1], device_id_type=MESH,
        )

    def stat_wait(step):
        return pltpu.make_async_remote_copy(
            src_ref=stat_in.at[(place - step + 2 * groups) % (2 * groups)],
            dst_ref=stat_in.at[(place - step + 2 * groups) % (2 * groups)],
            send_sem=stat_send.at[step], recv_sem=stat_recv.at[step],
            device_id=planes[step - 1], device_id_type=MESH,
        )

    for step in range(1, 2 * groups):
        stat_copy(step).start()
    for slot in range(2):
        high_part, low_part = split((col_s[slot] * (1.0 / math.sqrt(DS))).T)
        q_tr[0:DS, slot * rows:(slot + 1) * rows] = high_part
        q_tr[DS:2 * DS, slot * rows:(slot + 1) * rows] = low_part
    for step in range(1, 2 * groups):
        stat_wait(step).wait_recv()

    t_max = stat_in[0, :, 0:1, :]
    s_max = stat_in[0, :, 3:4, :]
    for other in range(1, 2 * groups):
        t_max = jnp.maximum(t_max, stat_in[other, :, 0:1, :])
        s_max = jnp.maximum(s_max, stat_in[other, :, 3:4, :])
    t_sum = cross = s_sum = jnp.zeros((2, 1, rows), jnp.float32)
    for other in range(2 * groups):
        t_scale = jnp.exp2(stat_in[other, :, 0:1, :] - t_max)
        s_scale = jnp.exp2(stat_in[other, :, 3:4, :] - s_max)
        t_sum = t_sum + stat_in[other, :, 1:2, :] * t_scale
        cross = cross + stat_in[other, :, 2:3, :] * t_scale
        s_sum = s_sum + stat_in[other, :, 4:5, :] * s_scale
    t_level = t_max + jnp.log2(t_sum)
    s_level = s_max + jnp.log2(s_sum)
    divergence = LN2 * (cross / t_sum - t_level + s_level)
    both = jnp.broadcast_to(jnp.sum(divergence, axis=0), (6, rows))
    wide[...] = jnp.concatenate([t_level, s_level], axis=1)
    level_in[z] = jnp.concatenate([wide[x], both], axis=0)

    def level_copy(step, slot):
        return pltpu.make_async_remote_copy(
            src_ref=level_in.at[slot], dst_ref=level_in.at[slot],
            send_sem=level_send.at[step], recv_sem=level_recv.at[step],
            device_id=line[step - 1], device_id_type=MESH,
        )

    for step in range(1, levels):
        level_copy(step, z).start()
    tiles = 2 * rows // TILE

    def row_weights(xb):
        rows_t = wide[xb, 0:1, :]
        rows_s = wide[xb, 1:2, :]

        def tile(j, carry):
            at = pl.ds(pl.multiple_of(j * TILE, TILE), TILE)
            w_row[xb, at, :] = jnp.exp2(s_sc[xb, at, :] - rows_s) - jnp.exp2(t_sc[xb, at, :] - rows_t)
            return carry

        lax.fori_loop(0, tiles, tile, 0)

    row_weights(1 - x)
    row_weights(x)
    for step in range(1, levels):
        level_copy(step, (z - step + levels) % levels).wait_recv()
    for slot in range(2):
        col_level[slot * rows:(slot + 1) * rows, :] = level_in[sources[slot]].T

    def part_copy(step):
        other = (place + step) % (2 * groups)
        return pltpu.make_async_remote_copy(
            src_ref=part.at[other // groups], dst_ref=part_in.at[step],
            send_sem=part_send.at[step], recv_sem=part_recv.at[step],
            device_id=planes[step - 1], device_id_type=MESH,
        )

    def gradient(xb):
        def tile(j, carry):
            at = pl.ds(pl.multiple_of(j * TILE, TILE), TILE)
            col = col_level[at, :]
            weight = (
                w_row[xb, at, :]
                + jnp.exp2(s_sc[xb, at, :] - col[:, 1:2])
                - jnp.exp2(t_sc[xb, at, :] - col[:, 0:1])
            )
            high_part, low_part = split(weight)
            w_high[at, :] = high_part
            w_low[at, :] = low_part
            return carry

        lax.fori_loop(0, tiles, tile, 0)
        first = nn(q_tr[...], w_high[...])
        part[xb] = first[:DS] + first[DS:] + nn(q_tr[0:DS, :], w_low[...])

    gradient(1 - x)
    for step in range(1, 2 * groups):
        other = (place + step) % (2 * groups)
        @pl.when(other // groups != x)
        def _():
            part_copy(step).start()
    gradient(x)
    for step in range(1, 2 * groups):
        other = (place + step) % (2 * groups)
        @pl.when(other // groups == x)
        def _():
            part_copy(step).start()
    total = level_in[0, 2:3, :]
    for level in range(1, levels):
        total = total + level_in[level, 2:3, :]
    total_in[seq] = jnp.broadcast_to(total, (8, rows))
    total_copy = pltpu.make_async_remote_copy(
        src_ref=total_in.at[seq], dst_ref=total_in.at[seq],
        send_sem=out_send.at[1], recv_sem=out_recv.at[1],
        device_id=(mate, ka), device_id_type=MESH,
    )
    total_copy.start()
    result = part[x]
    for step in range(1, 2 * groups):
        part_copy(step).wait_recv()
        result = result + part_in[step]
    out_ref[seq] = result.T
    out_copy = pltpu.make_async_remote_copy(
        src_ref=out_ref.at[seq], dst_ref=out_ref.at[seq],
        send_sem=out_send.at[0], recv_sem=out_recv.at[0],
        device_id=(mate, ka), device_id_type=MESH,
    )
    out_copy.start()
    total_copy.wait_send()
    pltpu.make_async_remote_copy(
        src_ref=total_in.at[1 - seq], dst_ref=total_in.at[1 - seq],
        send_sem=out_send.at[1], recv_sem=out_recv.at[1],
        device_id=(mate, ka), device_id_type=MESH,
    ).wait_recv()
    loss_ref[0, 0] = jnp.sum(total_in[0, 0:1, :] + total_in[1, 0:1, :]) / (
        batches * HEADS * rows * 2 * levels
    )
    for copy in x_copies:
        copy.wait_send()

    def sent(j, carry):
        for slot in range(2):
            for to in range(levels):
                goes = source_sends(slot, to)
                if to in (0, last):
                    goes = jnp.logical_or(goes, forwards(slot, to))

                @pl.when(goes)
                def _():
                    for copy in z_copies(slot, j, to):
                        copy.wait_send()
        return carry

    lax.fori_loop(0, chunks, sent, 0)
    for step in range(1, 2 * groups):
        stat_copy(step).wait_send()
        part_copy(step).wait_send()
    for step in range(1, levels):
        level_copy(step, z).wait_send()
    out_copy.wait_send()
    pltpu.make_async_remote_copy(
        src_ref=out_ref.at[1 - seq], dst_ref=out_ref.at[1 - seq],
        send_sem=out_send.at[0], recv_sem=out_recv.at[0],
        device_id=(mate, ka), device_id_type=MESH,
    ).wait_recv()


def solution(mesh):
    def shards(teacher_q, student_q):
        batches, rows = teacher_q.shape[0], teacher_q.shape[1]
        groups = mesh.shape["pb"] // batches
        levels = mesh.shape["ka"] // 2
        chunks = rows // CHUNK
        f32, bf16 = jnp.float32, jnp.bfloat16
        dma = pltpu.SemaphoreType.DMA
        grad, loss = pl.pallas_call(
            functools.partial(kernel, groups, levels, rows, batches),
            out_shape=(
                jax.ShapeDtypeStruct((batches, rows, DS), f32),
                jax.ShapeDtypeStruct((1, 1), f32),
            ),
            in_specs=[pl.BlockSpec(memory_space=pl.ANY)] * 2,
            out_specs=(
                pl.BlockSpec(memory_space=pltpu.VMEM),
                pl.BlockSpec(memory_space=pltpu.SMEM),
            ),
            scratch_shapes=[
                pltpu.VMEM((rows, DT), f32),
                pltpu.VMEM((rows, DS), f32),
                pltpu.VMEM((rows, DT), f32),
                pltpu.VMEM((rows, DS), f32),
                pltpu.VMEM((2, rows, DT), f32),
                pltpu.VMEM((2, rows, DS), f32),
                pltpu.VMEM((2, rows, 3 * DT), bf16),
                pltpu.VMEM((2, rows, 3 * DS), bf16),
                pltpu.VMEM((2, 2 * rows, rows), f32),
                pltpu.VMEM((2, 2 * rows, rows), f32),
                pltpu.VMEM((2, 5, 8, rows), f32),
                pltpu.VMEM((2 * groups, 2, 8, rows), f32),
                pltpu.VMEM((levels, 8, rows), f32),
                pltpu.VMEM((2, 2, rows), f32),
                pltpu.VMEM((2 * rows, 8), f32),
                pltpu.VMEM((2, 2 * rows, rows), f32),
                pltpu.VMEM((2 * DS, 2 * rows), bf16),
                pltpu.VMEM((2 * rows, rows), bf16),
                pltpu.VMEM((2 * rows, rows), bf16),
                pltpu.VMEM((2, DS, rows), f32),
                pltpu.VMEM((2 * groups, DS, rows), f32),
                pltpu.VMEM((batches, 8, rows), f32),
                dma((2,)),
                dma((2, 2)),
                dma((2,)),
                dma((2,)),
                dma((levels, 2, chunks, 2)),
                dma((2, chunks, 2)),
                dma((2 * groups,)),
                dma((2 * groups,)),
                dma((levels,)),
                dma((levels,)),
                dma((2 * groups,)),
                dma((2 * groups,)),
                dma((2,)),
                dma((2,)),
            ],
            compiler_params=pltpu.CompilerParams(
                collective_id=0, has_side_effects=True, vmem_limit_bytes=60 * 1024 * 1024
            ),
        )(teacher_q, student_q)
        return grad, loss.reshape(())

    in_specs = (P(None, "ka", None), P(None, "ka", None))
    out_specs = (P(None, "ka", None), P())
    return jax.shard_map(shards, mesh=mesh, in_specs=in_specs, out_specs=out_specs, check_vma=False)
```

```python
import functools
import math

import jax
import jax.numpy as jnp
from jax import lax
from jax.experimental import pallas as pl
from jax.experimental.pallas import tpu as pltpu
from jax.sharding import PartitionSpec as P

HEADS = 1
DT = 256
DS = 128
CHUNK = 64
LANES = 128
TILE = 64
MESH = pl.DeviceIdType.MESH
LOG2E = 1.4426950408889634
LN2 = 0.6931471805599453


def split(values):
    high = values.astype(jnp.bfloat16)
    low = (values - high.astype(jnp.float32)).astype(jnp.bfloat16)
    return high, low


def nt(left, right):
    return lax.dot_general(
        left, right, (((1,), (1,)), ((), ())), preferred_element_type=jnp.float32
    )


def nn(left, right):
    return jnp.dot(left, right, preferred_element_type=jnp.float32)


def kernel(
    groups, levels, rows, batches,
    t_hbm, s_hbm, out_ref, loss_ref,
    own_t, own_s, nbr_t, nbr_s, col_t, col_s, row_t, row_s, t_sc, s_sc, acc,
    stat_in, stat_col, div_in, wide, col_level, w_row, q_tr, w_high, w_low,
    part, x_in, x_sum, y_in, total_in,
    load_sem, slot_sem, x_send, x_recv, z_send, z_recv,
    stat_send, stat_recv, col_send, col_recv, div_send, div_recv,
    px_send, px_recv, py_send, py_recv, out_send, out_recv, total_send, total_recv,
):
    chunks = rows // CHUNK
    pb = lax.axis_index("pb")
    ka = lax.axis_index("ka")
    seq = pb % batches
    y = pb // batches
    z = ka // 2
    x = ka % 2
    place = x * groups + y
    low = jnp.where(seq == 0, y, groups - 1 - y)
    high = levels - 1 - low
    sources = (low, high)
    mate = y * batches + (1 - seq)
    x_device = (pb, z * 2 + (1 - x))

    planes = []
    for step in range(1, 2 * groups):
        other = (place + step) % (2 * groups)
        planes.append(((other % groups) * batches + seq, z * 2 + other // groups))
    line = [(pb, ((z + step) % levels) * 2 + x) for step in range(1, levels)]
    barrier = pltpu.get_barrier_semaphore()
    count = 2 * groups * levels
    index = place * levels + z

    def greet(step, carry):
        other = (index + step) % count
        spot, level = other // levels, other % levels
        device = ((spot % groups) * batches + seq, level * 2 + spot // groups)
        pl.semaphore_signal(barrier, inc=1, device_id=device, device_id_type=MESH)
        return carry

    lax.fori_loop(1, count, greet, 0)
    pl.semaphore_signal(barrier, inc=1, device_id=(mate, ka), device_id_type=MESH)

    loads = [
        pltpu.make_async_copy(t_hbm.at[seq], own_t, load_sem.at[0]),
        pltpu.make_async_copy(s_hbm.at[seq], own_s, load_sem.at[1]),
    ]
    for slot in range(2):
        @pl.when(z == sources[slot])
        def _():
            pltpu.make_async_copy(t_hbm.at[seq], col_t.at[slot], slot_sem.at[slot, 0]).start()
            pltpu.make_async_copy(s_hbm.at[seq], col_s.at[slot], slot_sem.at[slot, 1]).start()
    for load in loads:
        load.start()
    pl.semaphore_wait(barrier, count)

    x_copies = [
        pltpu.make_async_remote_copy(
            src_ref=src.at[seq], dst_ref=dst, send_sem=x_send.at[i], recv_sem=x_recv.at[i],
            device_id=x_device, device_id_type=MESH,
        )
        for i, (src, dst) in enumerate(((t_hbm, nbr_t), (s_hbm, nbr_s)))
    ]

    def z_copies(slot, j, to):
        span = pl.ds(pl.multiple_of(j * CHUNK, CHUNK), CHUNK)
        return [
            pltpu.make_async_remote_copy(
                src_ref=buf.at[slot, span, :], dst_ref=buf.at[slot, span, :],
                send_sem=z_send.at[to, slot, j, i], recv_sem=z_recv.at[slot, j, i],
                device_id=(pb, to * 2 + x), device_id_type=MESH,
            )
            for i, buf in enumerate((col_t, col_s))
        ]

    for slot in range(2):
        @pl.when(z == sources[slot])
        def _():
            pltpu.make_async_copy(t_hbm.at[seq], col_t.at[slot], slot_sem.at[slot, 0]).wait()
            pltpu.make_async_copy(s_hbm.at[seq], col_s.at[slot], slot_sem.at[slot, 1]).wait()

    last = levels - 1

    def source_sends(slot, to):
        near = abs(z - to) == 1
        reach = (to != z) if 0 < to < last else near
        return jnp.logical_and(z == sources[slot], reach)

    def forwards(slot, to):
        beside = 1 if to == 0 else last - 1
        waits = jnp.logical_and(sources[slot] != z, sources[slot] != to)
        return jnp.logical_and(z == beside, waits)

    def put_rows(xb, teacher, student):
        t_high, t_low = split(teacher * (LOG2E / math.sqrt(DT)))
        s_high, s_low = split(student * (LOG2E / math.sqrt(DS)))
        row_t[xb] = jnp.concatenate([t_high, t_low, t_high], axis=1)
        row_s[xb] = jnp.concatenate([s_high, s_low, s_high], axis=1)

    def relate(xb, j):
        span = pl.ds(pl.multiple_of(j * CHUNK, CHUNK), CHUNK)
        t_high, t_low = split(col_t[:, span, :].reshape(2 * CHUNK, DT))
        s_high, s_low = split(col_s[:, span, :].reshape(2 * CHUNK, DS))
        teacher = nt(jnp.concatenate([t_high, t_high, t_low], axis=1), row_t[xb])
        student = nt(jnp.concatenate([s_high, s_high, s_low], axis=1), row_s[xb])
        for slot in range(2):
            at = pl.ds(pl.multiple_of(slot * rows + j * CHUNK, CHUNK), CHUNK)
            t_sc[xb, at, :] = teacher[slot * CHUNK:(slot + 1) * CHUNK]
            s_sc[xb, at, :] = student[slot * CHUNK:(slot + 1) * CHUNK]
        t_three = teacher.reshape(2 * CHUNK // 8, 8, rows)
        s_three = student.reshape(2 * CHUNK // 8, 8, rows)
        t_old, s_old = acc[xb, 0], acc[xb, 3]
        t_max = jnp.maximum(t_old, jnp.max(t_three, axis=0))
        s_max = jnp.maximum(s_old, jnp.max(s_three, axis=0))
        t_scale = jnp.exp2(t_old - t_max)
        s_scale = jnp.exp2(s_old - s_max)
        t_exp = jnp.exp2(t_three - t_max[None])
        s_exp = jnp.exp2(s_three - s_max[None])
        acc[xb, 0] = t_max
        acc[xb, 1] = acc[xb, 1] * t_scale + jnp.sum(t_exp, axis=0)
        acc[xb, 2] = acc[xb, 2] * t_scale + jnp.sum(t_exp * (t_three - s_three), axis=0)
        acc[xb, 3] = s_max
        acc[xb, 4] = acc[xb, 4] * s_scale + jnp.sum(s_exp, axis=0)

    for xb in range(2):
        for kind in range(5):
            start = -jnp.inf if kind in (0, 3) else 0.0
            acc[xb, kind] = jnp.full((8, rows), start, jnp.float32)

    for copy in x_copies:
        copy.start()

    def first_send(j, carry):
        for slot in range(2):
            for to in range(levels):
                @pl.when(source_sends(slot, to))
                def _():
                    for copy in z_copies(slot, j, to):
                        copy.start()
        return carry

    lax.fori_loop(0, chunks, first_send, 0)
    for load in loads:
        load.wait()
    put_rows(x, own_t[...], own_s[...])
    half = chunks // 2

    def gather(j, carry):
        @pl.when(j == half)
        def _():
            for copy in x_copies:
                copy.wait_recv()
            put_rows(1 - x, nbr_t[...], nbr_s[...])

        @pl.when(j >= half)
        def _():
            relate(1 - x, j - half)

        for slot in range(2):
            @pl.when(z != sources[slot])
            def _():
                for copy in z_copies(slot, j, 1):
                    copy.wait_recv()
                for to in (0, last):
                    @pl.when(forwards(slot, to))
                    def _():
                        for copy in z_copies(slot, j, to):
                            copy.start()

        relate(x, j)

        @pl.when(j >= half)
        def _():
            relate(1 - x, j)
        return carry

    lax.fori_loop(0, chunks, gather, 0)

    for xb in range(2):
        t_max, s_max = acc[xb, 0], acc[xb, 3]
        t_top = jnp.max(t_max, axis=0, keepdims=True)
        s_top = jnp.max(s_max, axis=0, keepdims=True)
        t_scale = jnp.exp2(t_max - t_top)
        s_scale = jnp.exp2(s_max - s_top)
        t_sum = jnp.sum(acc[xb, 1] * t_scale, axis=0, keepdims=True)
        cross = jnp.sum(acc[xb, 2] * t_scale, axis=0, keepdims=True)
        s_sum = jnp.sum(acc[xb, 4] * s_scale, axis=0, keepdims=True)
        stat_in[place, xb] = jnp.concatenate(
            [t_top, t_sum, cross, s_top, s_sum, jnp.zeros((3, rows), jnp.float32)], axis=0
        )

    def stat_copy(step):
        return pltpu.make_async_remote_copy(
            src_ref=stat_in.at[place], dst_ref=stat_in.at[place],
            send_sem=stat_send.at[step], recv_sem=stat_recv.at[step],
            device_id=planes[step - 1], device_id_type=MESH,
        )

    def stat_wait(step):
        return pltpu.make_async_remote_copy(
            src_ref=stat_in.at[(place - step + 2 * groups) % (2 * groups)],
            dst_ref=stat_in.at[(place - step + 2 * groups) % (2 * groups)],
            send_sem=stat_send.at[step], recv_sem=stat_recv.at[step],
            device_id=planes[step - 1], device_id_type=MESH,
        )

    near = jnp.minimum(z, levels - 1 - z)
    user = jnp.where(seq == 0, near, groups - 1 - near)
    my_slot = jnp.where(z == near, 0, 1)

    def col_copy(xb, step):
        return pltpu.make_async_remote_copy(
            src_ref=stat_in.at[place, xb], dst_ref=stat_col.at[my_slot, place],
            send_sem=col_send.at[xb, step], recv_sem=col_recv.at[my_slot, place],
            device_id=(user * batches + seq, ((z + step) % levels) * 2 + xb), device_id_type=MESH,
        )

    for step in range(1, levels):
        for xb in range(2):
            col_copy(xb, step).start()
    for step in range(1, 2 * groups):
        stat_copy(step).start()
    for slot in range(2):
        high_part, low_part = split((col_s[slot] * (1.0 / math.sqrt(DS))).T)
        q_tr[0:DS, slot * rows:(slot + 1) * rows] = high_part
        q_tr[DS:2 * DS, slot * rows:(slot + 1) * rows] = low_part
    for step in range(1, 2 * groups):
        stat_wait(step).wait_recv()

    def combine(stats):
        t_max = functools.reduce(jnp.maximum, [stat[0:1] for stat in stats])
        s_max = functools.reduce(jnp.maximum, [stat[3:4] for stat in stats])
        t_sum = cross = s_sum = jnp.zeros((1, rows), jnp.float32)
        for stat in stats:
            t_scale = jnp.exp2(stat[0:1] - t_max)
            t_sum = t_sum + stat[1:2] * t_scale
            cross = cross + stat[2:3] * t_scale
            s_sum = s_sum + stat[4:5] * jnp.exp2(stat[3:4] - s_max)
        t_level = t_max + jnp.log2(t_sum)
        s_level = s_max + jnp.log2(s_sum)
        return t_level, s_level, LN2 * (cross / t_sum - t_level + s_level)

    divergence = jnp.zeros((1, rows), jnp.float32)
    for xb in range(2):
        t_level, s_level, share = combine([stat_in[other, xb] for other in range(2 * groups)])
        wide[xb] = jnp.concatenate([t_level, s_level], axis=0)
        divergence = divergence + share
    div_in[z] = jnp.broadcast_to(divergence, (8, rows))

    def div_copy(step, slot):
        return pltpu.make_async_remote_copy(
            src_ref=div_in.at[slot], dst_ref=div_in.at[slot],
            send_sem=div_send.at[step], recv_sem=div_recv.at[step],
            device_id=line[step - 1], device_id_type=MESH,
        )

    for step in range(1, levels):
        div_copy(step, z).start()

    tiles = 2 * rows // TILE

    def row_weights(xb):
        rows_t = wide[xb, 0:1, :]
        rows_s = wide[xb, 1:2, :]

        def tile(j, carry):
            at = pl.ds(pl.multiple_of(j * TILE, TILE), TILE)
            w_row[xb, at, :] = jnp.exp2(s_sc[xb, at, :] - rows_s) - jnp.exp2(t_sc[xb, at, :] - rows_t)
            return carry

        lax.fori_loop(0, tiles, tile, 0)

    row_weights(1 - x)
    row_weights(x)
    for slot in range(2):
        @pl.when(z == sources[slot])
        def _():
            for other in range(2 * groups):
                stat_col[slot, other] = stat_in[other, x]

        @pl.when(z != sources[slot])
        def _():
            for other in range(2 * groups):
                pltpu.make_async_remote_copy(
                    src_ref=stat_col.at[slot, other], dst_ref=stat_col.at[slot, other],
                    send_sem=col_send.at[0, 0], recv_sem=col_recv.at[slot, other],
                    device_id=x_device, device_id_type=MESH,
                ).wait_recv()

        t_level, s_level, _ = combine([stat_col[slot, other] for other in range(2 * groups)])
        both = jnp.concatenate([t_level, s_level, jnp.zeros((6, rows), jnp.float32)], axis=0)
        col_level[slot * rows:(slot + 1) * rows, :] = both.T

    blocks = rows // LANES

    def px_copy(b):
        return pltpu.make_async_remote_copy(
            src_ref=part.at[1 - x, b], dst_ref=x_in.at[b],
            send_sem=px_send.at[b], recv_sem=px_recv.at[b],
            device_id=x_device, device_id_type=MESH,
        )

    def py_copy(step, b):
        return pltpu.make_async_remote_copy(
            src_ref=x_sum.at[b], dst_ref=y_in.at[step, b],
            send_sem=py_send.at[step, b], recv_sem=py_recv.at[step, b],
            device_id=(((y + step) % groups) * batches + seq, ka), device_id_type=MESH,
        )

    def out_copy(which, b):
        span = pl.ds(b * LANES, LANES)
        return pltpu.make_async_remote_copy(
            src_ref=out_ref.at[which, span, :], dst_ref=out_ref.at[which, span, :],
            send_sem=out_send.at[b], recv_sem=out_recv.at[b],
            device_id=(mate, ka), device_id_type=MESH,
        )

    def total_copy(which):
        return pltpu.make_async_remote_copy(
            src_ref=total_in.at[which], dst_ref=total_in.at[which],
            send_sem=total_send, recv_sem=total_recv,
            device_id=(mate, ka), device_id_type=MESH,
        )

    def gradient(xb):
        def tile(j, carry):
            at = pl.ds(pl.multiple_of(j * TILE, TILE), TILE)
            col = col_level[at, :]
            weight = (
                w_row[xb, at, :]
                + jnp.exp2(s_sc[xb, at, :] - col[:, 1:2])
                - jnp.exp2(t_sc[xb, at, :] - col[:, 0:1])
            )
            high_part, low_part = split(weight)
            w_high[at, :] = high_part
            w_low[at, :] = low_part
            return carry

        lax.fori_loop(0, tiles, tile, 0)
        first = nn(q_tr[...], w_high[...])
        product = first[:DS] + first[DS:] + nn(q_tr[0:DS, :], w_low[...])
        for b in range(blocks):
            part[xb, b] = product[:, b * LANES:(b + 1) * LANES]

    gradient(1 - x)
    for b in range(blocks):
        px_copy(b).start()
    gradient(x)
    for b in range(blocks):
        px_copy(b).wait_recv()
        x_sum[b] = part[x, b] + x_in[b]
        for step in range(1, groups):
            py_copy(step, b).start()
    for step in range(1, levels):
        div_copy(step, (z - step + levels) % levels).wait_recv()
    total = div_in[0, 0:1, :]
    for level in range(1, levels):
        total = total + div_in[level, 0:1, :]
    total_in[seq] = jnp.broadcast_to(total, (8, rows))
    total_copy(seq).start()
    for b in range(blocks):
        result = x_sum[b]
        for step in range(1, groups):
            py_copy(step, b).wait_recv()
            result = result + y_in[step, b]
        out_ref[seq, b * LANES:(b + 1) * LANES, :] = result.T
        out_copy(seq, b).start()
    total_copy(1 - seq).wait_recv()
    loss_ref[0, 0] = jnp.sum(total_in[0, 0:1, :] + total_in[1, 0:1, :]) / (
        batches * HEADS * rows * 2 * levels
    )
    total_copy(seq).wait_send()
    for copy in x_copies:
        copy.wait_send()

    def sent(j, carry):
        for slot in range(2):
            for to in range(levels):
                goes = source_sends(slot, to)
                if to in (0, last):
                    goes = jnp.logical_or(goes, forwards(slot, to))

                @pl.when(goes)
                def _():
                    for copy in z_copies(slot, j, to):
                        copy.wait_send()
        return carry

    lax.fori_loop(0, chunks, sent, 0)
    for step in range(1, 2 * groups):
        stat_copy(step).wait_send()
    for step in range(1, levels):
        div_copy(step, z).wait_send()
        for xb in range(2):
            col_copy(xb, step).wait_send()
    for b in range(blocks):
        px_copy(b).wait_send()
        for step in range(1, groups):
            py_copy(step, b).wait_send()
        out_copy(seq, b).wait_send()
        out_copy(1 - seq, b).wait_recv()


def solution(mesh):
    def shards(teacher_q, student_q):
        batches, rows = teacher_q.shape[0], teacher_q.shape[1]
        groups = mesh.shape["pb"] // batches
        levels = mesh.shape["ka"] // 2
        chunks = rows // CHUNK
        blocks = rows // LANES
        f32, bf16 = jnp.float32, jnp.bfloat16
        dma = pltpu.SemaphoreType.DMA
        grad, loss = pl.pallas_call(
            functools.partial(kernel, groups, levels, rows, batches),
            out_shape=(
                jax.ShapeDtypeStruct((batches, rows, DS), f32),
                jax.ShapeDtypeStruct((1, 1), f32),
            ),
            in_specs=[pl.BlockSpec(memory_space=pl.ANY)] * 2,
            out_specs=(
                pl.BlockSpec(memory_space=pltpu.VMEM),
                pl.BlockSpec(memory_space=pltpu.SMEM),
            ),
            scratch_shapes=[
                pltpu.VMEM((rows, DT), f32),
                pltpu.VMEM((rows, DS), f32),
                pltpu.VMEM((rows, DT), f32),
                pltpu.VMEM((rows, DS), f32),
                pltpu.VMEM((2, rows, DT), f32),
                pltpu.VMEM((2, rows, DS), f32),
                pltpu.VMEM((2, rows, 3 * DT), bf16),
                pltpu.VMEM((2, rows, 3 * DS), bf16),
                pltpu.VMEM((2, 2 * rows, rows), f32),
                pltpu.VMEM((2, 2 * rows, rows), f32),
                pltpu.VMEM((2, 5, 8, rows), f32),
                pltpu.VMEM((2 * groups, 2, 8, rows), f32),
                pltpu.VMEM((2, 2 * groups, 8, rows), f32),
                pltpu.VMEM((levels, 8, rows), f32),
                pltpu.VMEM((2, 2, rows), f32),
                pltpu.VMEM((2 * rows, 8), f32),
                pltpu.VMEM((2, 2 * rows, rows), f32),
                pltpu.VMEM((2 * DS, 2 * rows), bf16),
                pltpu.VMEM((2 * rows, rows), bf16),
                pltpu.VMEM((2 * rows, rows), bf16),
                pltpu.VMEM((2, blocks, DS, LANES), f32),
                pltpu.VMEM((blocks, DS, LANES), f32),
                pltpu.VMEM((blocks, DS, LANES), f32),
                pltpu.VMEM((groups, blocks, DS, LANES), f32),
                pltpu.VMEM((batches, 8, rows), f32),
                dma((2,)),
                dma((2, 2)),
                dma((2,)),
                dma((2,)),
                dma((levels, 2, chunks, 2)),
                dma((2, chunks, 2)),
                dma((2 * groups,)),
                dma((2 * groups,)),
                dma((2, levels)),
                dma((2, 2 * groups)),
                dma((levels,)),
                dma((levels,)),
                dma((blocks,)),
                dma((blocks,)),
                dma((groups, blocks)),
                dma((groups, blocks)),
                dma((blocks,)),
                dma((blocks,)),
                dma,
                dma,
            ],
            compiler_params=pltpu.CompilerParams(
                collective_id=0, has_side_effects=True, vmem_limit_bytes=60 * 1024 * 1024
            ),
        )(teacher_q, student_q)
        return grad, loss.reshape(())

    in_specs = (P(None, "ka", None), P(None, "ka", None))
    out_specs = (P(None, "ka", None), P())
    return jax.shard_map(shards, mesh=mesh, in_specs=in_specs, out_specs=out_specs, check_vma=False)
```

```python
import functools
import math

import jax
import jax.numpy as jnp
from jax import lax
from jax.experimental import pallas as pl
from jax.experimental.pallas import tpu as pltpu
from jax.sharding import PartitionSpec as P

HEADS = 1
DT = 256
DS = 128
CHUNK = 96
LANES = 128
TILE = 64
PART = 32
MESH = pl.DeviceIdType.MESH
LOG2E = 1.4426950408889634
LN2 = 0.6931471805599453


def split(values):
    high = values.astype(jnp.bfloat16)
    low = (values - high.astype(jnp.float32)).astype(jnp.bfloat16)
    return high, low


def nn(left, right):
    return jnp.dot(left, right, preferred_element_type=jnp.float32)


def kernel(
    groups, levels, rows, batches,
    t_hbm, s_hbm, out_ref, loss_ref,
    own_t, own_s, nbr_t, nbr_s, col_t, col_s, row_t, row_s, t_sc, s_sc, acc,
    stat_in, stat_col, div_in, wide, col_level, w_row, q_tr, w_high, w_low,
    part, x_in, x_sum, y_in, total_in,
    load_sem, slot_sem, x_send, x_recv, z_send, z_recv,
    stat_send, stat_recv, col_send, col_recv, div_send, div_recv,
    px_send, px_recv, py_send, py_recv, out_send, out_recv, total_send, total_recv,
):
    chunks = rows // CHUNK
    pb = lax.axis_index("pb")
    ka = lax.axis_index("ka")
    seq = pb % batches
    y = pb // batches
    z = ka // 2
    x = ka % 2
    place = x * groups + y
    low = jnp.where(seq == 0, y, groups - 1 - y)
    high = levels - 1 - low
    sources = (low, high)
    mate = y * batches + (1 - seq)
    x_device = (pb, z * 2 + (1 - x))

    planes = []
    for step in range(1, 2 * groups):
        other = (place + step) % (2 * groups)
        planes.append(((other % groups) * batches + seq, z * 2 + other // groups))
    line = [(pb, ((z + step) % levels) * 2 + x) for step in range(1, levels)]
    barrier = pltpu.get_barrier_semaphore()
    count = 2 * groups * levels
    index = place * levels + z

    def greet(step, carry):
        other = (index + step) % count
        spot, level = other // levels, other % levels
        device = ((spot % groups) * batches + seq, level * 2 + spot // groups)
        pl.semaphore_signal(barrier, inc=1, device_id=device, device_id_type=MESH)
        return carry

    lax.fori_loop(1, count, greet, 0)
    pl.semaphore_signal(barrier, inc=1, device_id=(mate, ka), device_id_type=MESH)

    loads = [
        pltpu.make_async_copy(t_hbm.at[seq], own_t, load_sem.at[0]),
        pltpu.make_async_copy(s_hbm.at[seq], own_s, load_sem.at[1]),
    ]
    for slot in range(2):
        @pl.when(z == sources[slot])
        def _():
            pltpu.make_async_copy(t_hbm.at[seq], col_t.at[slot], slot_sem.at[slot, 0]).start()
            pltpu.make_async_copy(s_hbm.at[seq], col_s.at[slot], slot_sem.at[slot, 1]).start()
    for load in loads:
        load.start()
    pl.semaphore_wait(barrier, count)

    x_copies = [
        pltpu.make_async_remote_copy(
            src_ref=src.at[seq], dst_ref=dst, send_sem=x_send.at[i], recv_sem=x_recv.at[i],
            device_id=x_device, device_id_type=MESH,
        )
        for i, (src, dst) in enumerate(((t_hbm, nbr_t), (s_hbm, nbr_s)))
    ]

    def z_copies(slot, j, to):
        span = pl.ds(pl.multiple_of(j * CHUNK, CHUNK), CHUNK)
        return [
            pltpu.make_async_remote_copy(
                src_ref=buf.at[slot, span, :], dst_ref=buf.at[slot, span, :],
                send_sem=z_send.at[to, slot, j, i], recv_sem=z_recv.at[slot, j, i],
                device_id=(pb, to * 2 + x), device_id_type=MESH,
            )
            for i, buf in enumerate((col_t, col_s))
        ]

    for slot in range(2):
        @pl.when(z == sources[slot])
        def _():
            pltpu.make_async_copy(t_hbm.at[seq], col_t.at[slot], slot_sem.at[slot, 0]).wait()
            pltpu.make_async_copy(s_hbm.at[seq], col_s.at[slot], slot_sem.at[slot, 1]).wait()

    last = levels - 1

    def source_sends(slot, to):
        near = abs(z - to) == 1
        reach = (to != z) if 0 < to < last else near
        return jnp.logical_and(z == sources[slot], reach)

    def forwards(slot, to):
        beside = 1 if to == 0 else last - 1
        waits = jnp.logical_and(sources[slot] != z, sources[slot] != to)
        return jnp.logical_and(z == beside, waits)

    def put_rows(xb, teacher, student):
        t_high, t_low = split((teacher * (LOG2E / math.sqrt(DT))).T)
        s_high, s_low = split((student * (LOG2E / math.sqrt(DS))).T)
        for part_index, (t_part, s_part) in enumerate(
            ((t_high, s_high), (t_low, s_low), (t_high, s_high))
        ):
            row_t[xb, part_index * DT:(part_index + 1) * DT, :] = t_part
            row_s[xb, part_index * DS:(part_index + 1) * DS, :] = s_part

    def relate(xb, j):
        span = pl.ds(pl.multiple_of(j * CHUNK, CHUNK), CHUNK)
        t_high, t_low = split(col_t[:, span, :].reshape(2 * CHUNK, DT))
        s_high, s_low = split(col_s[:, span, :].reshape(2 * CHUNK, DS))
        teacher = nn(jnp.concatenate([t_high, t_high, t_low], axis=1), row_t[xb])
        student = nn(jnp.concatenate([s_high, s_high, s_low], axis=1), row_s[xb])
        tiles = []
        for slot in range(2):
            base = slot * rows + j * CHUNK
            at = pl.ds(pl.multiple_of(base, CHUNK), CHUNK)
            t_sc[xb, at, :] = teacher[slot * CHUNK:(slot + 1) * CHUNK]
            s_sc[xb, at, :] = student[slot * CHUNK:(slot + 1) * CHUNK]
            tiles += [pl.ds(pl.multiple_of(base + i * PART, PART), PART) for i in range(CHUNK // PART)]

        def read(ref, at):
            return ref[xb, at, :].reshape(PART // 8, 8, rows)

        t_old, s_old = acc[xb, 0], acc[xb, 3]
        t_max, s_max = t_old, s_old
        for at in tiles:
            t_max = jnp.maximum(t_max, jnp.max(read(t_sc, at), axis=0))
            s_max = jnp.maximum(s_max, jnp.max(read(s_sc, at), axis=0))
        t_scale = jnp.exp2(t_old - t_max)
        s_scale = jnp.exp2(s_old - s_max)
        t_sum, cross, s_sum = acc[xb, 1] * t_scale, acc[xb, 2] * t_scale, acc[xb, 4] * s_scale
        for at in tiles:
            t_tile, s_tile = read(t_sc, at), read(s_sc, at)
            t_exp = jnp.exp2(t_tile - t_max[None])
            t_sum = t_sum + jnp.sum(t_exp, axis=0)
            cross = cross + jnp.sum(t_exp * (t_tile - s_tile), axis=0)
            s_sum = s_sum + jnp.sum(jnp.exp2(s_tile - s_max[None]), axis=0)
        acc[xb, 0] = t_max
        acc[xb, 1] = t_sum
        acc[xb, 2] = cross
        acc[xb, 3] = s_max
        acc[xb, 4] = s_sum

    for xb in range(2):
        for kind in range(5):
            start = -jnp.inf if kind in (0, 3) else 0.0
            acc[xb, kind] = jnp.full((8, rows), start, jnp.float32)

    for copy in x_copies:
        copy.start()

    def first_send(j, carry):
        for slot in range(2):
            for to in range(levels):
                @pl.when(source_sends(slot, to))
                def _():
                    for copy in z_copies(slot, j, to):
                        copy.start()
        return carry

    lax.fori_loop(0, chunks, first_send, 0)
    for load in loads:
        load.wait()
    put_rows(x, own_t[...], own_s[...])
    half = chunks // 2

    def gather(j, carry):
        @pl.when(j == half)
        def _():
            for copy in x_copies:
                copy.wait_recv()
            put_rows(1 - x, nbr_t[...], nbr_s[...])

        @pl.when(j >= half)
        def _():
            relate(1 - x, j - half)

        for slot in range(2):
            @pl.when(z != sources[slot])
            def _():
                for copy in z_copies(slot, j, 1):
                    copy.wait_recv()
                for to in (0, last):
                    @pl.when(forwards(slot, to))
                    def _():
                        for copy in z_copies(slot, j, to):
                            copy.start()

        relate(x, j)

        @pl.when(j >= half)
        def _():
            relate(1 - x, j)
        return carry

    lax.fori_loop(0, chunks, gather, 0)

    for xb in range(2):
        t_max, s_max = acc[xb, 0], acc[xb, 3]
        t_top = jnp.max(t_max, axis=0, keepdims=True)
        s_top = jnp.max(s_max, axis=0, keepdims=True)
        t_scale = jnp.exp2(t_max - t_top)
        s_scale = jnp.exp2(s_max - s_top)
        t_sum = jnp.sum(acc[xb, 1] * t_scale, axis=0, keepdims=True)
        cross = jnp.sum(acc[xb, 2] * t_scale, axis=0, keepdims=True)
        s_sum = jnp.sum(acc[xb, 4] * s_scale, axis=0, keepdims=True)
        stat_in[place, xb] = jnp.concatenate(
            [t_top, t_sum, cross, s_top, s_sum, jnp.zeros((3, rows), jnp.float32)], axis=0
        )

    def stat_copy(step):
        return pltpu.make_async_remote_copy(
            src_ref=stat_in.at[place], dst_ref=stat_in.at[place],
            send_sem=stat_send.at[step], recv_sem=stat_recv.at[step],
            device_id=planes[step - 1], device_id_type=MESH,
        )

    def stat_wait(step):
        return pltpu.make_async_remote_copy(
            src_ref=stat_in.at[(place - step + 2 * groups) % (2 * groups)],
            dst_ref=stat_in.at[(place - step + 2 * groups) % (2 * groups)],
            send_sem=stat_send.at[step], recv_sem=stat_recv.at[step],
            device_id=planes[step - 1], device_id_type=MESH,
        )

    near = jnp.minimum(z, levels - 1 - z)
    user = jnp.where(seq == 0, near, groups - 1 - near)
    my_slot = jnp.where(z == near, 0, 1)

    def col_copy(xb, step):
        return pltpu.make_async_remote_copy(
            src_ref=stat_in.at[place, xb], dst_ref=stat_col.at[my_slot, place],
            send_sem=col_send.at[xb, step], recv_sem=col_recv.at[my_slot, place],
            device_id=(user * batches + seq, ((z + step) % levels) * 2 + xb), device_id_type=MESH,
        )

    for step in range(1, levels):
        for xb in range(2):
            col_copy(xb, step).start()
    for step in range(1, 2 * groups):
        stat_copy(step).start()
    for slot in range(2):
        high_part, low_part = split((col_s[slot] * (1.0 / math.sqrt(DS))).T)
        q_tr[0:DS, slot * rows:(slot + 1) * rows] = high_part
        q_tr[DS:2 * DS, slot * rows:(slot + 1) * rows] = low_part
    for step in range(1, 2 * groups):
        stat_wait(step).wait_recv()

    def combine(stats):
        t_max = functools.reduce(jnp.maximum, [stat[0:1] for stat in stats])
        s_max = functools.reduce(jnp.maximum, [stat[3:4] for stat in stats])
        t_sum = cross = s_sum = jnp.zeros((1, rows), jnp.float32)
        for stat in stats:
            t_scale = jnp.exp2(stat[0:1] - t_max)
            t_sum = t_sum + stat[1:2] * t_scale
            cross = cross + stat[2:3] * t_scale
            s_sum = s_sum + stat[4:5] * jnp.exp2(stat[3:4] - s_max)
        t_level = t_max + jnp.log2(t_sum)
        s_level = s_max + jnp.log2(s_sum)
        return t_level, s_level, LN2 * (cross / t_sum - t_level + s_level)

    divergence = jnp.zeros((1, rows), jnp.float32)
    for xb in range(2):
        t_level, s_level, share = combine([stat_in[other, xb] for other in range(2 * groups)])
        wide[xb] = jnp.concatenate([t_level, s_level], axis=0)
        divergence = divergence + share
    div_in[z] = jnp.broadcast_to(divergence, (8, rows))

    def div_copy(step, slot):
        return pltpu.make_async_remote_copy(
            src_ref=div_in.at[slot], dst_ref=div_in.at[slot],
            send_sem=div_send.at[step], recv_sem=div_recv.at[step],
            device_id=line[step - 1], device_id_type=MESH,
        )

    for step in range(1, levels):
        div_copy(step, z).start()

    tiles = 2 * rows // TILE

    def row_weights(xb):
        rows_t = wide[xb, 0:1, :]
        rows_s = wide[xb, 1:2, :]

        def tile(j, carry):
            at = pl.ds(pl.multiple_of(j * TILE, TILE), TILE)
            w_row[xb, at, :] = jnp.exp2(s_sc[xb, at, :] - rows_s) - jnp.exp2(t_sc[xb, at, :] - rows_t)
            return carry

        lax.fori_loop(0, tiles, tile, 0)

    row_weights(1 - x)
    row_weights(x)
    for slot in range(2):
        @pl.when(z == sources[slot])
        def _():
            for other in range(2 * groups):
                stat_col[slot, other] = stat_in[other, x]

        @pl.when(z != sources[slot])
        def _():
            for other in range(2 * groups):
                pltpu.make_async_remote_copy(
                    src_ref=stat_col.at[slot, other], dst_ref=stat_col.at[slot, other],
                    send_sem=col_send.at[0, 0], recv_sem=col_recv.at[slot, other],
                    device_id=x_device, device_id_type=MESH,
                ).wait_recv()

        t_level, s_level, _ = combine([stat_col[slot, other] for other in range(2 * groups)])
        both = jnp.concatenate([t_level, s_level, jnp.zeros((6, rows), jnp.float32)], axis=0)
        col_level[slot * rows:(slot + 1) * rows, :] = both.T

    blocks = rows // LANES

    def px_copy(b):
        return pltpu.make_async_remote_copy(
            src_ref=part.at[1 - x, b], dst_ref=x_in.at[b],
            send_sem=px_send.at[b], recv_sem=px_recv.at[b],
            device_id=x_device, device_id_type=MESH,
        )

    def py_copy(step, b):
        return pltpu.make_async_remote_copy(
            src_ref=x_sum.at[b], dst_ref=y_in.at[step, b],
            send_sem=py_send.at[step, b], recv_sem=py_recv.at[step, b],
            device_id=(((y + step) % groups) * batches + seq, ka), device_id_type=MESH,
        )

    def out_copy(which, b):
        span = pl.ds(b * LANES, LANES)
        return pltpu.make_async_remote_copy(
            src_ref=out_ref.at[which, span, :], dst_ref=out_ref.at[which, span, :],
            send_sem=out_send.at[b], recv_sem=out_recv.at[b],
            device_id=(mate, ka), device_id_type=MESH,
        )

    def total_copy(which):
        return pltpu.make_async_remote_copy(
            src_ref=total_in.at[which], dst_ref=total_in.at[which],
            send_sem=total_send, recv_sem=total_recv,
            device_id=(mate, ka), device_id_type=MESH,
        )

    def gradient(xb):
        def tile(j, carry):
            at = pl.ds(pl.multiple_of(j * TILE, TILE), TILE)
            col = col_level[at, :]
            weight = (
                w_row[xb, at, :]
                + jnp.exp2(s_sc[xb, at, :] - col[:, 1:2])
                - jnp.exp2(t_sc[xb, at, :] - col[:, 0:1])
            )
            high_part, low_part = split(weight)
            w_high[at, :] = high_part
            w_low[at, :] = low_part
            return carry

        lax.fori_loop(0, tiles, tile, 0)
        first = nn(q_tr[...], w_high[...])
        product = first[:DS] + first[DS:] + nn(q_tr[0:DS, :], w_low[...])
        for b in range(blocks):
            part[xb, b] = product[:, b * LANES:(b + 1) * LANES]

    gradient(1 - x)
    for b in range(blocks):
        px_copy(b).start()
    gradient(x)
    for b in range(blocks):
        px_copy(b).wait_recv()
        x_sum[b] = part[x, b] + x_in[b]
        for step in range(1, groups):
            py_copy(step, b).start()
    for step in range(1, levels):
        div_copy(step, (z - step + levels) % levels).wait_recv()
    total = div_in[0, 0:1, :]
    for level in range(1, levels):
        total = total + div_in[level, 0:1, :]
    total_in[seq] = jnp.broadcast_to(total, (8, rows))
    total_copy(seq).start()
    for b in range(blocks):
        result = x_sum[b]
        for step in range(1, groups):
            py_copy(step, b).wait_recv()
            result = result + y_in[step, b]
        out_ref[seq, b * LANES:(b + 1) * LANES, :] = result.T
        out_copy(seq, b).start()
    total_copy(1 - seq).wait_recv()
    loss_ref[0, 0] = jnp.sum(total_in[0, 0:1, :] + total_in[1, 0:1, :]) / (
        batches * HEADS * rows * 2 * levels
    )
    total_copy(seq).wait_send()
    for copy in x_copies:
        copy.wait_send()

    def sent(j, carry):
        for slot in range(2):
            for to in range(levels):
                goes = source_sends(slot, to)
                if to in (0, last):
                    goes = jnp.logical_or(goes, forwards(slot, to))

                @pl.when(goes)
                def _():
                    for copy in z_copies(slot, j, to):
                        copy.wait_send()
        return carry

    lax.fori_loop(0, chunks, sent, 0)
    for step in range(1, 2 * groups):
        stat_copy(step).wait_send()
    for step in range(1, levels):
        div_copy(step, z).wait_send()
        for xb in range(2):
            col_copy(xb, step).wait_send()
    for b in range(blocks):
        px_copy(b).wait_send()
        for step in range(1, groups):
            py_copy(step, b).wait_send()
        out_copy(seq, b).wait_send()
        out_copy(1 - seq, b).wait_recv()


def solution(mesh):
    def shards(teacher_q, student_q):
        batches, rows = teacher_q.shape[0], teacher_q.shape[1]
        groups = mesh.shape["pb"] // batches
        levels = mesh.shape["ka"] // 2
        chunks = rows // CHUNK
        blocks = rows // LANES
        f32, bf16 = jnp.float32, jnp.bfloat16
        dma = pltpu.SemaphoreType.DMA
        grad, loss = pl.pallas_call(
            functools.partial(kernel, groups, levels, rows, batches),
            out_shape=(
                jax.ShapeDtypeStruct((batches, rows, DS), f32),
                jax.ShapeDtypeStruct((1, 1), f32),
            ),
            in_specs=[pl.BlockSpec(memory_space=pl.ANY)] * 2,
            out_specs=(
                pl.BlockSpec(memory_space=pltpu.VMEM),
                pl.BlockSpec(memory_space=pltpu.SMEM),
            ),
            scratch_shapes=[
                pltpu.VMEM((rows, DT), f32),
                pltpu.VMEM((rows, DS), f32),
                pltpu.VMEM((rows, DT), f32),
                pltpu.VMEM((rows, DS), f32),
                pltpu.VMEM((2, rows, DT), f32),
                pltpu.VMEM((2, rows, DS), f32),
                pltpu.VMEM((2, 3 * DT, rows), bf16),
                pltpu.VMEM((2, 3 * DS, rows), bf16),
                pltpu.VMEM((2, 2 * rows, rows), f32),
                pltpu.VMEM((2, 2 * rows, rows), f32),
                pltpu.VMEM((2, 5, 8, rows), f32),
                pltpu.VMEM((2 * groups, 2, 8, rows), f32),
                pltpu.VMEM((2, 2 * groups, 8, rows), f32),
                pltpu.VMEM((levels, 8, rows), f32),
                pltpu.VMEM((2, 2, rows), f32),
                pltpu.VMEM((2 * rows, 8), f32),
                pltpu.VMEM((2, 2 * rows, rows), f32),
                pltpu.VMEM((2 * DS, 2 * rows), bf16),
                pltpu.VMEM((2 * rows, rows), bf16),
                pltpu.VMEM((2 * rows, rows), bf16),
                pltpu.VMEM((2, blocks, DS, LANES), f32),
                pltpu.VMEM((blocks, DS, LANES), f32),
                pltpu.VMEM((blocks, DS, LANES), f32),
                pltpu.VMEM((groups, blocks, DS, LANES), f32),
                pltpu.VMEM((batches, 8, rows), f32),
                dma((2,)),
                dma((2, 2)),
                dma((2,)),
                dma((2,)),
                dma((levels, 2, chunks, 2)),
                dma((2, chunks, 2)),
                dma((2 * groups,)),
                dma((2 * groups,)),
                dma((2, levels)),
                dma((2, 2 * groups)),
                dma((levels,)),
                dma((levels,)),
                dma((blocks,)),
                dma((blocks,)),
                dma((groups, blocks)),
                dma((groups, blocks)),
                dma((blocks,)),
                dma((blocks,)),
                dma,
                dma,
            ],
            compiler_params=pltpu.CompilerParams(
                collective_id=0, has_side_effects=True, vmem_limit_bytes=60 * 1024 * 1024
            ),
        )(teacher_q, student_q)
        return grad, loss.reshape(())

    in_specs = (P(None, "ka", None), P(None, "ka", None))
    out_specs = (P(None, "ka", None), P())
    return jax.shard_map(shards, mesh=mesh, in_specs=in_specs, out_specs=out_specs, check_vma=False)
```

```python
import functools
import math

import jax
import jax.numpy as jnp
from jax import lax
from jax.experimental import pallas as pl
from jax.experimental.pallas import tpu as pltpu
from jax.sharding import PartitionSpec as P

HEADS = 1
DT = 256
DS = 128
CHUNK = 96
LANES = 128
TILE = 64
PART = 32
MESH = pl.DeviceIdType.MESH
LOG2E = 1.4426950408889634
LN2 = 0.6931471805599453


def split(values):
    high = values.astype(jnp.bfloat16)
    low = (values - high.astype(jnp.float32)).astype(jnp.bfloat16)
    return high, low


def nn(left, right):
    return jnp.dot(left, right, preferred_element_type=jnp.float32)


def kernel(
    groups, levels, rows, batches,
    t_hbm, s_hbm, out_ref, loss_ref,
    in_t, in_s, col_t, col_s, row_t, row_s, t_sc, s_sc, acc,
    stat_in, stat_col, div_in, wide, col_level, w_row, q_tr, w_high, w_low,
    part, x_in, x_sum, y_in, total_in,
    load_sem, slot_sem, x_send, x_recv, z_send, z_recv,
    stat_send, stat_recv, col_send, col_recv, div_send, div_recv,
    px_send, px_recv, py_send, py_recv, out_send, out_recv, total_send, total_recv,
):
    chunks = rows // CHUNK
    pb = lax.axis_index("pb")
    ka = lax.axis_index("ka")
    seq = pb % batches
    y = pb // batches
    z = ka // 2
    x = ka % 2
    place = x * groups + y
    low = jnp.where(seq == 0, y, groups - 1 - y)
    high = levels - 1 - low
    sources = (low, high)
    mate = y * batches + (1 - seq)
    x_device = (pb, z * 2 + (1 - x))

    planes = []
    for step in range(1, 2 * groups):
        other = (place + step) % (2 * groups)
        planes.append(((other % groups) * batches + seq, z * 2 + other // groups))
    line = [(pb, ((z + step) % levels) * 2 + x) for step in range(1, levels)]
    barrier = pltpu.get_barrier_semaphore()
    count = 2 * groups * levels
    index = place * levels + z

    def greet(step, carry):
        other = (index + step) % count
        spot, level = other // levels, other % levels
        device = ((spot % groups) * batches + seq, level * 2 + spot // groups)
        pl.semaphore_signal(barrier, inc=1, device_id=device, device_id_type=MESH)
        return carry

    lax.fori_loop(1, count, greet, 0)
    pl.semaphore_signal(barrier, inc=1, device_id=(mate, ka), device_id_type=MESH)

    loads = [
        pltpu.make_async_copy(t_hbm.at[seq], in_t.at[0], load_sem.at[0]),
        pltpu.make_async_copy(s_hbm.at[seq], in_s.at[0], load_sem.at[1]),
    ]
    for slot in range(2):
        @pl.when(z == sources[slot])
        def _():
            pltpu.make_async_copy(t_hbm.at[seq], col_t.at[slot], slot_sem.at[slot, 0]).start()
            pltpu.make_async_copy(s_hbm.at[seq], col_s.at[slot], slot_sem.at[slot, 1]).start()
    for load in loads:
        load.start()
    pl.semaphore_wait(barrier, count)

    x_copies = [
        pltpu.make_async_remote_copy(
            src_ref=src.at[seq], dst_ref=dst, send_sem=x_send.at[i], recv_sem=x_recv.at[i],
            device_id=x_device, device_id_type=MESH,
        )
        for i, (src, dst) in enumerate(((t_hbm, in_t.at[1]), (s_hbm, in_s.at[1])))
    ]

    def z_copies(slot, j, to):
        span = pl.ds(pl.multiple_of(j * CHUNK, CHUNK), CHUNK)
        return [
            pltpu.make_async_remote_copy(
                src_ref=buf.at[slot, span, :], dst_ref=buf.at[slot, span, :],
                send_sem=z_send.at[to, slot, j, i], recv_sem=z_recv.at[slot, j, i],
                device_id=(pb, to * 2 + x), device_id_type=MESH,
            )
            for i, buf in enumerate((col_t, col_s))
        ]

    for slot in range(2):
        @pl.when(z == sources[slot])
        def _():
            pltpu.make_async_copy(t_hbm.at[seq], col_t.at[slot], slot_sem.at[slot, 0]).wait()
            pltpu.make_async_copy(s_hbm.at[seq], col_s.at[slot], slot_sem.at[slot, 1]).wait()

    last = levels - 1

    def source_sends(slot, to):
        near = abs(z - to) == 1
        reach = (to != z) if 0 < to < last else near
        return jnp.logical_and(z == sources[slot], reach)

    def forwards(slot, to):
        beside = 1 if to == 0 else last - 1
        waits = jnp.logical_and(sources[slot] != z, sources[slot] != to)
        return jnp.logical_and(z == beside, waits)

    def put_rows(xb, teacher, student):
        t_high, t_low = split((teacher * (LOG2E / math.sqrt(DT))).T)
        s_high, s_low = split((student * (LOG2E / math.sqrt(DS))).T)
        for part_index, (t_part, s_part) in enumerate(
            ((t_high, s_high), (t_low, s_low), (t_high, s_high))
        ):
            row_t[xb, part_index * DT:(part_index + 1) * DT, :] = t_part
            row_s[xb, part_index * DS:(part_index + 1) * DS, :] = s_part

    def relate(xb, j):
        span = pl.ds(pl.multiple_of(j * CHUNK, CHUNK), CHUNK)
        t_high, t_low = split(col_t[:, span, :].reshape(2 * CHUNK, DT))
        s_high, s_low = split(col_s[:, span, :].reshape(2 * CHUNK, DS))
        teacher = nn(jnp.concatenate([t_high, t_high, t_low], axis=1), row_t[xb])
        student = nn(jnp.concatenate([s_high, s_high, s_low], axis=1), row_s[xb])
        tiles = []
        for slot in range(2):
            base = slot * rows + j * CHUNK
            at = pl.ds(pl.multiple_of(base, CHUNK), CHUNK)
            t_sc[xb, at, :] = teacher[slot * CHUNK:(slot + 1) * CHUNK]
            s_sc[xb, at, :] = student[slot * CHUNK:(slot + 1) * CHUNK]
            tiles += [pl.ds(pl.multiple_of(base + i * PART, PART), PART) for i in range(CHUNK // PART)]

        def read(ref, at):
            return ref[xb, at, :].reshape(PART // 8, 8, rows)

        t_old, s_old = acc[xb, 0], acc[xb, 3]
        t_max, s_max = t_old, s_old
        for at in tiles:
            t_max = jnp.maximum(t_max, jnp.max(read(t_sc, at), axis=0))
            s_max = jnp.maximum(s_max, jnp.max(read(s_sc, at), axis=0))
        t_scale = jnp.exp2(t_old - t_max)
        s_scale = jnp.exp2(s_old - s_max)
        t_sum, cross, s_sum = acc[xb, 1] * t_scale, acc[xb, 2] * t_scale, acc[xb, 4] * s_scale
        for at in tiles:
            t_tile, s_tile = read(t_sc, at), read(s_sc, at)
            t_exp = jnp.exp2(t_tile - t_max[None])
            t_sum = t_sum + jnp.sum(t_exp, axis=0)
            cross = cross + jnp.sum(t_exp * (t_tile - s_tile), axis=0)
            s_sum = s_sum + jnp.sum(jnp.exp2(s_tile - s_max[None]), axis=0)
        acc[xb, 0] = t_max
        acc[xb, 1] = t_sum
        acc[xb, 2] = cross
        acc[xb, 3] = s_max
        acc[xb, 4] = s_sum

    for xb in range(2):
        for kind in range(5):
            start = -jnp.inf if kind in (0, 3) else 0.0
            acc[xb, kind] = jnp.full((8, rows), start, jnp.float32)

    for copy in x_copies:
        copy.start()

    def first_send(j, carry):
        for slot in range(2):
            for to in range(levels):
                @pl.when(source_sends(slot, to))
                def _():
                    for copy in z_copies(slot, j, to):
                        copy.start()
        return carry

    lax.fori_loop(0, chunks, first_send, 0)
    half = chunks // 2

    def arrive(j):
        for slot in range(2):
            @pl.when(z != sources[slot])
            def _():
                for copy in z_copies(slot, j, 1):
                    copy.wait_recv()
                for to in (0, last):
                    @pl.when(forwards(slot, to))
                    def _():
                        for copy in z_copies(slot, j, to):
                            copy.start()

    def gather(k, carry):
        late = k - half
        phase = jnp.where(k < half, 1, late % 3)
        j = jnp.where(k < half, k, late // 3 + jnp.where(phase == 0, 0, half))
        own = phase == 1

        @pl.when(k == 0)
        def _():
            for load in loads:
                load.wait()

        @pl.when(k == half)
        def _():
            for copy in x_copies:
                copy.wait_recv()

        @pl.when(jnp.logical_or(k == 0, k == half))
        def _():
            which = jnp.where(k == 0, 0, 1)
            put_rows(jnp.where(k == 0, x, 1 - x), in_t[which], in_s[which])

        @pl.when(own)
        def _():
            arrive(j)

        relate(jnp.where(own, x, 1 - x), j)
        return carry

    lax.fori_loop(0, 2 * chunks, gather, 0)

    for xb in range(2):
        t_max, s_max = acc[xb, 0], acc[xb, 3]
        t_top = jnp.max(t_max, axis=0, keepdims=True)
        s_top = jnp.max(s_max, axis=0, keepdims=True)
        t_scale = jnp.exp2(t_max - t_top)
        s_scale = jnp.exp2(s_max - s_top)
        t_sum = jnp.sum(acc[xb, 1] * t_scale, axis=0, keepdims=True)
        cross = jnp.sum(acc[xb, 2] * t_scale, axis=0, keepdims=True)
        s_sum = jnp.sum(acc[xb, 4] * s_scale, axis=0, keepdims=True)
        stat_in[place, xb] = jnp.concatenate(
            [t_top, t_sum, cross, s_top, s_sum, jnp.zeros((3, rows), jnp.float32)], axis=0
        )

    def stat_copy(step):
        return pltpu.make_async_remote_copy(
            src_ref=stat_in.at[place], dst_ref=stat_in.at[place],
            send_sem=stat_send.at[step], recv_sem=stat_recv.at[step],
            device_id=planes[step - 1], device_id_type=MESH,
        )

    def stat_wait(step):
        return pltpu.make_async_remote_copy(
            src_ref=stat_in.at[(place - step + 2 * groups) % (2 * groups)],
            dst_ref=stat_in.at[(place - step + 2 * groups) % (2 * groups)],
            send_sem=stat_send.at[step], recv_sem=stat_recv.at[step],
            device_id=planes[step - 1], device_id_type=MESH,
        )

    near = jnp.minimum(z, levels - 1 - z)
    user = jnp.where(seq == 0, near, groups - 1 - near)
    my_slot = jnp.where(z == near, 0, 1)

    def col_copy(xb, step):
        return pltpu.make_async_remote_copy(
            src_ref=stat_in.at[place, xb], dst_ref=stat_col.at[my_slot, place],
            send_sem=col_send.at[xb, step], recv_sem=col_recv.at[my_slot, place],
            device_id=(user * batches + seq, ((z + step) % levels) * 2 + xb), device_id_type=MESH,
        )

    for step in range(1, levels):
        for xb in range(2):
            col_copy(xb, step).start()
    for step in range(1, 2 * groups):
        stat_copy(step).start()
    for slot in range(2):
        high_part, low_part = split((col_s[slot] * (1.0 / math.sqrt(DS))).T)
        q_tr[0:DS, slot * rows:(slot + 1) * rows] = high_part
        q_tr[DS:2 * DS, slot * rows:(slot + 1) * rows] = low_part
    for step in range(1, 2 * groups):
        stat_wait(step).wait_recv()

    def combine(stats):
        t_max = functools.reduce(jnp.maximum, [stat[0:1] for stat in stats])
        s_max = functools.reduce(jnp.maximum, [stat[3:4] for stat in stats])
        t_sum = cross = s_sum = jnp.zeros((1, rows), jnp.float32)
        for stat in stats:
            t_scale = jnp.exp2(stat[0:1] - t_max)
            t_sum = t_sum + stat[1:2] * t_scale
            cross = cross + stat[2:3] * t_scale
            s_sum = s_sum + stat[4:5] * jnp.exp2(stat[3:4] - s_max)
        t_level = t_max + jnp.log2(t_sum)
        s_level = s_max + jnp.log2(s_sum)
        return t_level, s_level, LN2 * (cross / t_sum - t_level + s_level)

    divergence = jnp.zeros((1, rows), jnp.float32)
    for xb in range(2):
        t_level, s_level, share = combine([stat_in[other, xb] for other in range(2 * groups)])
        wide[xb] = jnp.concatenate([t_level, s_level], axis=0)
        divergence = divergence + share
    div_in[z] = jnp.broadcast_to(divergence, (8, rows))

    def div_copy(step, slot):
        return pltpu.make_async_remote_copy(
            src_ref=div_in.at[slot], dst_ref=div_in.at[slot],
            send_sem=div_send.at[step], recv_sem=div_recv.at[step],
            device_id=line[step - 1], device_id_type=MESH,
        )

    for step in range(1, levels):
        div_copy(step, z).start()

    tiles = 2 * rows // TILE

    def row_weights(xb):
        rows_t = wide[xb, 0:1, :]
        rows_s = wide[xb, 1:2, :]

        def tile(j, carry):
            at = pl.ds(pl.multiple_of(j * TILE, TILE), TILE)
            w_row[xb, at, :] = jnp.exp2(s_sc[xb, at, :] - rows_s) - jnp.exp2(t_sc[xb, at, :] - rows_t)
            return carry

        lax.fori_loop(0, tiles, tile, 0)

    def both_weights(xb, carry):
        row_weights(xb)
        return carry

    lax.fori_loop(0, 2, both_weights, 0)
    for slot in range(2):
        @pl.when(z == sources[slot])
        def _():
            for other in range(2 * groups):
                stat_col[slot, other] = stat_in[other, x]

        @pl.when(z != sources[slot])
        def _():
            for other in range(2 * groups):
                pltpu.make_async_remote_copy(
                    src_ref=stat_col.at[slot, other], dst_ref=stat_col.at[slot, other],
                    send_sem=col_send.at[0, 0], recv_sem=col_recv.at[slot, other],
                    device_id=x_device, device_id_type=MESH,
                ).wait_recv()

        t_level, s_level, _ = combine([stat_col[slot, other] for other in range(2 * groups)])
        both = jnp.concatenate([t_level, s_level, jnp.zeros((6, rows), jnp.float32)], axis=0)
        col_level[slot * rows:(slot + 1) * rows, :] = both.T

    blocks = rows // LANES

    def px_copy(b):
        return pltpu.make_async_remote_copy(
            src_ref=part.at[1 - x, b], dst_ref=x_in.at[b],
            send_sem=px_send.at[b], recv_sem=px_recv.at[b],
            device_id=x_device, device_id_type=MESH,
        )

    def py_copy(step, b):
        return pltpu.make_async_remote_copy(
            src_ref=x_sum.at[b], dst_ref=y_in.at[step, b],
            send_sem=py_send.at[step, b], recv_sem=py_recv.at[step, b],
            device_id=(((y + step) % groups) * batches + seq, ka), device_id_type=MESH,
        )

    def out_copy(which, b):
        span = pl.ds(b * LANES, LANES)
        return pltpu.make_async_remote_copy(
            src_ref=out_ref.at[which, span, :], dst_ref=out_ref.at[which, span, :],
            send_sem=out_send.at[b], recv_sem=out_recv.at[b],
            device_id=(mate, ka), device_id_type=MESH,
        )

    def total_copy(which):
        return pltpu.make_async_remote_copy(
            src_ref=total_in.at[which], dst_ref=total_in.at[which],
            send_sem=total_send, recv_sem=total_recv,
            device_id=(mate, ka), device_id_type=MESH,
        )

    def gradient(xb):
        def tile(j, carry):
            at = pl.ds(pl.multiple_of(j * TILE, TILE), TILE)
            col = col_level[at, :]
            weight = (
                w_row[xb, at, :]
                + jnp.exp2(s_sc[xb, at, :] - col[:, 1:2])
                - jnp.exp2(t_sc[xb, at, :] - col[:, 0:1])
            )
            high_part, low_part = split(weight)
            w_high[at, :] = high_part
            w_low[at, :] = low_part
            return carry

        lax.fori_loop(0, tiles, tile, 0)
        first = nn(q_tr[...], w_high[...])
        product = first[:DS] + first[DS:] + nn(q_tr[0:DS, :], w_low[...])
        for b in range(blocks):
            part[xb, b] = product[:, b * LANES:(b + 1) * LANES]

    def both_gradients(step, carry):
        gradient(jnp.where(step == 0, 1 - x, x))

        @pl.when(step == 0)
        def _():
            for b in range(blocks):
                px_copy(b).start()
        return carry

    lax.fori_loop(0, 2, both_gradients, 0)
    for b in range(blocks):
        px_copy(b).wait_recv()
        x_sum[b] = part[x, b] + x_in[b]
        for step in range(1, groups):
            py_copy(step, b).start()
    for step in range(1, levels):
        div_copy(step, (z - step + levels) % levels).wait_recv()
    total = div_in[0, 0:1, :]
    for level in range(1, levels):
        total = total + div_in[level, 0:1, :]
    total_in[seq] = jnp.broadcast_to(total, (8, rows))
    total_copy(seq).start()
    for b in range(blocks):
        result = x_sum[b]
        for step in range(1, groups):
            py_copy(step, b).wait_recv()
            result = result + y_in[step, b]
        out_ref[seq, b * LANES:(b + 1) * LANES, :] = result.T
        out_copy(seq, b).start()
    total_copy(1 - seq).wait_recv()
    loss_ref[0, 0] = jnp.sum(total_in[0, 0:1, :] + total_in[1, 0:1, :]) / (
        batches * HEADS * rows * 2 * levels
    )
    total_copy(seq).wait_send()
    for copy in x_copies:
        copy.wait_send()

    def sent(j, carry):
        for slot in range(2):
            for to in range(levels):
                goes = source_sends(slot, to)
                if to in (0, last):
                    goes = jnp.logical_or(goes, forwards(slot, to))

                @pl.when(goes)
                def _():
                    for copy in z_copies(slot, j, to):
                        copy.wait_send()
        return carry

    lax.fori_loop(0, chunks, sent, 0)
    for step in range(1, 2 * groups):
        stat_copy(step).wait_send()
    for step in range(1, levels):
        div_copy(step, z).wait_send()
        for xb in range(2):
            col_copy(xb, step).wait_send()
    for b in range(blocks):
        px_copy(b).wait_send()
        for step in range(1, groups):
            py_copy(step, b).wait_send()
        out_copy(seq, b).wait_send()
        out_copy(1 - seq, b).wait_recv()


def solution(mesh):
    def shards(teacher_q, student_q):
        batches, rows = teacher_q.shape[0], teacher_q.shape[1]
        groups = mesh.shape["pb"] // batches
        levels = mesh.shape["ka"] // 2
        chunks = rows // CHUNK
        blocks = rows // LANES
        f32, bf16 = jnp.float32, jnp.bfloat16
        dma = pltpu.SemaphoreType.DMA
        grad, loss = pl.pallas_call(
            functools.partial(kernel, groups, levels, rows, batches),
            out_shape=(
                jax.ShapeDtypeStruct((batches, rows, DS), f32),
                jax.ShapeDtypeStruct((1, 1), f32),
            ),
            in_specs=[pl.BlockSpec(memory_space=pl.ANY)] * 2,
            out_specs=(
                pl.BlockSpec(memory_space=pltpu.VMEM),
                pl.BlockSpec(memory_space=pltpu.SMEM),
            ),
            scratch_shapes=[
                pltpu.VMEM((2, rows, DT), f32),
                pltpu.VMEM((2, rows, DS), f32),
                pltpu.VMEM((2, rows, DT), f32),
                pltpu.VMEM((2, rows, DS), f32),
                pltpu.VMEM((2, 3 * DT, rows), bf16),
                pltpu.VMEM((2, 3 * DS, rows), bf16),
                pltpu.VMEM((2, 2 * rows, rows), f32),
                pltpu.VMEM((2, 2 * rows, rows), f32),
                pltpu.VMEM((2, 5, 8, rows), f32),
                pltpu.VMEM((2 * groups, 2, 8, rows), f32),
                pltpu.VMEM((2, 2 * groups, 8, rows), f32),
                pltpu.VMEM((levels, 8, rows), f32),
                pltpu.VMEM((2, 2, rows), f32),
                pltpu.VMEM((2 * rows, 8), f32),
                pltpu.VMEM((2, 2 * rows, rows), f32),
                pltpu.VMEM((2 * DS, 2 * rows), bf16),
                pltpu.VMEM((2 * rows, rows), bf16),
                pltpu.VMEM((2 * rows, rows), bf16),
                pltpu.VMEM((2, blocks, DS, LANES), f32),
                pltpu.VMEM((blocks, DS, LANES), f32),
                pltpu.VMEM((blocks, DS, LANES), f32),
                pltpu.VMEM((groups, blocks, DS, LANES), f32),
                pltpu.VMEM((batches, 8, rows), f32),
                dma((2,)),
                dma((2, 2)),
                dma((2,)),
                dma((2,)),
                dma((levels, 2, chunks, 2)),
                dma((2, chunks, 2)),
                dma((2 * groups,)),
                dma((2 * groups,)),
                dma((2, levels)),
                dma((2, 2 * groups)),
                dma((levels,)),
                dma((levels,)),
                dma((blocks,)),
                dma((blocks,)),
                dma((groups, blocks)),
                dma((groups, blocks)),
                dma((blocks,)),
                dma((blocks,)),
                dma,
                dma,
            ],
            compiler_params=pltpu.CompilerParams(
                collective_id=0, has_side_effects=True, vmem_limit_bytes=60 * 1024 * 1024
            ),
        )(teacher_q, student_q)
        return grad, loss.reshape(())

    in_specs = (P(None, "ka", None), P(None, "ka", None))
    out_specs = (P(None, "ka", None), P())
    return jax.shard_map(shards, mesh=mesh, in_specs=in_specs, out_specs=out_specs, check_vma=False)
```

```python
import functools
import math

import jax
import jax.numpy as jnp
from jax import lax
from jax.experimental import pallas as pl
from jax.experimental.pallas import tpu as pltpu
from jax.sharding import PartitionSpec as P

HEADS = 1
DT = 256
DS = 128
CHUNK = 96
LANES = 128
TILE = 64
PART = 32
MESH = pl.DeviceIdType.MESH
LOG2E = 1.4426950408889634
LN2 = 0.6931471805599453


def split(values):
    high = values.astype(jnp.bfloat16)
    low = (values - high.astype(jnp.float32)).astype(jnp.bfloat16)
    return high, low


def nt(left, right):
    return lax.dot_general(
        left, right, (((1,), (1,)), ((), ())), preferred_element_type=jnp.float32
    )


def nn(left, right):
    return jnp.dot(left, right, preferred_element_type=jnp.float32)


def kernel(
    groups, levels, rows, batches,
    t_hbm, s_hbm, out_ref, loss_ref,
    in_t, in_s, col_t, col_s, row_t, row_s, t_sc, s_sc, acc,
    stat_in, stat_col, div_in, wide, col_level, w_row, q_tr, w_high, w_low,
    part, x_in, x_sum, y_in, total_in,
    load_sem, slot_sem, x_send, x_recv, z_send, z_recv,
    stat_send, stat_recv, col_send, col_recv, div_send, div_recv,
    px_send, px_recv, py_send, py_recv, out_send, out_recv, total_send, total_recv,
):
    chunks = rows // CHUNK
    pb = lax.axis_index("pb")
    ka = lax.axis_index("ka")
    seq = pb % batches
    y = pb // batches
    z = ka // 2
    x = ka % 2
    place = x * groups + y
    low = jnp.where(seq == 0, y, groups - 1 - y)
    high = levels - 1 - low
    sources = (low, high)
    mate = y * batches + (1 - seq)
    x_device = (pb, z * 2 + (1 - x))

    planes = []
    for step in range(1, 2 * groups):
        other = (place + step) % (2 * groups)
        planes.append(((other % groups) * batches + seq, z * 2 + other // groups))
    line = [(pb, ((z + step) % levels) * 2 + x) for step in range(1, levels)]
    barrier = pltpu.get_barrier_semaphore()
    count = 2 * groups * levels
    index = place * levels + z

    def greet(step, carry):
        other = (index + step) % count
        spot, level = other // levels, other % levels
        device = ((spot % groups) * batches + seq, level * 2 + spot // groups)
        pl.semaphore_signal(barrier, inc=1, device_id=device, device_id_type=MESH)
        return carry

    lax.fori_loop(1, count, greet, 0)
    pl.semaphore_signal(barrier, inc=1, device_id=(mate, ka), device_id_type=MESH)

    loads = [
        pltpu.make_async_copy(t_hbm.at[seq], in_t.at[0], load_sem.at[0]),
        pltpu.make_async_copy(s_hbm.at[seq], in_s.at[0], load_sem.at[1]),
    ]
    for slot in range(2):
        @pl.when(z == sources[slot])
        def _():
            pltpu.make_async_copy(t_hbm.at[seq], col_t.at[slot], slot_sem.at[slot, 0]).start()
            pltpu.make_async_copy(s_hbm.at[seq], col_s.at[slot], slot_sem.at[slot, 1]).start()
    for load in loads:
        load.start()
    pl.semaphore_wait(barrier, count)

    x_copies = [
        pltpu.make_async_remote_copy(
            src_ref=src.at[seq], dst_ref=dst, send_sem=x_send.at[i], recv_sem=x_recv.at[i],
            device_id=x_device, device_id_type=MESH,
        )
        for i, (src, dst) in enumerate(((t_hbm, in_t.at[1]), (s_hbm, in_s.at[1])))
    ]

    def z_copies(slot, j, to):
        span = pl.ds(pl.multiple_of(j * CHUNK, CHUNK), CHUNK)
        return [
            pltpu.make_async_remote_copy(
                src_ref=buf.at[slot, span, :], dst_ref=buf.at[slot, span, :],
                send_sem=z_send.at[to, slot, j, i], recv_sem=z_recv.at[slot, j, i],
                device_id=(pb, to * 2 + x), device_id_type=MESH,
            )
            for i, buf in enumerate((col_t, col_s))
        ]

    for slot in range(2):
        @pl.when(z == sources[slot])
        def _():
            pltpu.make_async_copy(t_hbm.at[seq], col_t.at[slot], slot_sem.at[slot, 0]).wait()
            pltpu.make_async_copy(s_hbm.at[seq], col_s.at[slot], slot_sem.at[slot, 1]).wait()

    last = levels - 1

    def source_sends(slot, to):
        near = abs(z - to) == 1
        reach = (to != z) if 0 < to < last else near
        return jnp.logical_and(z == sources[slot], reach)

    def forwards(slot, to):
        beside = 1 if to == 0 else last - 1
        waits = jnp.logical_and(sources[slot] != z, sources[slot] != to)
        return jnp.logical_and(z == beside, waits)

    def put_rows(xb, teacher, student):
        t_high, t_low = split((teacher * (LOG2E / math.sqrt(DT))).T)
        s_high, s_low = split((student * (LOG2E / math.sqrt(DS))).T)
        for part_index, (t_part, s_part) in enumerate(
            ((t_high, s_high), (t_low, s_low), (t_high, s_high))
        ):
            row_t[xb, part_index * DT:(part_index + 1) * DT, :] = t_part
            row_s[xb, part_index * DS:(part_index + 1) * DS, :] = s_part

    def relate(xb, j):
        span = pl.ds(pl.multiple_of(j * CHUNK, CHUNK), CHUNK)
        t_high, t_low = split(col_t[:, span, :].reshape(2 * CHUNK, DT))
        s_high, s_low = split(col_s[:, span, :].reshape(2 * CHUNK, DS))
        teacher = nn(jnp.concatenate([t_high, t_high, t_low], axis=1), row_t[xb])
        student = nn(jnp.concatenate([s_high, s_high, s_low], axis=1), row_s[xb])
        tiles = []
        for slot in range(2):
            base = slot * rows + j * CHUNK
            at = pl.ds(pl.multiple_of(base, CHUNK), CHUNK)
            t_sc[xb, at, :] = teacher[slot * CHUNK:(slot + 1) * CHUNK]
            s_sc[xb, at, :] = student[slot * CHUNK:(slot + 1) * CHUNK]
            tiles += [pl.ds(pl.multiple_of(base + i * PART, PART), PART) for i in range(CHUNK // PART)]

        def read(ref, at):
            return ref[xb, at, :].reshape(PART // 8, 8, rows)

        t_old, s_old = acc[xb, 0], acc[xb, 3]
        t_max, s_max = t_old, s_old
        for at in tiles:
            t_max = jnp.maximum(t_max, jnp.max(read(t_sc, at), axis=0))
            s_max = jnp.maximum(s_max, jnp.max(read(s_sc, at), axis=0))
        t_scale = jnp.exp2(t_old - t_max)
        s_scale = jnp.exp2(s_old - s_max)
        t_sum, cross, s_sum = acc[xb, 1] * t_scale, acc[xb, 2] * t_scale, acc[xb, 4] * s_scale
        for at in tiles:
            t_tile, s_tile = read(t_sc, at), read(s_sc, at)
            t_exp = jnp.exp2(t_tile - t_max[None])
            t_sum = t_sum + jnp.sum(t_exp, axis=0)
            cross = cross + jnp.sum(t_exp * (t_tile - s_tile), axis=0)
            s_sum = s_sum + jnp.sum(jnp.exp2(s_tile - s_max[None]), axis=0)
        acc[xb, 0] = t_max
        acc[xb, 1] = t_sum
        acc[xb, 2] = cross
        acc[xb, 3] = s_max
        acc[xb, 4] = s_sum

    for xb in range(2):
        for kind in range(5):
            start = -jnp.inf if kind in (0, 3) else 0.0
            acc[xb, kind] = jnp.full((8, rows), start, jnp.float32)

    for copy in x_copies:
        copy.start()

    def first_send(j, carry):
        for slot in range(2):
            for to in range(levels):
                @pl.when(source_sends(slot, to))
                def _():
                    for copy in z_copies(slot, j, to):
                        copy.start()
        return carry

    lax.fori_loop(0, chunks, first_send, 0)
    half = chunks // 2

    def arrive(j):
        for slot in range(2):
            @pl.when(z != sources[slot])
            def _():
                for copy in z_copies(slot, j, 1):
                    copy.wait_recv()
                for to in (0, last):
                    @pl.when(forwards(slot, to))
                    def _():
                        for copy in z_copies(slot, j, to):
                            copy.start()

    def gather(k, carry):
        late = k - half
        phase = jnp.where(k < half, 1, late % 3)
        j = jnp.where(k < half, k, late // 3 + jnp.where(phase == 0, 0, half))
        own = phase == 1

        @pl.when(k == 0)
        def _():
            for load in loads:
                load.wait()

        @pl.when(k == half)
        def _():
            for copy in x_copies:
                copy.wait_recv()

        @pl.when(jnp.logical_or(k == 0, k == half))
        def _():
            which = jnp.where(k == 0, 0, 1)
            put_rows(jnp.where(k == 0, x, 1 - x), in_t[which], in_s[which])

        @pl.when(own)
        def _():
            arrive(j)

        relate(jnp.where(own, x, 1 - x), j)
        return carry

    lax.fori_loop(0, 2 * chunks, gather, 0)

    for xb in range(2):
        t_max, s_max = acc[xb, 0], acc[xb, 3]
        t_top = jnp.max(t_max, axis=0, keepdims=True)
        s_top = jnp.max(s_max, axis=0, keepdims=True)
        t_scale = jnp.exp2(t_max - t_top)
        s_scale = jnp.exp2(s_max - s_top)
        t_sum = jnp.sum(acc[xb, 1] * t_scale, axis=0, keepdims=True)
        cross = jnp.sum(acc[xb, 2] * t_scale, axis=0, keepdims=True)
        s_sum = jnp.sum(acc[xb, 4] * s_scale, axis=0, keepdims=True)
        stat_in[place, xb] = jnp.concatenate(
            [t_top, t_sum, cross, s_top, s_sum, jnp.zeros((3, rows), jnp.float32)], axis=0
        )

    def stat_copy(step):
        return pltpu.make_async_remote_copy(
            src_ref=stat_in.at[place], dst_ref=stat_in.at[place],
            send_sem=stat_send.at[step], recv_sem=stat_recv.at[step],
            device_id=planes[step - 1], device_id_type=MESH,
        )

    def stat_wait(step):
        return pltpu.make_async_remote_copy(
            src_ref=stat_in.at[(place - step + 2 * groups) % (2 * groups)],
            dst_ref=stat_in.at[(place - step + 2 * groups) % (2 * groups)],
            send_sem=stat_send.at[step], recv_sem=stat_recv.at[step],
            device_id=planes[step - 1], device_id_type=MESH,
        )

    near = jnp.minimum(z, levels - 1 - z)
    user = jnp.where(seq == 0, near, groups - 1 - near)
    my_slot = jnp.where(z == near, 0, 1)

    def col_copy(xb, step):
        return pltpu.make_async_remote_copy(
            src_ref=stat_in.at[place, xb], dst_ref=stat_col.at[my_slot, place],
            send_sem=col_send.at[xb, step], recv_sem=col_recv.at[my_slot, place],
            device_id=(user * batches + seq, ((z + step) % levels) * 2 + xb), device_id_type=MESH,
        )

    for step in range(1, levels):
        for xb in range(2):
            col_copy(xb, step).start()
    for step in range(1, 2 * groups):
        stat_copy(step).start()
    for slot in range(2):
        high_part, low_part = split((col_s[slot] * (1.0 / math.sqrt(DS))).T)
        q_tr[0:DS, slot * rows:(slot + 1) * rows] = high_part
        q_tr[DS:2 * DS, slot * rows:(slot + 1) * rows] = low_part
    for step in range(1, 2 * groups):
        stat_wait(step).wait_recv()

    def combine(stats):
        t_max = functools.reduce(jnp.maximum, [stat[0:1] for stat in stats])
        s_max = functools.reduce(jnp.maximum, [stat[3:4] for stat in stats])
        t_sum = cross = s_sum = jnp.zeros((1, rows), jnp.float32)
        for stat in stats:
            t_scale = jnp.exp2(stat[0:1] - t_max)
            t_sum = t_sum + stat[1:2] * t_scale
            cross = cross + stat[2:3] * t_scale
            s_sum = s_sum + stat[4:5] * jnp.exp2(stat[3:4] - s_max)
        t_level = t_max + jnp.log2(t_sum)
        s_level = s_max + jnp.log2(s_sum)
        return t_level, s_level, LN2 * (cross / t_sum - t_level + s_level)

    divergence = jnp.zeros((1, rows), jnp.float32)
    for xb in range(2):
        t_level, s_level, share = combine([stat_in[other, xb] for other in range(2 * groups)])
        wide[xb] = jnp.concatenate([t_level, s_level], axis=0)
        divergence = divergence + share
    div_in[z] = jnp.broadcast_to(divergence, (8, rows))

    def div_copy(step, slot):
        return pltpu.make_async_remote_copy(
            src_ref=div_in.at[slot], dst_ref=div_in.at[slot],
            send_sem=div_send.at[step], recv_sem=div_recv.at[step],
            device_id=line[step - 1], device_id_type=MESH,
        )

    for step in range(1, levels):
        div_copy(step, z).start()

    tiles = 2 * rows // TILE

    def row_weights(xb):
        rows_t = wide[xb, 0:1, :]
        rows_s = wide[xb, 1:2, :]

        def tile(j, carry):
            at = pl.ds(pl.multiple_of(j * TILE, TILE), TILE)
            w_row[xb, at, :] = jnp.exp2(s_sc[xb, at, :] - rows_s) - jnp.exp2(t_sc[xb, at, :] - rows_t)
            return carry

        lax.fori_loop(0, tiles, tile, 0)

    def both_weights(xb, carry):
        row_weights(xb)
        return carry

    lax.fori_loop(0, 2, both_weights, 0)
    for slot in range(2):
        @pl.when(z == sources[slot])
        def _():
            for other in range(2 * groups):
                stat_col[slot, other] = stat_in[other, x]

        @pl.when(z != sources[slot])
        def _():
            for other in range(2 * groups):
                pltpu.make_async_remote_copy(
                    src_ref=stat_col.at[slot, other], dst_ref=stat_col.at[slot, other],
                    send_sem=col_send.at[0, 0], recv_sem=col_recv.at[slot, other],
                    device_id=x_device, device_id_type=MESH,
                ).wait_recv()

        t_level, s_level, _ = combine([stat_col[slot, other] for other in range(2 * groups)])
        both = jnp.concatenate([t_level, s_level, jnp.zeros((6, rows), jnp.float32)], axis=0)
        col_level[slot * rows:(slot + 1) * rows, :] = both.T

    blocks = rows // LANES

    def px_copy(b):
        return pltpu.make_async_remote_copy(
            src_ref=part.at[1 - x, b], dst_ref=x_in.at[b],
            send_sem=px_send.at[b], recv_sem=px_recv.at[b],
            device_id=x_device, device_id_type=MESH,
        )

    def py_copy(step, b):
        return pltpu.make_async_remote_copy(
            src_ref=x_sum.at[b], dst_ref=y_in.at[step, b],
            send_sem=py_send.at[step, b], recv_sem=py_recv.at[step, b],
            device_id=(((y + step) % groups) * batches + seq, ka), device_id_type=MESH,
        )

    def out_copy(which, b):
        span = pl.ds(b * LANES, LANES)
        return pltpu.make_async_remote_copy(
            src_ref=out_ref.at[which, span, :], dst_ref=out_ref.at[which, span, :],
            send_sem=out_send.at[b], recv_sem=out_recv.at[b],
            device_id=(mate, ka), device_id_type=MESH,
        )

    def total_copy(which):
        return pltpu.make_async_remote_copy(
            src_ref=total_in.at[which], dst_ref=total_in.at[which],
            send_sem=total_send, recv_sem=total_recv,
            device_id=(mate, ka), device_id_type=MESH,
        )

    def gradient(xb):
        def tile(j, carry):
            at = pl.ds(pl.multiple_of(j * TILE, TILE), TILE)
            col = col_level[at, :]
            weight = (
                w_row[xb, at, :]
                + jnp.exp2(s_sc[xb, at, :] - col[:, 1:2])
                - jnp.exp2(t_sc[xb, at, :] - col[:, 0:1])
            )
            high_part, low_part = split(weight)
            w_high[at, :] = high_part
            w_low[at, :] = low_part
            return carry

        lax.fori_loop(0, tiles, tile, 0)
        first = nn(q_tr[...], w_high[...])
        product = first[:DS] + first[DS:] + nn(q_tr[0:DS, :], w_low[...])
        for b in range(blocks):
            part[xb, b] = product[:, b * LANES:(b + 1) * LANES]

    def both_gradients(step, carry):
        gradient(jnp.where(step == 0, 1 - x, x))

        @pl.when(step == 0)
        def _():
            for b in range(blocks):
                px_copy(b).start()
        return carry

    lax.fori_loop(0, 2, both_gradients, 0)
    for b in range(blocks):
        px_copy(b).wait_recv()
        x_sum[b] = part[x, b] + x_in[b]
        for step in range(1, groups):
            py_copy(step, b).start()
    for step in range(1, levels):
        div_copy(step, (z - step + levels) % levels).wait_recv()
    total = div_in[0, 0:1, :]
    for level in range(1, levels):
        total = total + div_in[level, 0:1, :]
    total_in[seq] = jnp.broadcast_to(total, (8, rows))
    total_copy(seq).start()
    for b in range(blocks):
        result = x_sum[b]
        for step in range(1, groups):
            py_copy(step, b).wait_recv()
            result = result + y_in[step, b]
        out_ref[seq, b * LANES:(b + 1) * LANES, :] = result.T
        out_copy(seq, b).start()
    total_copy(1 - seq).wait_recv()
    loss_ref[0, 0] = jnp.sum(total_in[0, 0:1, :] + total_in[1, 0:1, :]) / (
        batches * HEADS * rows * 2 * levels
    )
    total_copy(seq).wait_send()
    for copy in x_copies:
        copy.wait_send()

    def sent(j, carry):
        for slot in range(2):
            for to in range(levels):
                goes = source_sends(slot, to)
                if to in (0, last):
                    goes = jnp.logical_or(goes, forwards(slot, to))

                @pl.when(goes)
                def _():
                    for copy in z_copies(slot, j, to):
                        copy.wait_send()
        return carry

    lax.fori_loop(0, chunks, sent, 0)
    for step in range(1, 2 * groups):
        stat_copy(step).wait_send()
    for step in range(1, levels):
        div_copy(step, z).wait_send()
        for xb in range(2):
            col_copy(xb, step).wait_send()
    for b in range(blocks):
        px_copy(b).wait_send()
        for step in range(1, groups):
            py_copy(step, b).wait_send()
        out_copy(seq, b).wait_send()
        out_copy(1 - seq, b).wait_recv()


def folded_kernel(
    groups, levels, rows, batches,
    t_hbm, s_hbm, out_ref, loss_ref,
    in_t, in_s, col_t, col_s, row_t, row_s, t_sc, s_sc, acc,
    row_stat, col_stat, col_part, div_in, wide, col_level, w_row, q_tr, w_high, w_low,
    part, x_in, x_sum, y_in, turned, turned_in, total_in,
    load_sem, slot_sem, x_send, x_recv, z_send, z_recv,
    row_send, row_recv, end_send, end_recv, col_send, col_recv, div_send, div_recv,
    px_send, px_recv, py_send, py_recv, pz_send, pz_recv, out_send, out_recv, total_send, total_recv,
):
    chunks = rows // CHUNK
    pb = lax.axis_index("pb")
    ka = lax.axis_index("ka")
    seq = pb % batches
    y = pb // batches
    z = ka // 2
    x = ka % 2
    place = x * groups + y
    low = jnp.where(seq == 0, y, groups - 1 - y)
    high = levels - 1 - low
    sources = (low, high)
    outer = low == 0
    inner_level = jnp.logical_and(z > 0, z < levels - 1)
    end_level = jnp.logical_not(inner_level)
    active = jnp.logical_or(outer, inner_level)
    turning = jnp.logical_and(outer, inner_level)
    outer_end = jnp.logical_and(outer, end_level)
    y_outer = seq
    y_inner = 1 - seq
    mate = y * batches + (1 - seq)
    x_device = (pb, z * 2 + (1 - x))

    planes = []
    for step in range(1, 2 * groups):
        other = (place + step) % (2 * groups)
        planes.append(((other % groups) * batches + seq, z * 2 + other // groups))
    line = [(pb, ((z + step) % levels) * 2 + x) for step in range(1, levels)]
    barrier = pltpu.get_barrier_semaphore()
    count = 2 * groups * levels
    index = place * levels + z

    def greet(step, carry):
        other = (index + step) % count
        spot, level = other // levels, other % levels
        device = ((spot % groups) * batches + seq, level * 2 + spot // groups)
        pl.semaphore_signal(barrier, inc=1, device_id=device, device_id_type=MESH)
        return carry

    lax.fori_loop(1, count, greet, 0)
    diagonal = (1 - y) * batches + (1 - seq)
    for other in (mate, diagonal):
        pl.semaphore_signal(barrier, inc=1, device_id=(other, ka), device_id_type=MESH)

    loads = [
        pltpu.make_async_copy(t_hbm.at[seq], in_t.at[0], load_sem.at[0]),
        pltpu.make_async_copy(s_hbm.at[seq], in_s.at[0], load_sem.at[1]),
    ]
    for slot in range(2):
        @pl.when(z == sources[slot])
        def _():
            pltpu.make_async_copy(t_hbm.at[seq], col_t.at[slot], slot_sem.at[slot, 0]).start()
            pltpu.make_async_copy(s_hbm.at[seq], col_s.at[slot], slot_sem.at[slot, 1]).start()
    for load in loads:
        load.start()
    pl.semaphore_wait(barrier, count + 1)

    x_copies = [
        pltpu.make_async_remote_copy(
            src_ref=src.at[seq], dst_ref=dst, send_sem=x_send.at[i], recv_sem=x_recv.at[i],
            device_id=x_device, device_id_type=MESH,
        )
        for i, (src, dst) in enumerate(((t_hbm, in_t.at[1]), (s_hbm, in_s.at[1])))
    ]

    def z_copies(slot, j, to):
        span = pl.ds(pl.multiple_of(j * CHUNK, CHUNK), CHUNK)
        return [
            pltpu.make_async_remote_copy(
                src_ref=buf.at[slot, span, :], dst_ref=buf.at[slot, span, :],
                send_sem=z_send.at[to, slot, j, i], recv_sem=z_recv.at[slot, j, i],
                device_id=(pb, to * 2 + x), device_id_type=MESH,
            )
            for i, buf in enumerate((col_t, col_s))
        ]

    for slot in range(2):
        @pl.when(z == sources[slot])
        def _():
            pltpu.make_async_copy(t_hbm.at[seq], col_t.at[slot], slot_sem.at[slot, 0]).wait()
            pltpu.make_async_copy(s_hbm.at[seq], col_s.at[slot], slot_sem.at[slot, 1]).wait()

    last = levels - 1

    def source_sends(slot, to):
        return jnp.logical_and(z == sources[slot], to != z) if 0 < to < last else None

    def forwards(slot, to):
        beside = 1 if to == 0 else last - 1
        return jnp.logical_and(jnp.logical_and(outer, z == beside), sources[slot] != to)

    def put_rows(xb, teacher, student):
        t_high, t_low = split((teacher * (LOG2E / math.sqrt(DT))).T)
        s_high, s_low = split((student * (LOG2E / math.sqrt(DS))).T)
        for part_index, (t_part, s_part) in enumerate(
            ((t_high, s_high), (t_low, s_low), (t_high, s_high))
        ):
            row_t[xb, part_index * DT:(part_index + 1) * DT, :] = t_part
            row_s[xb, part_index * DS:(part_index + 1) * DS, :] = s_part

    def relate(xb, j):
        span = pl.ds(pl.multiple_of(j * CHUNK, CHUNK), CHUNK)
        t_high, t_low = split(col_t[:, span, :].reshape(2 * CHUNK, DT))
        s_high, s_low = split(col_s[:, span, :].reshape(2 * CHUNK, DS))
        teacher = nn(jnp.concatenate([t_high, t_high, t_low], axis=1), row_t[xb])
        student = nn(jnp.concatenate([s_high, s_high, s_low], axis=1), row_s[xb])
        tiles = []
        for slot in range(2):
            base = slot * rows + j * CHUNK
            at = pl.ds(pl.multiple_of(base, CHUNK), CHUNK)
            t_sc[xb, at, :] = teacher[slot * CHUNK:(slot + 1) * CHUNK]
            s_sc[xb, at, :] = student[slot * CHUNK:(slot + 1) * CHUNK]
            tiles += [pl.ds(pl.multiple_of(base + i * PART, PART), PART) for i in range(CHUNK // PART)]

        def read(ref, at):
            return ref[xb, at, :].reshape(PART // 8, 8, rows)

        t_old, s_old = acc[xb, 0], acc[xb, 3]
        t_max, s_max = t_old, s_old
        for at in tiles:
            t_max = jnp.maximum(t_max, jnp.max(read(t_sc, at), axis=0))
            s_max = jnp.maximum(s_max, jnp.max(read(s_sc, at), axis=0))
        t_scale = jnp.exp2(t_old - t_max)
        s_scale = jnp.exp2(s_old - s_max)
        t_sum, cross, s_sum = acc[xb, 1] * t_scale, acc[xb, 2] * t_scale, acc[xb, 4] * s_scale
        for at in tiles:
            t_tile, s_tile = read(t_sc, at), read(s_sc, at)
            t_exp = jnp.exp2(t_tile - t_max[None])
            t_sum = t_sum + jnp.sum(t_exp, axis=0)
            cross = cross + jnp.sum(t_exp * (t_tile - s_tile), axis=0)
            s_sum = s_sum + jnp.sum(jnp.exp2(s_tile - s_max[None]), axis=0)
        acc[xb, 0] = t_max
        acc[xb, 1] = t_sum
        acc[xb, 2] = cross
        acc[xb, 3] = s_max
        acc[xb, 4] = s_sum

    def turn(j):
        for slot in range(2):
            at = pl.ds(pl.multiple_of(slot * rows + j * CHUNK, PART), CHUNK)
            t_top = jnp.max(jnp.maximum(t_sc[0, at, :], t_sc[1, at, :]), axis=1, keepdims=True)
            s_top = jnp.max(jnp.maximum(s_sc[0, at, :], s_sc[1, at, :]), axis=1, keepdims=True)
            t_all = c_all = s_all = jnp.zeros((CHUNK, rows), jnp.float32)
            for xb in range(2):
                t_exp = jnp.exp2(t_sc[xb, at, :] - t_top)
                t_all = t_all + t_exp
                c_all = c_all + t_exp * (t_sc[xb, at, :] - s_sc[xb, at, :])
                s_all = s_all + jnp.exp2(s_sc[xb, at, :] - s_top)
            sums = [jnp.sum(v, axis=1, keepdims=True) for v in (t_all, c_all, s_all)]
            col_part[at, 0:1] = t_top
            col_part[at, 1:2] = sums[0]
            col_part[at, 2:3] = sums[1]
            col_part[at, 3:4] = s_top
            col_part[at, 4:5] = sums[2]
            col_part[at, 5:8] = jnp.zeros((CHUNK, 3), jnp.float32)

    for xb in range(2):
        for kind in range(5):
            start = -jnp.inf if kind in (0, 3) else 0.0
            acc[xb, kind] = jnp.full((8, rows), start, jnp.float32)

    @pl.when(active)
    def _():
        for copy in x_copies:
            copy.start()


    def first_send(j, carry):
        for slot in range(2):
            for to in range(1, last):
                @pl.when(source_sends(slot, to))
                def _():
                    for copy in z_copies(slot, j, to):
                        copy.start()
        return carry

    lax.fori_loop(0, chunks, first_send, 0)
    half = chunks // 2

    def arrive(j):
        for slot in range(2):
            @pl.when(z != sources[slot])
            def _():
                for copy in z_copies(slot, j, 1):
                    copy.wait_recv()
                for to in (0, last):
                    @pl.when(forwards(slot, to))
                    def _():
                        for copy in z_copies(slot, j, to):
                            copy.start()

    def gather(k, carry):
        late = k - half
        phase = jnp.where(k < half, 1, late % 3)
        j = jnp.where(k < half, k, late // 3 + jnp.where(phase == 0, 0, half))
        own = phase == 1

        @pl.when(k == half)
        def _():
            for copy in x_copies:
                copy.wait_recv()

        @pl.when(jnp.logical_or(k == 0, k == half))
        def _():
            which = jnp.where(k == 0, 0, 1)
            put_rows(jnp.where(k == 0, x, 1 - x), in_t[which], in_s[which])

        @pl.when(own)
        def _():
            arrive(j)

        relate(jnp.where(own, x, 1 - x), j)

        @pl.when(jnp.logical_and(turning, jnp.logical_not(own)))
        def _():
            turn(j)
        return carry

    for load in loads:
        load.wait()
    lax.fori_loop(0, jnp.where(active, 2 * chunks, 0), gather, 0)

    mine = jnp.where(inner_level, place, x)

    @pl.when(active)
    def _():
        for xb in range(2):
            t_max, s_max = acc[xb, 0], acc[xb, 3]
            t_top = jnp.max(t_max, axis=0, keepdims=True)
            s_top = jnp.max(s_max, axis=0, keepdims=True)
            t_scale = jnp.exp2(t_max - t_top)
            s_scale = jnp.exp2(s_max - s_top)
            t_sum = jnp.sum(acc[xb, 1] * t_scale, axis=0, keepdims=True)
            cross = jnp.sum(acc[xb, 2] * t_scale, axis=0, keepdims=True)
            s_sum = jnp.sum(acc[xb, 4] * s_scale, axis=0, keepdims=True)
            row_stat[mine, xb] = jnp.concatenate(
                [t_top, t_sum, cross, s_top, s_sum, jnp.zeros((3, rows), jnp.float32)], axis=0
            )

    @pl.when(turning)
    def _():
        for slot in range(2):
            col_stat[slot, 1 + z] = col_part[slot * rows:(slot + 1) * rows, :].T

    def remote(src, dst, send, recv, device):
        return pltpu.make_async_remote_copy(
            src_ref=src, dst_ref=dst, send_sem=send, recv_sem=recv,
            device_id=device, device_id_type=MESH,
        )

    outer_pb = y_outer * batches + seq
    inner_pb = y_inner * batches + seq
    other_inner = last - z
    my_slot = jnp.where(z * 2 < levels, 0, 1)

    def inner_sends():
        copies = [
            remote(row_stat.at[place], row_stat.at[place], row_send.at[step], row_recv.at[place], planes[step - 1])
            for step in range(1, 2 * groups)
        ]
        for xb in range(2):
            copies.append(remote(
                row_stat.at[place, xb], col_stat.at[my_slot, place], col_send.at[xb, 0],
                col_recv.at[my_slot, place], (inner_pb, other_inner * 2 + xb),
            ))
        return copies

    def turning_sends():
        copies = []
        for slot, end in ((0, 0), (1, last)):
            src = col_stat.at[slot, 1 + z]
            for xb in range(2):
                copies.append(remote(
                    src, row_stat.at[1 + z, x], end_send.at[slot, xb], end_recv.at[z - 1, x],
                    (pb, end * 2 + xb),
                ))
            for i, level in enumerate((other_inner, last - end)):
                copies.append(remote(
                    src, col_stat.at[slot, 1 + z], end_send.at[slot, 2 + i], col_recv.at[slot, 1 + z],
                    (pb, level * 2 + x),
                ))
        return copies

    def end_sends():
        copies = [remote(row_stat.at[x], row_stat.at[x], row_send.at[0], row_recv.at[x], x_device)]
        for xb in range(2):
            for i, level in enumerate((1, last - 1, last - z)):
                copies.append(remote(
                    row_stat.at[x, xb], col_stat.at[my_slot, x], col_send.at[xb, 1 + i],
                    col_recv.at[my_slot, x], (pb, level * 2 + xb),
                ))
        return copies

    kinds = ((turning, turning_sends), (inner_level, inner_sends), (outer_end, end_sends))
    for case, sends in kinds:
        @pl.when(case)
        def _():
            for copy in sends():
                copy.start()

    @pl.when(active)
    def _():
        for slot in range(2):
            high_part, low_part = split((col_s[slot] * (1.0 / math.sqrt(DS))).T)
            q_tr[0:DS, slot * rows:(slot + 1) * rows] = high_part
            q_tr[DS:2 * DS, slot * rows:(slot + 1) * rows] = low_part

    def landed(ref, sem):
        remote(ref, ref, row_send.at[0], sem, x_device).wait_recv()

    @pl.when(inner_level)
    def _():
        for step in range(1, 2 * groups):
            other = (place + step) % (2 * groups)
            landed(row_stat.at[other], row_recv.at[other])

    @pl.when(outer_end)
    def _():
        landed(row_stat.at[1 - x], row_recv.at[1 - x])
        for xb in range(2):
            for level in range(2):
                landed(row_stat.at[2 + level, xb], end_recv.at[level, xb])

    def combine(stats):
        t_max = functools.reduce(jnp.maximum, [stat[0:1] for stat in stats])
        s_max = functools.reduce(jnp.maximum, [stat[3:4] for stat in stats])
        t_sum = cross = s_sum = jnp.zeros((1, rows), jnp.float32)
        for stat in stats:
            t_scale = jnp.exp2(stat[0:1] - t_max)
            t_sum = t_sum + stat[1:2] * t_scale
            cross = cross + stat[2:3] * t_scale
            s_sum = s_sum + stat[4:5] * jnp.exp2(stat[3:4] - s_max)
        t_level = t_max + jnp.log2(t_sum)
        s_level = s_max + jnp.log2(s_sum)
        return t_level, s_level, LN2 * (cross / t_sum - t_level + s_level)

    @pl.when(active)
    def _():
        divergence = jnp.zeros((1, rows), jnp.float32)
        for xb in range(2):
            t_level, s_level, share = combine([row_stat[other, xb] for other in range(2 * groups)])
            wide[xb] = jnp.concatenate([t_level, s_level], axis=0)
            divergence = divergence + share
        div_in[z] = jnp.broadcast_to(divergence, (8, rows))

    def div_copy(step, slot):
        return pltpu.make_async_remote_copy(
            src_ref=div_in.at[slot], dst_ref=div_in.at[slot],
            send_sem=div_send.at[step], recv_sem=div_recv.at[step],
            device_id=line[step - 1], device_id_type=MESH,
        )

    @pl.when(outer)
    def _():
        for step in range(1, levels):
            div_copy(step, z).start()

    tiles = 2 * rows // TILE

    def row_weights(xb):
        rows_t = wide[xb, 0:1, :]
        rows_s = wide[xb, 1:2, :]

        def tile(j, carry):
            at = pl.ds(pl.multiple_of(j * TILE, TILE), TILE)
            w_row[xb, at, :] = jnp.exp2(s_sc[xb, at, :] - rows_s) - jnp.exp2(t_sc[xb, at, :] - rows_t)
            return carry

        lax.fori_loop(0, tiles, tile, 0)

    def both_weights(xb, carry):
        row_weights(xb)
        return carry

    passes = jnp.where(active, 2, 0)
    lax.fori_loop(0, passes, both_weights, 0)
    for slot in range(2):
        @pl.when(jnp.logical_and(active, z == sources[slot]))
        def _():
            for other in range(2 * groups):
                col_stat[slot, other] = row_stat[other, x]

        @pl.when(jnp.logical_and(active, z != sources[slot]))
        def _():
            for other in range(2 * groups):
                @pl.when(jnp.logical_not(jnp.logical_and(turning, other == 1 + z)))
                def _():
                    landed(col_stat.at[slot, other], col_recv.at[slot, other])

    @pl.when(active)
    def _():
        for slot in range(2):
            t_level, s_level, _ = combine([col_stat[slot, other] for other in range(2 * groups)])
            both = jnp.concatenate([t_level, s_level, jnp.zeros((6, rows), jnp.float32)], axis=0)
            col_level[slot * rows:(slot + 1) * rows, :] = both.T

    blocks = rows // LANES

    def px_copy(b):
        return pltpu.make_async_remote_copy(
            src_ref=part.at[1 - x, b], dst_ref=x_in.at[b],
            send_sem=px_send.at[b], recv_sem=px_recv.at[b],
            device_id=x_device, device_id_type=MESH,
        )

    def py_copy(step, b):
        return pltpu.make_async_remote_copy(
            src_ref=x_sum.at[b], dst_ref=y_in.at[step, b],
            send_sem=py_send.at[step, b], recv_sem=py_recv.at[step, b],
            device_id=(((y + step) % groups) * batches + seq, ka), device_id_type=MESH,
        )

    def out_copy(which, b):
        span = pl.ds(b * LANES, LANES)
        return pltpu.make_async_remote_copy(
            src_ref=out_ref.at[which, span, :], dst_ref=out_ref.at[which, span, :],
            send_sem=out_send.at[b], recv_sem=out_recv.at[b],
            device_id=(mate, ka), device_id_type=MESH,
        )

    totals = [(((1 - y) * batches + seq), ka), (mate, ka), (diagonal, ka)]

    def total_copy(i):
        return remote(total_in.at[seq], total_in.at[seq], total_send.at[i], total_recv.at[seq], totals[i])

    def turned_copy(slot, b):
        end = 0 if slot == 0 else last
        return remote(
            turned.at[slot, b], turned_in.at[z - 1, b], pz_send.at[slot, b], pz_recv.at[z - 1, b],
            (pb, end * 2 + x),
        )

    def gradient(xb):
        def tile(j, carry):
            at = pl.ds(pl.multiple_of(j * TILE, TILE), TILE)
            col = col_level[at, :]
            weight = (
                w_row[xb, at, :]
                + jnp.exp2(s_sc[xb, at, :] - col[:, 1:2])
                - jnp.exp2(t_sc[xb, at, :] - col[:, 0:1])
            )
            high_part, low_part = split(weight)
            w_high[at, :] = high_part
            w_low[at, :] = low_part
            return carry

        lax.fori_loop(0, tiles, tile, 0)
        first = nn(q_tr[...], w_high[...])
        product = first[:DS] + first[DS:] + nn(q_tr[0:DS, :], w_low[...])
        for b in range(blocks):
            part[xb, b] = product[:, b * LANES:(b + 1) * LANES]

        @pl.when(turning)
        def _():
            q_rows = row_s[xb, 0:2 * DS, :]
            back = nt(q_rows, w_high[...])
            back = (back[:DS] + back[DS:] + nt(q_rows[:DS], w_low[...])) * LN2
            for slot in range(2):
                for b in range(blocks):
                    piece = back[:, slot * rows + b * LANES:slot * rows + (b + 1) * LANES]
                    turned[slot, b] = jnp.where(xb == x, turned[slot, b] + piece, piece)

    def both_gradients(step, carry):
        gradient(jnp.where(step == 0, 1 - x, x))

        @pl.when(step == 0)
        def _():
            for b in range(blocks):
                px_copy(b).start()
        return carry

    lax.fori_loop(0, passes, both_gradients, 0)

    @pl.when(turning)
    def _():
        for b in range(blocks):
            for slot in range(2):
                turned_copy(slot, b).start()

    sends_y = jnp.logical_or(inner_level, outer)
    gets_y = jnp.logical_or(inner_level, jnp.logical_not(outer))
    for b in range(blocks):
        @pl.when(active)
        def _():
            px_copy(b).wait_recv()
            x_sum[b] = part[x, b] + x_in[b]

        @pl.when(outer_end)
        def _():
            for level in range(2):
                landed(turned_in.at[level, b], pz_recv.at[level, b])
                x_sum[b] = x_sum[b] + turned_in[level, b]

        @pl.when(sends_y)
        def _():
            py_copy(1, b).start()

    @pl.when(outer)
    def _():
        for step in range(1, levels):
            div_copy(step, (z - step + levels) % levels).wait_recv()
        total = div_in[0, 0:1, :]
        for level in range(1, levels):
            total = total + div_in[level, 0:1, :]
        total_in[seq] = jnp.broadcast_to(total, (8, rows))
        for i in range(3):
            total_copy(i).start()

    for b in range(blocks):
        span = slice(b * LANES, (b + 1) * LANES)

        @pl.when(gets_y)
        def _():
            py_copy(1, b).wait_recv()

        @pl.when(inner_level)
        def _():
            out_ref[seq, span, :] = (x_sum[b] + y_in[1, b]).T

        @pl.when(outer_end)
        def _():
            out_ref[seq, span, :] = x_sum[b].T

        @pl.when(jnp.logical_not(active))
        def _():
            out_ref[seq, span, :] = y_in[1, b].T
        out_copy(seq, b).start()

    landed(total_in.at[1 - seq], total_recv.at[1 - seq])

    @pl.when(jnp.logical_not(outer))
    def _():
        landed(total_in.at[seq], total_recv.at[seq])
    loss_ref[0, 0] = jnp.sum(total_in[0, 0:1, :] + total_in[1, 0:1, :]) / (
        batches * HEADS * rows * 2 * levels
    )

    @pl.when(outer)
    def _():
        for i in range(3):
            total_copy(i).wait_send()

    @pl.when(active)
    def _():
        for copy in x_copies:
            copy.wait_send()

    def sent(j, carry):
        for slot in range(2):
            for to in range(levels):
                goes = source_sends(slot, to) if 0 < to < last else forwards(slot, to)

                @pl.when(goes)
                def _():
                    for copy in z_copies(slot, j, to):
                        copy.wait_send()
        return carry

    lax.fori_loop(0, chunks, sent, 0)
    for case, sends in kinds:
        @pl.when(case)
        def _():
            for copy in sends():
                copy.wait_send()

    @pl.when(outer)
    def _():
        for step in range(1, levels):
            div_copy(step, z).wait_send()

    for b in range(blocks):
        @pl.when(active)
        def _():
            px_copy(b).wait_send()

        @pl.when(turning)
        def _():
            for slot in range(2):
                turned_copy(slot, b).wait_send()

        @pl.when(sends_y)
        def _():
            py_copy(1, b).wait_send()
        out_copy(seq, b).wait_send()
        out_copy(1 - seq, b).wait_recv()


def solution(mesh):
    def shards(teacher_q, student_q):
        batches, rows = teacher_q.shape[0], teacher_q.shape[1]
        groups = mesh.shape["pb"] // batches
        levels = mesh.shape["ka"] // 2
        chunks = rows // CHUNK
        blocks = rows // LANES
        f32, bf16 = jnp.float32, jnp.bfloat16
        dma = pltpu.SemaphoreType.DMA
        folds = groups == 2 and levels == 4
        chosen = folded_kernel if folds else kernel
        scratch = [
            pltpu.VMEM((2, rows, DT), f32),
            pltpu.VMEM((2, rows, DS), f32),
            pltpu.VMEM((2, rows, DT), f32),
            pltpu.VMEM((2, rows, DS), f32),
            pltpu.VMEM((2, 3 * DT, rows), bf16),
            pltpu.VMEM((2, 3 * DS, rows), bf16),
            pltpu.VMEM((2, 2 * rows, rows), f32),
            pltpu.VMEM((2, 2 * rows, rows), f32),
            pltpu.VMEM((2, 5, 8, rows), f32),
        ]
        scratch += [
            pltpu.VMEM((4, 2, 8, rows), f32),
            pltpu.VMEM((2, 4, 8, rows), f32),
            pltpu.VMEM((2 * rows, 8), f32),
            pltpu.VMEM((levels, 8, rows), f32),
            pltpu.VMEM((2, 2, rows), f32),
            pltpu.VMEM((2 * rows, 8), f32),
            pltpu.VMEM((2, 2 * rows, rows), f32),
            pltpu.VMEM((2 * DS, 2 * rows), bf16),
            pltpu.VMEM((2 * rows, rows), bf16),
            pltpu.VMEM((2 * rows, rows), bf16),
            pltpu.VMEM((2, blocks, DS, LANES), f32),
            pltpu.VMEM((blocks, DS, LANES), f32),
            pltpu.VMEM((blocks, DS, LANES), f32),
            pltpu.VMEM((groups, blocks, DS, LANES), f32),
            pltpu.VMEM((2, blocks, DS, LANES), f32),
            pltpu.VMEM((2, blocks, DS, LANES), f32),
            pltpu.VMEM((batches, 8, rows), f32),
            dma((2,)),
            dma((2, 2)),
            dma((2,)),
            dma((2,)),
            dma((levels, 2, chunks, 2)),
            dma((2, chunks, 2)),
            dma((4,)),
            dma((4,)),
            dma((2, 4)),
            dma((2, 2)),
            dma((2, 4)),
            dma((2, 4)),
            dma((levels,)),
            dma((levels,)),
            dma((blocks,)),
            dma((blocks,)),
            dma((groups, blocks)),
            dma((groups, blocks)),
            dma((2, blocks)),
            dma((2, blocks)),
            dma((blocks,)),
            dma((blocks,)),
            dma((3,)),
            dma((2,)),
        ] if folds else [
            pltpu.VMEM((2 * groups, 2, 8, rows), f32),
            pltpu.VMEM((2, 2 * groups, 8, rows), f32),
            pltpu.VMEM((levels, 8, rows), f32),
            pltpu.VMEM((2, 2, rows), f32),
            pltpu.VMEM((2 * rows, 8), f32),
            pltpu.VMEM((2, 2 * rows, rows), f32),
            pltpu.VMEM((2 * DS, 2 * rows), bf16),
            pltpu.VMEM((2 * rows, rows), bf16),
            pltpu.VMEM((2 * rows, rows), bf16),
            pltpu.VMEM((2, blocks, DS, LANES), f32),
            pltpu.VMEM((blocks, DS, LANES), f32),
            pltpu.VMEM((blocks, DS, LANES), f32),
            pltpu.VMEM((groups, blocks, DS, LANES), f32),
            pltpu.VMEM((batches, 8, rows), f32),
            dma((2,)),
            dma((2, 2)),
            dma((2,)),
            dma((2,)),
            dma((levels, 2, chunks, 2)),
            dma((2, chunks, 2)),
            dma((2 * groups,)),
            dma((2 * groups,)),
            dma((2, levels)),
            dma((2, 2 * groups)),
            dma((levels,)),
            dma((levels,)),
            dma((blocks,)),
            dma((blocks,)),
            dma((groups, blocks)),
            dma((groups, blocks)),
            dma((blocks,)),
            dma((blocks,)),
            dma,
            dma,
        ]
        grad, loss = pl.pallas_call(
            functools.partial(chosen, groups, levels, rows, batches),
            out_shape=(
                jax.ShapeDtypeStruct((batches, rows, DS), f32),
                jax.ShapeDtypeStruct((1, 1), f32),
            ),
            in_specs=[pl.BlockSpec(memory_space=pl.ANY)] * 2,
            out_specs=(
                pl.BlockSpec(memory_space=pltpu.VMEM),
                pl.BlockSpec(memory_space=pltpu.SMEM),
            ),
            scratch_shapes=scratch,
            compiler_params=pltpu.CompilerParams(
                collective_id=1 if folds else 0, has_side_effects=True, vmem_limit_bytes=60 * 1024 * 1024
            ),
        )(teacher_q, student_q)
        return grad, loss.reshape(())

    in_specs = (P(None, "ka", None), P(None, "ka", None))
    out_specs = (P(None, "ka", None), P())
    return jax.shard_map(shards, mesh=mesh, in_specs=in_specs, out_specs=out_specs, check_vma=False)
```

```python
import functools
import math

import jax
import jax.numpy as jnp
from jax import lax
from jax.experimental import pallas as pl
from jax.experimental.pallas import tpu as pltpu
from jax.sharding import PartitionSpec as P

HEADS = 1
DT = 256
DS = 128
CHUNK = 96
LANES = 128
TILE = 64
PART = 32
MESH = pl.DeviceIdType.MESH
LOG2E = 1.4426950408889634
LN2 = 0.6931471805599453


def split(values):
    high = values.astype(jnp.bfloat16)
    low = (values - high.astype(jnp.float32)).astype(jnp.bfloat16)
    return high, low


def nn(left, right):
    return jnp.dot(left, right, preferred_element_type=jnp.float32)


def kernel(
    groups, levels, rows, batches,
    t_hbm, s_hbm, out_ref, loss_ref,
    in_t, in_s, col_t, col_s, row_t, row_s, t_sc, s_sc, acc,
    stat_in, stat_col, div_in, wide, col_level, w_row, q_tr, w_high, w_low,
    part, x_in, x_sum, y_in, total_in,
    load_sem, slot_sem, x_send, x_recv, z_send, z_recv,
    stat_send, stat_recv, col_send, col_recv, div_send, div_recv,
    px_send, px_recv, py_send, py_recv, out_send, out_recv, total_send, total_recv,
):
    chunks = rows // CHUNK
    pb = lax.axis_index("pb")
    ka = lax.axis_index("ka")
    seq = pb % batches
    y = pb // batches
    z = ka // 2
    x = ka % 2
    place = x * groups + y
    low = jnp.where(seq == 0, y, groups - 1 - y)
    high = levels - 1 - low
    sources = (low, high)
    mate = y * batches + (1 - seq)
    x_device = (pb, z * 2 + (1 - x))

    planes = []
    for step in range(1, 2 * groups):
        other = (place + step) % (2 * groups)
        planes.append(((other % groups) * batches + seq, z * 2 + other // groups))
    line = [(pb, ((z + step) % levels) * 2 + x) for step in range(1, levels)]
    barrier = pltpu.get_barrier_semaphore()
    count = 2 * groups * levels
    index = place * levels + z

    def greet(step, carry):
        other = (index + step) % count
        spot, level = other // levels, other % levels
        device = ((spot % groups) * batches + seq, level * 2 + spot // groups)
        pl.semaphore_signal(barrier, inc=1, device_id=device, device_id_type=MESH)
        return carry

    lax.fori_loop(1, count, greet, 0)
    pl.semaphore_signal(barrier, inc=1, device_id=(mate, ka), device_id_type=MESH)

    loads = [
        pltpu.make_async_copy(t_hbm.at[seq], in_t.at[0], load_sem.at[0]),
        pltpu.make_async_copy(s_hbm.at[seq], in_s.at[0], load_sem.at[1]),
    ]
    for slot in range(2):
        @pl.when(z == sources[slot])
        def _():
            pltpu.make_async_copy(t_hbm.at[seq], col_t.at[slot], slot_sem.at[slot, 0]).start()
            pltpu.make_async_copy(s_hbm.at[seq], col_s.at[slot], slot_sem.at[slot, 1]).start()
    for load in loads:
        load.start()
    pl.semaphore_wait(barrier, count)

    x_copies = [
        pltpu.make_async_remote_copy(
            src_ref=src.at[seq], dst_ref=dst, send_sem=x_send.at[i], recv_sem=x_recv.at[i],
            device_id=x_device, device_id_type=MESH,
        )
        for i, (src, dst) in enumerate(((t_hbm, in_t.at[1]), (s_hbm, in_s.at[1])))
    ]

    def z_copies(slot, j, to):
        span = pl.ds(pl.multiple_of(j * CHUNK, CHUNK), CHUNK)
        return [
            pltpu.make_async_remote_copy(
                src_ref=buf.at[slot, span, :], dst_ref=buf.at[slot, span, :],
                send_sem=z_send.at[to, slot, j, i], recv_sem=z_recv.at[slot, j, i],
                device_id=(pb, to * 2 + x), device_id_type=MESH,
            )
            for i, buf in enumerate((col_t, col_s))
        ]

    for slot in range(2):
        @pl.when(z == sources[slot])
        def _():
            pltpu.make_async_copy(t_hbm.at[seq], col_t.at[slot], slot_sem.at[slot, 0]).wait()
            pltpu.make_async_copy(s_hbm.at[seq], col_s.at[slot], slot_sem.at[slot, 1]).wait()

    last = levels - 1

    def source_sends(slot, to):
        near = abs(z - to) == 1
        reach = (to != z) if 0 < to < last else near
        return jnp.logical_and(z == sources[slot], reach)

    def forwards(slot, to):
        beside = 1 if to == 0 else last - 1
        waits = jnp.logical_and(sources[slot] != z, sources[slot] != to)
        return jnp.logical_and(z == beside, waits)

    def put_rows(xb, teacher, student):
        t_high, t_low = split((teacher * (LOG2E / math.sqrt(DT))).T)
        s_high, s_low = split((student * (LOG2E / math.sqrt(DS))).T)
        for part_index, (t_part, s_part) in enumerate(
            ((t_high, s_high), (t_low, s_low), (t_high, s_high))
        ):
            row_t[xb, part_index * DT:(part_index + 1) * DT, :] = t_part
            row_s[xb, part_index * DS:(part_index + 1) * DS, :] = s_part

    def relate(xb, j):
        span = pl.ds(pl.multiple_of(j * CHUNK, CHUNK), CHUNK)
        t_high, t_low = split(col_t[:, span, :].reshape(2 * CHUNK, DT))
        s_high, s_low = split(col_s[:, span, :].reshape(2 * CHUNK, DS))
        teacher = nn(jnp.concatenate([t_high, t_high, t_low], axis=1), row_t[xb])
        student = nn(jnp.concatenate([s_high, s_high, s_low], axis=1), row_s[xb])
        tiles = []
        for slot in range(2):
            base = slot * rows + j * CHUNK
            at = pl.ds(pl.multiple_of(base, CHUNK), CHUNK)
            t_sc[xb, at, :] = teacher[slot * CHUNK:(slot + 1) * CHUNK]
            s_sc[xb, at, :] = student[slot * CHUNK:(slot + 1) * CHUNK]
            tiles += [pl.ds(pl.multiple_of(base + i * PART, PART), PART) for i in range(CHUNK // PART)]

        def read(ref, at):
            return ref[xb, at, :].reshape(PART // 8, 8, rows)

        t_old, s_old = acc[xb, 0], acc[xb, 3]
        t_max, s_max = t_old, s_old
        for at in tiles:
            t_max = jnp.maximum(t_max, jnp.max(read(t_sc, at), axis=0))
            s_max = jnp.maximum(s_max, jnp.max(read(s_sc, at), axis=0))
        t_scale = jnp.exp2(t_old - t_max)
        s_scale = jnp.exp2(s_old - s_max)
        t_sum, cross, s_sum = acc[xb, 1] * t_scale, acc[xb, 2] * t_scale, acc[xb, 4] * s_scale
        for at in tiles:
            t_tile, s_tile = read(t_sc, at), read(s_sc, at)
            t_exp = jnp.exp2(t_tile - t_max[None])
            t_sum = t_sum + jnp.sum(t_exp, axis=0)
            cross = cross + jnp.sum(t_exp * (t_tile - s_tile), axis=0)
            s_sum = s_sum + jnp.sum(jnp.exp2(s_tile - s_max[None]), axis=0)
        acc[xb, 0] = t_max
        acc[xb, 1] = t_sum
        acc[xb, 2] = cross
        acc[xb, 3] = s_max
        acc[xb, 4] = s_sum

    for xb in range(2):
        for kind in range(5):
            start = -jnp.inf if kind in (0, 3) else 0.0
            acc[xb, kind] = jnp.full((8, rows), start, jnp.float32)

    for copy in x_copies:
        copy.start()

    def first_send(j, carry):
        for slot in range(2):
            for to in range(levels):
                @pl.when(source_sends(slot, to))
                def _():
                    for copy in z_copies(slot, j, to):
                        copy.start()
        return carry

    lax.fori_loop(0, chunks, first_send, 0)
    half = chunks // 2

    def arrive(j):
        for slot in range(2):
            @pl.when(z != sources[slot])
            def _():
                for copy in z_copies(slot, j, 1):
                    copy.wait_recv()
                for to in (0, last):
                    @pl.when(forwards(slot, to))
                    def _():
                        for copy in z_copies(slot, j, to):
                            copy.start()

    def gather(k, carry):
        late = k - half
        phase = jnp.where(k < half, 1, late % 3)
        j = jnp.where(k < half, k, late // 3 + jnp.where(phase == 0, 0, half))
        own = phase == 1

        @pl.when(k == 0)
        def _():
            for load in loads:
                load.wait()

        @pl.when(k == half)
        def _():
            for copy in x_copies:
                copy.wait_recv()

        @pl.when(jnp.logical_or(k == 0, k == half))
        def _():
            which = jnp.where(k == 0, 0, 1)
            put_rows(jnp.where(k == 0, x, 1 - x), in_t[which], in_s[which])

        @pl.when(own)
        def _():
            arrive(j)

        relate(jnp.where(own, x, 1 - x), j)
        return carry

    lax.fori_loop(0, 2 * chunks, gather, 0)

    for xb in range(2):
        t_max, s_max = acc[xb, 0], acc[xb, 3]
        t_top = jnp.max(t_max, axis=0, keepdims=True)
        s_top = jnp.max(s_max, axis=0, keepdims=True)
        t_scale = jnp.exp2(t_max - t_top)
        s_scale = jnp.exp2(s_max - s_top)
        t_sum = jnp.sum(acc[xb, 1] * t_scale, axis=0, keepdims=True)
        cross = jnp.sum(acc[xb, 2] * t_scale, axis=0, keepdims=True)
        s_sum = jnp.sum(acc[xb, 4] * s_scale, axis=0, keepdims=True)
        stat_in[place, xb] = jnp.concatenate(
            [t_top, t_sum, cross, s_top, s_sum, jnp.zeros((3, rows), jnp.float32)], axis=0
        )

    def stat_copy(step):
        return pltpu.make_async_remote_copy(
            src_ref=stat_in.at[place], dst_ref=stat_in.at[place],
            send_sem=stat_send.at[step], recv_sem=stat_recv.at[step],
            device_id=planes[step - 1], device_id_type=MESH,
        )

    def stat_wait(step):
        return pltpu.make_async_remote_copy(
            src_ref=stat_in.at[(place - step + 2 * groups) % (2 * groups)],
            dst_ref=stat_in.at[(place - step + 2 * groups) % (2 * groups)],
            send_sem=stat_send.at[step], recv_sem=stat_recv.at[step],
            device_id=planes[step - 1], device_id_type=MESH,
        )

    near = jnp.minimum(z, levels - 1 - z)
    user = jnp.where(seq == 0, near, groups - 1 - near)
    my_slot = jnp.where(z == near, 0, 1)

    def col_copy(xb, step):
        return pltpu.make_async_remote_copy(
            src_ref=stat_in.at[place, xb], dst_ref=stat_col.at[my_slot, place],
            send_sem=col_send.at[xb, step], recv_sem=col_recv.at[my_slot, place],
            device_id=(user * batches + seq, ((z + step) % levels) * 2 + xb), device_id_type=MESH,
        )

    for step in range(1, levels):
        for xb in range(2):
            col_copy(xb, step).start()
    for step in range(1, 2 * groups):
        stat_copy(step).start()
    for slot in range(2):
        high_part, low_part = split((col_s[slot] * (1.0 / math.sqrt(DS))).T)
        q_tr[0:DS, slot * rows:(slot + 1) * rows] = high_part
        q_tr[DS:2 * DS, slot * rows:(slot + 1) * rows] = low_part
    for step in range(1, 2 * groups):
        stat_wait(step).wait_recv()

    def combine(stats):
        t_max = functools.reduce(jnp.maximum, [stat[0:1] for stat in stats])
        s_max = functools.reduce(jnp.maximum, [stat[3:4] for stat in stats])
        t_sum = cross = s_sum = jnp.zeros((1, rows), jnp.float32)
        for stat in stats:
            t_scale = jnp.exp2(stat[0:1] - t_max)
            t_sum = t_sum + stat[1:2] * t_scale
            cross = cross + stat[2:3] * t_scale
            s_sum = s_sum + stat[4:5] * jnp.exp2(stat[3:4] - s_max)
        t_level = t_max + jnp.log2(t_sum)
        s_level = s_max + jnp.log2(s_sum)
        return t_level, s_level, LN2 * (cross / t_sum - t_level + s_level)

    divergence = jnp.zeros((1, rows), jnp.float32)
    for xb in range(2):
        t_level, s_level, share = combine([stat_in[other, xb] for other in range(2 * groups)])
        wide[xb] = jnp.concatenate([t_level, s_level], axis=0)
        divergence = divergence + share
    div_in[z] = jnp.broadcast_to(divergence, (8, rows))

    def div_copy(step, slot):
        return pltpu.make_async_remote_copy(
            src_ref=div_in.at[slot], dst_ref=div_in.at[slot],
            send_sem=div_send.at[step], recv_sem=div_recv.at[step],
            device_id=line[step - 1], device_id_type=MESH,
        )

    for step in range(1, levels):
        div_copy(step, z).start()

    tiles = 2 * rows // TILE

    def row_weights(xb):
        rows_t = wide[xb, 0:1, :]
        rows_s = wide[xb, 1:2, :]

        def tile(j, carry):
            at = pl.ds(pl.multiple_of(j * TILE, TILE), TILE)
            w_row[xb, at, :] = jnp.exp2(s_sc[xb, at, :] - rows_s) - jnp.exp2(t_sc[xb, at, :] - rows_t)
            return carry

        lax.fori_loop(0, tiles, tile, 0)

    def both_weights(xb, carry):
        row_weights(xb)
        return carry

    lax.fori_loop(0, 2, both_weights, 0)
    for slot in range(2):
        @pl.when(z == sources[slot])
        def _():
            for other in range(2 * groups):
                stat_col[slot, other] = stat_in[other, x]

        @pl.when(z != sources[slot])
        def _():
            for other in range(2 * groups):
                pltpu.make_async_remote_copy(
                    src_ref=stat_col.at[slot, other], dst_ref=stat_col.at[slot, other],
                    send_sem=col_send.at[0, 0], recv_sem=col_recv.at[slot, other],
                    device_id=x_device, device_id_type=MESH,
                ).wait_recv()

        t_level, s_level, _ = combine([stat_col[slot, other] for other in range(2 * groups)])
        both = jnp.concatenate([t_level, s_level, jnp.zeros((6, rows), jnp.float32)], axis=0)
        col_level[slot * rows:(slot + 1) * rows, :] = both.T

    blocks = rows // LANES

    def px_copy(b):
        return pltpu.make_async_remote_copy(
            src_ref=part.at[1 - x, b], dst_ref=x_in.at[b],
            send_sem=px_send.at[b], recv_sem=px_recv.at[b],
            device_id=x_device, device_id_type=MESH,
        )

    def py_copy(step, b):
        return pltpu.make_async_remote_copy(
            src_ref=x_sum.at[b], dst_ref=y_in.at[step, b],
            send_sem=py_send.at[step, b], recv_sem=py_recv.at[step, b],
            device_id=(((y + step) % groups) * batches + seq, ka), device_id_type=MESH,
        )

    def out_copy(which, b):
        span = pl.ds(b * LANES, LANES)
        return pltpu.make_async_remote_copy(
            src_ref=out_ref.at[which, span, :], dst_ref=out_ref.at[which, span, :],
            send_sem=out_send.at[b], recv_sem=out_recv.at[b],
            device_id=(mate, ka), device_id_type=MESH,
        )

    def total_copy(which):
        return pltpu.make_async_remote_copy(
            src_ref=total_in.at[which], dst_ref=total_in.at[which],
            send_sem=total_send, recv_sem=total_recv,
            device_id=(mate, ka), device_id_type=MESH,
        )

    def gradient(xb):
        def tile(j, carry):
            at = pl.ds(pl.multiple_of(j * TILE, TILE), TILE)
            col = col_level[at, :]
            weight = (
                w_row[xb, at, :]
                + jnp.exp2(s_sc[xb, at, :] - col[:, 1:2])
                - jnp.exp2(t_sc[xb, at, :] - col[:, 0:1])
            )
            high_part, low_part = split(weight)
            w_high[at, :] = high_part
            w_low[at, :] = low_part
            return carry

        lax.fori_loop(0, tiles, tile, 0)
        first = nn(q_tr[...], w_high[...])
        product = first[:DS] + first[DS:] + nn(q_tr[0:DS, :], w_low[...])
        for b in range(blocks):
            part[xb, b] = product[:, b * LANES:(b + 1) * LANES]

    def both_gradients(step, carry):
        gradient(jnp.where(step == 0, 1 - x, x))

        @pl.when(step == 0)
        def _():
            for b in range(blocks):
                px_copy(b).start()
        return carry

    lax.fori_loop(0, 2, both_gradients, 0)
    for b in range(blocks):
        px_copy(b).wait_recv()
        x_sum[b] = part[x, b] + x_in[b]
        for step in range(1, groups):
            py_copy(step, b).start()
    for step in range(1, levels):
        div_copy(step, (z - step + levels) % levels).wait_recv()
    total = div_in[0, 0:1, :]
    for level in range(1, levels):
        total = total + div_in[level, 0:1, :]
    total_in[seq] = jnp.broadcast_to(total, (8, rows))
    total_copy(seq).start()
    for b in range(blocks):
        result = x_sum[b]
        for step in range(1, groups):
            py_copy(step, b).wait_recv()
            result = result + y_in[step, b]
        out_ref[seq, b * LANES:(b + 1) * LANES, :] = result.T
        out_copy(seq, b).start()
    total_copy(1 - seq).wait_recv()
    loss_ref[0, 0] = jnp.sum(total_in[0, 0:1, :] + total_in[1, 0:1, :]) / (
        batches * HEADS * rows * 2 * levels
    )
    total_copy(seq).wait_send()
    for copy in x_copies:
        copy.wait_send()

    def sent(j, carry):
        for slot in range(2):
            for to in range(levels):
                goes = source_sends(slot, to)
                if to in (0, last):
                    goes = jnp.logical_or(goes, forwards(slot, to))

                @pl.when(goes)
                def _():
                    for copy in z_copies(slot, j, to):
                        copy.wait_send()
        return carry

    lax.fori_loop(0, chunks, sent, 0)
    for step in range(1, 2 * groups):
        stat_copy(step).wait_send()
    for step in range(1, levels):
        div_copy(step, z).wait_send()
        for xb in range(2):
            col_copy(xb, step).wait_send()
    for b in range(blocks):
        px_copy(b).wait_send()
        for step in range(1, groups):
            py_copy(step, b).wait_send()
        out_copy(seq, b).wait_send()
        out_copy(1 - seq, b).wait_recv()


def folded_kernel(
    groups, levels, rows, batches,
    t_hbm, s_hbm, out_ref, loss_ref,
    in_t, in_s, row_n, col_t, col_s, row_t, row_s, t_sc, s_sc, acc,
    row_stat, col_stat, col_part, div_in, wide, col_level, w_row, q_tr, w_high, w_low,
    part, x_in, x_sum, y_in, turned, turned_in, total_in,
    load_sem, slot_sem, x_send, x_recv, z_send, z_recv,
    row_send, row_recv, end_send, end_recv, col_send, col_recv, div_send, div_recv,
    px_send, px_recv, py_send, py_recv, pz_send, pz_recv, out_send, out_recv, total_send, total_recv,
):
    chunks = rows // CHUNK
    pb = lax.axis_index("pb")
    ka = lax.axis_index("ka")
    seq = pb % batches
    y = pb // batches
    z = ka // 2
    x = ka % 2
    place = x * groups + y
    low = jnp.where(seq == 0, y, groups - 1 - y)
    high = levels - 1 - low
    sources = (low, high)
    outer = low == 0
    inner_level = jnp.logical_and(z > 0, z < levels - 1)
    end_level = jnp.logical_not(inner_level)
    active = jnp.logical_or(outer, inner_level)
    turning = jnp.logical_and(outer, inner_level)
    outer_end = jnp.logical_and(outer, end_level)
    y_outer = seq
    y_inner = 1 - seq
    mate = y * batches + (1 - seq)
    x_device = (pb, z * 2 + (1 - x))

    planes = []
    for step in range(1, 2 * groups):
        other = (place + step) % (2 * groups)
        planes.append(((other % groups) * batches + seq, z * 2 + other // groups))
    line = [(pb, ((z + step) % levels) * 2 + x) for step in range(1, levels)]
    barrier = pltpu.get_barrier_semaphore()
    count = 2 * groups * levels
    index = place * levels + z

    def greet(step, carry):
        other = (index + step) % count
        spot, level = other // levels, other % levels
        device = ((spot % groups) * batches + seq, level * 2 + spot // groups)
        pl.semaphore_signal(barrier, inc=1, device_id=device, device_id_type=MESH)
        return carry

    lax.fori_loop(1, count, greet, 0)
    diagonal = (1 - y) * batches + (1 - seq)
    for other in (mate, diagonal):
        pl.semaphore_signal(barrier, inc=1, device_id=(other, ka), device_id_type=MESH)

    loads = [
        pltpu.make_async_copy(t_hbm.at[seq], in_t.at[0], load_sem.at[0]),
        pltpu.make_async_copy(s_hbm.at[seq], in_s.at[0], load_sem.at[1]),
    ]
    for slot in range(2):
        @pl.when(z == sources[slot])
        def _():
            pltpu.make_async_copy(t_hbm.at[seq], col_t.at[slot], slot_sem.at[slot, 0]).start()
            pltpu.make_async_copy(s_hbm.at[seq], col_s.at[slot], slot_sem.at[slot, 1]).start()
    for load in loads:
        load.start()
    pl.semaphore_wait(barrier, count + 1)

    y_device = ((1 - y) * batches + seq, ka)

    def piece_copies(q, over_x):
        span = pl.ds(pl.multiple_of(q * CHUNK, CHUNK), CHUNK)
        return [
            pltpu.make_async_remote_copy(
                src_ref=src.at[seq, span, :] if over_x else dst.at[1, span, :], dst_ref=dst.at[1, span, :],
                send_sem=x_send.at[0 if over_x else 1, q, i], recv_sem=x_recv.at[q, i],
                device_id=x_device if over_x else y_device, device_id_type=MESH,
            )
            for i, (src, dst) in enumerate(((t_hbm, in_t), (s_hbm, in_s)))
        ]

    def z_copies(slot, j, to):
        span = pl.ds(pl.multiple_of(j * CHUNK, CHUNK), CHUNK)
        return [
            pltpu.make_async_remote_copy(
                src_ref=buf.at[slot, span, :], dst_ref=buf.at[slot, span, :],
                send_sem=z_send.at[to, slot, j, i], recv_sem=z_recv.at[slot, j, i],
                device_id=(pb, to * 2 + x), device_id_type=MESH,
            )
            for i, buf in enumerate((col_t, col_s))
        ]

    for slot in range(2):
        @pl.when(z == sources[slot])
        def _():
            pltpu.make_async_copy(t_hbm.at[seq], col_t.at[slot], slot_sem.at[slot, 0]).wait()
            pltpu.make_async_copy(s_hbm.at[seq], col_s.at[slot], slot_sem.at[slot, 1]).wait()

    last = levels - 1

    def source_sends(slot, to):
        return jnp.logical_and(z == sources[slot], to != z) if 0 < to < last else None

    def forwards(slot, to):
        beside = 1 if to == 0 else last - 1
        return jnp.logical_and(jnp.logical_and(outer, z == beside), sources[slot] != to)

    def put_rows(xb, teacher, student):
        t_high, t_low = split((teacher * (LOG2E / math.sqrt(DT))).T)
        s_high, s_low = split((student * (LOG2E / math.sqrt(DS))).T)
        row_n[xb] = jnp.concatenate(split(student * (1.0 / math.sqrt(DS))), axis=1)
        for part_index, (t_part, s_part) in enumerate(
            ((t_high, s_high), (t_low, s_low), (t_high, s_high))
        ):
            row_t[xb, part_index * DT:(part_index + 1) * DT, :] = t_part
            row_s[xb, part_index * DS:(part_index + 1) * DS, :] = s_part

    def relate(xb, j):
        span = pl.ds(pl.multiple_of(j * CHUNK, CHUNK), CHUNK)
        t_high, t_low = split(col_t[:, span, :].reshape(2 * CHUNK, DT))
        s_high, s_low = split(col_s[:, span, :].reshape(2 * CHUNK, DS))
        teacher = nn(jnp.concatenate([t_high, t_high, t_low], axis=1), row_t[xb])
        student = nn(jnp.concatenate([s_high, s_high, s_low], axis=1), row_s[xb])
        tiles = []
        for slot in range(2):
            base = slot * rows + j * CHUNK
            at = pl.ds(pl.multiple_of(base, CHUNK), CHUNK)
            t_sc[xb, at, :] = teacher[slot * CHUNK:(slot + 1) * CHUNK]
            s_sc[xb, at, :] = student[slot * CHUNK:(slot + 1) * CHUNK]
            tiles += [pl.ds(pl.multiple_of(base + i * PART, PART), PART) for i in range(CHUNK // PART)]

        def read(ref, at):
            return ref[xb, at, :].reshape(PART // 8, 8, rows)

        t_old, s_old = acc[xb, 0], acc[xb, 3]
        t_max, s_max = t_old, s_old
        for at in tiles:
            t_max = jnp.maximum(t_max, jnp.max(read(t_sc, at), axis=0))
            s_max = jnp.maximum(s_max, jnp.max(read(s_sc, at), axis=0))
        t_scale = jnp.exp2(t_old - t_max)
        s_scale = jnp.exp2(s_old - s_max)
        t_sum, cross, s_sum = acc[xb, 1] * t_scale, acc[xb, 2] * t_scale, acc[xb, 4] * s_scale
        for at in tiles:
            t_tile, s_tile = read(t_sc, at), read(s_sc, at)
            t_exp = jnp.exp2(t_tile - t_max[None])
            t_sum = t_sum + jnp.sum(t_exp, axis=0)
            cross = cross + jnp.sum(t_exp * (t_tile - s_tile), axis=0)
            s_sum = s_sum + jnp.sum(jnp.exp2(s_tile - s_max[None]), axis=0)
        acc[xb, 0] = t_max
        acc[xb, 1] = t_sum
        acc[xb, 2] = cross
        acc[xb, 3] = s_max
        acc[xb, 4] = s_sum

    def turn(j):
        for slot in range(2):
            at = pl.ds(pl.multiple_of(slot * rows + j * CHUNK, PART), CHUNK)
            t_top = jnp.max(jnp.maximum(t_sc[0, at, :], t_sc[1, at, :]), axis=1, keepdims=True)
            s_top = jnp.max(jnp.maximum(s_sc[0, at, :], s_sc[1, at, :]), axis=1, keepdims=True)
            t_all = c_all = s_all = jnp.zeros((CHUNK, rows), jnp.float32)
            for xb in range(2):
                t_exp = jnp.exp2(t_sc[xb, at, :] - t_top)
                t_all = t_all + t_exp
                c_all = c_all + t_exp * (t_sc[xb, at, :] - s_sc[xb, at, :])
                s_all = s_all + jnp.exp2(s_sc[xb, at, :] - s_top)
            sums = [jnp.sum(v, axis=1, keepdims=True) for v in (t_all, c_all, s_all)]
            col_part[at, 0:1] = t_top
            col_part[at, 1:2] = sums[0]
            col_part[at, 2:3] = sums[1]
            col_part[at, 3:4] = s_top
            col_part[at, 4:5] = sums[2]
            col_part[at, 5:8] = jnp.zeros((CHUNK, 3), jnp.float32)

    for xb in range(2):
        for kind in range(5):
            start = -jnp.inf if kind in (0, 3) else 0.0
            acc[xb, kind] = jnp.full((8, rows), start, jnp.float32)

    half = chunks // 2

    @pl.when(active)
    def _():
        for q in range(chunks):
            @pl.when(jnp.logical_or(end_level, q // half == y))
            def _():
                for copy in piece_copies(q, True):
                    copy.start()


    def first_send(j, carry):
        for slot in range(2):
            for to in range(1, last):
                @pl.when(source_sends(slot, to))
                def _():
                    for copy in z_copies(slot, j, to):
                        copy.start()
        return carry

    lax.fori_loop(0, chunks, first_send, 0)
    def arrive(j):
        for slot in range(2):
            @pl.when(z != sources[slot])
            def _():
                for copy in z_copies(slot, j, 1):
                    copy.wait_recv()
                for to in (0, last):
                    @pl.when(forwards(slot, to))
                    def _():
                        for copy in z_copies(slot, j, to):
                            copy.start()

    def gather(k, carry):
        late = k - half
        phase = jnp.where(k < half, 1, late % 3)
        j = jnp.where(k < half, k, late // 3 + jnp.where(phase == 0, 0, half))
        own = phase == 1

        @pl.when(k == half)
        def _():
            for q in range(chunks):
                @pl.when(jnp.logical_or(end_level, q // half != y))
                def _():
                    for copy in piece_copies(q, True):
                        copy.wait_recv()

        @pl.when(jnp.logical_or(k == 0, k == half))
        def _():
            which = jnp.where(k == 0, 0, 1)
            put_rows(jnp.where(k == 0, x, 1 - x), in_t[which], in_s[which])

        @pl.when(own)
        def _():
            arrive(j)

        @pl.when(jnp.logical_and(inner_level, k < half))
        def _():
            for copy in piece_copies(y * half + k, True):
                copy.wait_recv()
            for copy in piece_copies(y * half + k, False):
                copy.start()

        relate(jnp.where(own, x, 1 - x), j)

        @pl.when(jnp.logical_and(turning, jnp.logical_not(own)))
        def _():
            turn(j)
        return carry

    for load in loads:
        load.wait()
    lax.fori_loop(0, jnp.where(active, 2 * chunks, 0), gather, 0)

    mine = jnp.where(inner_level, place, x)

    @pl.when(active)
    def _():
        for xb in range(2):
            t_max, s_max = acc[xb, 0], acc[xb, 3]
            t_top = jnp.max(t_max, axis=0, keepdims=True)
            s_top = jnp.max(s_max, axis=0, keepdims=True)
            t_scale = jnp.exp2(t_max - t_top)
            s_scale = jnp.exp2(s_max - s_top)
            t_sum = jnp.sum(acc[xb, 1] * t_scale, axis=0, keepdims=True)
            cross = jnp.sum(acc[xb, 2] * t_scale, axis=0, keepdims=True)
            s_sum = jnp.sum(acc[xb, 4] * s_scale, axis=0, keepdims=True)
            row_stat[mine, xb] = jnp.concatenate(
                [t_top, t_sum, cross, s_top, s_sum, jnp.zeros((3, rows), jnp.float32)], axis=0
            )

    @pl.when(turning)
    def _():
        for slot in range(2):
            col_stat[slot, 1 + z] = col_part[slot * rows:(slot + 1) * rows, :].T

    def remote(src, dst, send, recv, device):
        return pltpu.make_async_remote_copy(
            src_ref=src, dst_ref=dst, send_sem=send, recv_sem=recv,
            device_id=device, device_id_type=MESH,
        )

    outer_pb = y_outer * batches + seq
    inner_pb = y_inner * batches + seq
    other_inner = last - z
    my_slot = jnp.where(z * 2 < levels, 0, 1)

    def inner_sends():
        copies = [
            remote(row_stat.at[place], row_stat.at[place], row_send.at[step], row_recv.at[place], planes[step - 1])
            for step in range(1, 2 * groups)
        ]
        for xb in range(2):
            copies.append(remote(
                row_stat.at[place, xb], col_stat.at[my_slot, place], col_send.at[xb, 0],
                col_recv.at[my_slot, place], (inner_pb, other_inner * 2 + xb),
            ))
        return copies

    def turning_sends():
        copies = []
        for slot, end in ((0, 0), (1, last)):
            src = col_stat.at[slot, 1 + z]
            for xb in range(2):
                copies.append(remote(
                    src, row_stat.at[1 + z, x], end_send.at[slot, xb], end_recv.at[z - 1, x],
                    (pb, end * 2 + xb),
                ))
            for i, level in enumerate((other_inner, last - end)):
                copies.append(remote(
                    src, col_stat.at[slot, 1 + z], end_send.at[slot, 2 + i], col_recv.at[slot, 1 + z],
                    (pb, level * 2 + x),
                ))
        return copies

    def end_sends():
        copies = [remote(row_stat.at[x], row_stat.at[x], row_send.at[0], row_recv.at[x], x_device)]
        for xb in range(2):
            for i, level in enumerate((1, last - 1, last - z)):
                copies.append(remote(
                    row_stat.at[x, xb], col_stat.at[my_slot, x], col_send.at[xb, 1 + i],
                    col_recv.at[my_slot, x], (pb, level * 2 + xb),
                ))
        return copies

    kinds = ((turning, turning_sends), (inner_level, inner_sends), (outer_end, end_sends))
    for case, sends in kinds:
        @pl.when(case)
        def _():
            for copy in sends():
                copy.start()

    @pl.when(active)
    def _():
        for slot in range(2):
            high_part, low_part = split((col_s[slot] * (1.0 / math.sqrt(DS))).T)
            q_tr[0:DS, slot * rows:(slot + 1) * rows] = high_part
            q_tr[DS:2 * DS, slot * rows:(slot + 1) * rows] = low_part

    def landed(ref, sem):
        remote(ref, ref, row_send.at[0], sem, x_device).wait_recv()

    @pl.when(inner_level)
    def _():
        for step in range(1, 2 * groups):
            other = (place + step) % (2 * groups)
            landed(row_stat.at[other], row_recv.at[other])

    @pl.when(outer_end)
    def _():
        landed(row_stat.at[1 - x], row_recv.at[1 - x])
        for xb in range(2):
            for level in range(2):
                landed(row_stat.at[2 + level, xb], end_recv.at[level, xb])

    def combine(stats):
        t_max = functools.reduce(jnp.maximum, [stat[0:1] for stat in stats])
        s_max = functools.reduce(jnp.maximum, [stat[3:4] for stat in stats])
        t_sum = cross = s_sum = jnp.zeros((1, rows), jnp.float32)
        for stat in stats:
            t_scale = jnp.exp2(stat[0:1] - t_max)
            t_sum = t_sum + stat[1:2] * t_scale
            cross = cross + stat[2:3] * t_scale
            s_sum = s_sum + stat[4:5] * jnp.exp2(stat[3:4] - s_max)
        t_level = t_max + jnp.log2(t_sum)
        s_level = s_max + jnp.log2(s_sum)
        return t_level, s_level, LN2 * (cross / t_sum - t_level + s_level)

    @pl.when(active)
    def _():
        divergence = jnp.zeros((1, rows), jnp.float32)
        for xb in range(2):
            t_level, s_level, share = combine([row_stat[other, xb] for other in range(2 * groups)])
            wide[xb] = jnp.concatenate([t_level, s_level], axis=0)
            divergence = divergence + share
        div_in[z] = jnp.broadcast_to(divergence, (8, rows))

    def div_copy(step, slot):
        return pltpu.make_async_remote_copy(
            src_ref=div_in.at[slot], dst_ref=div_in.at[slot],
            send_sem=div_send.at[step], recv_sem=div_recv.at[step],
            device_id=line[step - 1], device_id_type=MESH,
        )

    @pl.when(outer)
    def _():
        for step in range(1, levels):
            div_copy(step, z).start()

    tiles = 2 * rows // TILE

    def row_weights(xb):
        rows_t = wide[xb, 0:1, :]
        rows_s = wide[xb, 1:2, :]

        def tile(j, carry):
            at = pl.ds(pl.multiple_of(j * TILE, TILE), TILE)
            w_row[xb, at, :] = jnp.exp2(s_sc[xb, at, :] - rows_s) - jnp.exp2(t_sc[xb, at, :] - rows_t)
            return carry

        lax.fori_loop(0, tiles, tile, 0)

    def both_weights(xb, carry):
        row_weights(xb)
        return carry

    passes = jnp.where(active, 2, 0)
    lax.fori_loop(0, passes, both_weights, 0)
    for slot in range(2):
        @pl.when(jnp.logical_and(active, z == sources[slot]))
        def _():
            for other in range(2 * groups):
                col_stat[slot, other] = row_stat[other, x]

        @pl.when(jnp.logical_and(active, z != sources[slot]))
        def _():
            for other in range(2 * groups):
                @pl.when(jnp.logical_not(jnp.logical_and(turning, other == 1 + z)))
                def _():
                    landed(col_stat.at[slot, other], col_recv.at[slot, other])

    @pl.when(active)
    def _():
        for slot in range(2):
            t_level, s_level, _ = combine([col_stat[slot, other] for other in range(2 * groups)])
            both = jnp.concatenate([t_level, s_level, jnp.zeros((6, rows), jnp.float32)], axis=0)
            col_level[slot * rows:(slot + 1) * rows, :] = both.T

    blocks = rows // LANES

    def px_copy(b):
        return pltpu.make_async_remote_copy(
            src_ref=part.at[1 - x, b], dst_ref=x_in.at[b],
            send_sem=px_send.at[b], recv_sem=px_recv.at[b],
            device_id=x_device, device_id_type=MESH,
        )

    def py_copy(step, b):
        return pltpu.make_async_remote_copy(
            src_ref=x_sum.at[b], dst_ref=y_in.at[step, b],
            send_sem=py_send.at[step, b], recv_sem=py_recv.at[step, b],
            device_id=(((y + step) % groups) * batches + seq, ka), device_id_type=MESH,
        )

    def out_copy(which, b):
        span = pl.ds(b * LANES, LANES)
        return pltpu.make_async_remote_copy(
            src_ref=out_ref.at[which, span, :], dst_ref=out_ref.at[which, span, :],
            send_sem=out_send.at[b], recv_sem=out_recv.at[b],
            device_id=(mate, ka), device_id_type=MESH,
        )

    totals = [(((1 - y) * batches + seq), ka), (mate, ka), (diagonal, ka)]

    def total_copy(i):
        return remote(total_in.at[seq], total_in.at[seq], total_send.at[i], total_recv.at[seq], totals[i])

    def turned_copy(slot, b):
        end = 0 if slot == 0 else last
        return remote(
            turned.at[slot, b], turned_in.at[z - 1, b], pz_send.at[slot, b], pz_recv.at[z - 1, b],
            (pb, end * 2 + x),
        )

    def gradient(xb):
        def tile(j, carry):
            at = pl.ds(pl.multiple_of(j * TILE, TILE), TILE)
            col = col_level[at, :]
            weight = (
                w_row[xb, at, :]
                + jnp.exp2(s_sc[xb, at, :] - col[:, 1:2])
                - jnp.exp2(t_sc[xb, at, :] - col[:, 0:1])
            )
            high_part, low_part = split(weight)
            w_high[at, :] = high_part
            w_low[at, :] = low_part
            return carry

        lax.fori_loop(0, tiles, tile, 0)
        first = nn(q_tr[...], w_high[...])
        product = first[:DS] + first[DS:] + nn(q_tr[0:DS, :], w_low[...])
        for b in range(blocks):
            part[xb, b] = product[:, b * LANES:(b + 1) * LANES]

    def turn_back(xb):
        back = nn(w_high[...], row_n[xb])
        back = back[:, :DS] + back[:, DS:] + nn(w_low[...], row_n[xb, :, 0:DS])
        for slot in range(2):
            for b in range(blocks):
                start = slot * rows + b * LANES
                piece = back[start:start + LANES]
                turned[slot, b] = jnp.where(xb == x, turned[slot, b] + piece, piece)

    def both_gradients(step, carry):
        xb = jnp.where(step == 0, 1 - x, x)
        gradient(xb)

        @pl.when(step == 0)
        def _():
            for b in range(blocks):
                px_copy(b).start()

        @pl.when(turning)
        def _():
            turn_back(xb)
        return carry

    lax.fori_loop(0, passes, both_gradients, 0)

    @pl.when(turning)
    def _():
        for b in range(blocks):
            for slot in range(2):
                turned_copy(slot, b).start()

    sends_y = jnp.logical_or(inner_level, outer)
    gets_y = jnp.logical_or(inner_level, jnp.logical_not(outer))
    for b in range(blocks):
        @pl.when(active)
        def _():
            px_copy(b).wait_recv()
            x_sum[b] = part[x, b] + x_in[b]

        @pl.when(outer_end)
        def _():
            for level in range(2):
                landed(turned_in.at[level, b], pz_recv.at[level, b])
            x_sum[b] = x_sum[b] + (turned_in[0, b] + turned_in[1, b]).T

        @pl.when(sends_y)
        def _():
            py_copy(1, b).start()

    @pl.when(outer)
    def _():
        for step in range(1, levels):
            div_copy(step, (z - step + levels) % levels).wait_recv()
        total = div_in[0, 0:1, :]
        for level in range(1, levels):
            total = total + div_in[level, 0:1, :]
        total_in[seq] = jnp.broadcast_to(total, (8, rows))
        for i in range(3):
            total_copy(i).start()

    for b in range(blocks):
        span = slice(b * LANES, (b + 1) * LANES)

        @pl.when(gets_y)
        def _():
            py_copy(1, b).wait_recv()

        @pl.when(inner_level)
        def _():
            out_ref[seq, span, :] = (x_sum[b] + y_in[1, b]).T

        @pl.when(outer_end)
        def _():
            out_ref[seq, span, :] = x_sum[b].T

        @pl.when(jnp.logical_not(active))
        def _():
            out_ref[seq, span, :] = y_in[1, b].T
        out_copy(seq, b).start()

    landed(total_in.at[1 - seq], total_recv.at[1 - seq])

    @pl.when(jnp.logical_not(outer))
    def _():
        landed(total_in.at[seq], total_recv.at[seq])
    loss_ref[0, 0] = jnp.sum(total_in[0, 0:1, :] + total_in[1, 0:1, :]) / (
        batches * HEADS * rows * 2 * levels
    )

    @pl.when(outer)
    def _():
        for i in range(3):
            total_copy(i).wait_send()

    @pl.when(active)
    def _():
        for q in range(chunks):
            @pl.when(jnp.logical_or(end_level, q // half == y))
            def _():
                for copy in piece_copies(q, True):
                    copy.wait_send()

            @pl.when(jnp.logical_and(inner_level, q // half == y))
            def _():
                for copy in piece_copies(q, False):
                    copy.wait_send()

    def sent(j, carry):
        for slot in range(2):
            for to in range(levels):
                goes = source_sends(slot, to) if 0 < to < last else forwards(slot, to)

                @pl.when(goes)
                def _():
                    for copy in z_copies(slot, j, to):
                        copy.wait_send()
        return carry

    lax.fori_loop(0, chunks, sent, 0)
    for case, sends in kinds:
        @pl.when(case)
        def _():
            for copy in sends():
                copy.wait_send()

    @pl.when(outer)
    def _():
        for step in range(1, levels):
            div_copy(step, z).wait_send()

    for b in range(blocks):
        @pl.when(active)
        def _():
            px_copy(b).wait_send()

        @pl.when(turning)
        def _():
            for slot in range(2):
                turned_copy(slot, b).wait_send()

        @pl.when(sends_y)
        def _():
            py_copy(1, b).wait_send()
        out_copy(seq, b).wait_send()
        out_copy(1 - seq, b).wait_recv()


def solution(mesh):
    def shards(teacher_q, student_q):
        batches, rows = teacher_q.shape[0], teacher_q.shape[1]
        groups = mesh.shape["pb"] // batches
        levels = mesh.shape["ka"] // 2
        chunks = rows // CHUNK
        blocks = rows // LANES
        f32, bf16 = jnp.float32, jnp.bfloat16
        dma = pltpu.SemaphoreType.DMA
        folds = groups == 2 and levels == 4
        chosen = folded_kernel if folds else kernel
        scratch = [
            pltpu.VMEM((2, rows, DT), f32),
            pltpu.VMEM((2, rows, DS), f32),
            pltpu.VMEM((2, rows, DT), f32),
            pltpu.VMEM((2, rows, DS), f32),
            pltpu.VMEM((2, 3 * DT, rows), bf16),
            pltpu.VMEM((2, 3 * DS, rows), bf16),
            pltpu.VMEM((2, 2 * rows, rows), f32),
            pltpu.VMEM((2, 2 * rows, rows), f32),
            pltpu.VMEM((2, 5, 8, rows), f32),
        ]
        if folds:
            scratch.insert(2, pltpu.VMEM((2, rows, 2 * DS), bf16))
        scratch += [
            pltpu.VMEM((4, 2, 8, rows), f32),
            pltpu.VMEM((2, 4, 8, rows), f32),
            pltpu.VMEM((2 * rows, 8), f32),
            pltpu.VMEM((levels, 8, rows), f32),
            pltpu.VMEM((2, 2, rows), f32),
            pltpu.VMEM((2 * rows, 8), f32),
            pltpu.VMEM((2, 2 * rows, rows), f32),
            pltpu.VMEM((2 * DS, 2 * rows), bf16),
            pltpu.VMEM((2 * rows, rows), bf16),
            pltpu.VMEM((2 * rows, rows), bf16),
            pltpu.VMEM((2, blocks, DS, LANES), f32),
            pltpu.VMEM((blocks, DS, LANES), f32),
            pltpu.VMEM((blocks, DS, LANES), f32),
            pltpu.VMEM((groups, blocks, DS, LANES), f32),
            pltpu.VMEM((2, blocks, LANES, DS), f32),
            pltpu.VMEM((2, blocks, LANES, DS), f32),
            pltpu.VMEM((batches, 8, rows), f32),
            dma((2,)),
            dma((2, 2)),
            dma((2, chunks, 2)),
            dma((chunks, 2)),
            dma((levels, 2, chunks, 2)),
            dma((2, chunks, 2)),
            dma((4,)),
            dma((4,)),
            dma((2, 4)),
            dma((2, 2)),
            dma((2, 4)),
            dma((2, 4)),
            dma((levels,)),
            dma((levels,)),
            dma((blocks,)),
            dma((blocks,)),
            dma((groups, blocks)),
            dma((groups, blocks)),
            dma((2, blocks)),
            dma((2, blocks)),
            dma((blocks,)),
            dma((blocks,)),
            dma((3,)),
            dma((2,)),
        ] if folds else [
            pltpu.VMEM((2 * groups, 2, 8, rows), f32),
            pltpu.VMEM((2, 2 * groups, 8, rows), f32),
            pltpu.VMEM((levels, 8, rows), f32),
            pltpu.VMEM((2, 2, rows), f32),
            pltpu.VMEM((2 * rows, 8), f32),
            pltpu.VMEM((2, 2 * rows, rows), f32),
            pltpu.VMEM((2 * DS, 2 * rows), bf16),
            pltpu.VMEM((2 * rows, rows), bf16),
            pltpu.VMEM((2 * rows, rows), bf16),
            pltpu.VMEM((2, blocks, DS, LANES), f32),
            pltpu.VMEM((blocks, DS, LANES), f32),
            pltpu.VMEM((blocks, DS, LANES), f32),
            pltpu.VMEM((groups, blocks, DS, LANES), f32),
            pltpu.VMEM((batches, 8, rows), f32),
            dma((2,)),
            dma((2, 2)),
            dma((2,)),
            dma((2,)),
            dma((levels, 2, chunks, 2)),
            dma((2, chunks, 2)),
            dma((2 * groups,)),
            dma((2 * groups,)),
            dma((2, levels)),
            dma((2, 2 * groups)),
            dma((levels,)),
            dma((levels,)),
            dma((blocks,)),
            dma((blocks,)),
            dma((groups, blocks)),
            dma((groups, blocks)),
            dma((blocks,)),
            dma((blocks,)),
            dma,
            dma,
        ]
        grad, loss = pl.pallas_call(
            functools.partial(chosen, groups, levels, rows, batches),
            out_shape=(
                jax.ShapeDtypeStruct((batches, rows, DS), f32),
                jax.ShapeDtypeStruct((1, 1), f32),
            ),
            in_specs=[pl.BlockSpec(memory_space=pl.ANY)] * 2,
            out_specs=(
                pl.BlockSpec(memory_space=pltpu.VMEM),
                pl.BlockSpec(memory_space=pltpu.SMEM),
            ),
            scratch_shapes=scratch,
            compiler_params=pltpu.CompilerParams(
                collective_id=1 if folds else 0, has_side_effects=True, vmem_limit_bytes=40 * 1024 * 1024
            ),
        )(pltpu.with_memory_space_constraint(teacher_q, pltpu.HBM), pltpu.with_memory_space_constraint(student_q, pltpu.HBM))
        return grad, loss.reshape(())

    in_specs = (P(None, "ka", None), P(None, "ka", None))
    out_specs = (P(None, "ka", None), P())
    return jax.shard_map(shards, mesh=mesh, in_specs=in_specs, out_specs=out_specs, check_vma=False)
```

```python
import functools
import math

import jax
import jax.numpy as jnp
from jax import lax
from jax.experimental import pallas as pl
from jax.experimental.pallas import tpu as pltpu
from jax.sharding import PartitionSpec as P

HEADS = 1
DT = 256
DS = 128
CHUNK = 96
LANES = 128
TILE = 64
PART = 32
WIDE = 192
STEP = 256
MESH = pl.DeviceIdType.MESH
LOG2E = 1.4426950408889634
LN2 = 0.6931471805599453


def split(values):
    high = values.astype(jnp.bfloat16)
    low = (values - high.astype(jnp.float32)).astype(jnp.bfloat16)
    return high, low


def nn(left, right):
    return jnp.dot(left, right, preferred_element_type=jnp.float32)


def kernel(
    groups, levels, rows, batches,
    t_hbm, s_hbm, out_ref, loss_ref,
    in_t, in_s, col_t, col_s, row_t, row_s, t_sc, s_sc, acc,
    stat_in, stat_col, div_in, wide, col_level, w_row, q_tr, w_high, w_low,
    part, x_in, x_sum, y_in, total_in,
    load_sem, slot_sem, x_send, x_recv, z_send, z_recv,
    stat_send, stat_recv, col_send, col_recv, div_send, div_recv,
    px_send, px_recv, py_send, py_recv, out_send, out_recv, total_send, total_recv,
):
    chunks = rows // CHUNK
    pb = lax.axis_index("pb")
    ka = lax.axis_index("ka")
    seq = pb % batches
    y = pb // batches
    z = ka // 2
    x = ka % 2
    place = x * groups + y
    low = jnp.where(seq == 0, y, groups - 1 - y)
    high = levels - 1 - low
    sources = (low, high)
    mate = y * batches + (1 - seq)
    x_device = (pb, z * 2 + (1 - x))

    planes = []
    for step in range(1, 2 * groups):
        other = (place + step) % (2 * groups)
        planes.append(((other % groups) * batches + seq, z * 2 + other // groups))
    line = [(pb, ((z + step) % levels) * 2 + x) for step in range(1, levels)]
    barrier = pltpu.get_barrier_semaphore()
    count = 2 * groups * levels
    index = place * levels + z

    def greet(step, carry):
        other = (index + step) % count
        spot, level = other // levels, other % levels
        device = ((spot % groups) * batches + seq, level * 2 + spot // groups)
        pl.semaphore_signal(barrier, inc=1, device_id=device, device_id_type=MESH)
        return carry

    lax.fori_loop(1, count, greet, 0)
    pl.semaphore_signal(barrier, inc=1, device_id=(mate, ka), device_id_type=MESH)

    loads = [
        pltpu.make_async_copy(t_hbm.at[seq], in_t.at[0], load_sem.at[0]),
        pltpu.make_async_copy(s_hbm.at[seq], in_s.at[0], load_sem.at[1]),
    ]
    for slot in range(2):
        @pl.when(z == sources[slot])
        def _():
            pltpu.make_async_copy(t_hbm.at[seq], col_t.at[slot], slot_sem.at[slot, 0]).start()
            pltpu.make_async_copy(s_hbm.at[seq], col_s.at[slot], slot_sem.at[slot, 1]).start()
    for load in loads:
        load.start()
    pl.semaphore_wait(barrier, count)

    x_copies = [
        pltpu.make_async_remote_copy(
            src_ref=src.at[seq], dst_ref=dst, send_sem=x_send.at[i], recv_sem=x_recv.at[i],
            device_id=x_device, device_id_type=MESH,
        )
        for i, (src, dst) in enumerate(((t_hbm, in_t.at[1]), (s_hbm, in_s.at[1])))
    ]

    def z_copies(slot, j, to):
        span = pl.ds(pl.multiple_of(j * CHUNK, CHUNK), CHUNK)
        return [
            pltpu.make_async_remote_copy(
                src_ref=buf.at[slot, span, :], dst_ref=buf.at[slot, span, :],
                send_sem=z_send.at[to, slot, j, i], recv_sem=z_recv.at[slot, j, i],
                device_id=(pb, to * 2 + x), device_id_type=MESH,
            )
            for i, buf in enumerate((col_t, col_s))
        ]

    for slot in range(2):
        @pl.when(z == sources[slot])
        def _():
            pltpu.make_async_copy(t_hbm.at[seq], col_t.at[slot], slot_sem.at[slot, 0]).wait()
            pltpu.make_async_copy(s_hbm.at[seq], col_s.at[slot], slot_sem.at[slot, 1]).wait()

    last = levels - 1

    def source_sends(slot, to):
        near = abs(z - to) == 1
        reach = (to != z) if 0 < to < last else near
        return jnp.logical_and(z == sources[slot], reach)

    def forwards(slot, to):
        beside = 1 if to == 0 else last - 1
        waits = jnp.logical_and(sources[slot] != z, sources[slot] != to)
        return jnp.logical_and(z == beside, waits)

    def put_rows(xb, teacher, student):
        t_high, t_low = split((teacher * (LOG2E / math.sqrt(DT))).T)
        s_high, s_low = split((student * (LOG2E / math.sqrt(DS))).T)
        for part_index, (t_part, s_part) in enumerate(
            ((t_high, s_high), (t_low, s_low), (t_high, s_high))
        ):
            row_t[xb, part_index * DT:(part_index + 1) * DT, :] = t_part
            row_s[xb, part_index * DS:(part_index + 1) * DS, :] = s_part

    def relate(xb, j):
        span = pl.ds(pl.multiple_of(j * CHUNK, CHUNK), CHUNK)
        t_high, t_low = split(col_t[:, span, :].reshape(2 * CHUNK, DT))
        s_high, s_low = split(col_s[:, span, :].reshape(2 * CHUNK, DS))
        teacher = nn(jnp.concatenate([t_high, t_high, t_low], axis=1), row_t[xb])
        student = nn(jnp.concatenate([s_high, s_high, s_low], axis=1), row_s[xb])
        tiles = []
        for slot in range(2):
            base = slot * rows + j * CHUNK
            at = pl.ds(pl.multiple_of(base, CHUNK), CHUNK)
            t_sc[xb, at, :] = teacher[slot * CHUNK:(slot + 1) * CHUNK]
            s_sc[xb, at, :] = student[slot * CHUNK:(slot + 1) * CHUNK]
            tiles += [pl.ds(pl.multiple_of(base + i * PART, PART), PART) for i in range(CHUNK // PART)]

        def read(ref, at):
            return ref[xb, at, :].reshape(PART // 8, 8, rows)

        t_old, s_old = acc[xb, 0], acc[xb, 3]
        t_max, s_max = t_old, s_old
        for at in tiles:
            t_max = jnp.maximum(t_max, jnp.max(read(t_sc, at), axis=0))
            s_max = jnp.maximum(s_max, jnp.max(read(s_sc, at), axis=0))
        t_scale = jnp.exp2(t_old - t_max)
        s_scale = jnp.exp2(s_old - s_max)
        t_sum, cross, s_sum = acc[xb, 1] * t_scale, acc[xb, 2] * t_scale, acc[xb, 4] * s_scale
        for at in tiles:
            t_tile, s_tile = read(t_sc, at), read(s_sc, at)
            t_exp = jnp.exp2(t_tile - t_max[None])
            t_sum = t_sum + jnp.sum(t_exp, axis=0)
            cross = cross + jnp.sum(t_exp * (t_tile - s_tile), axis=0)
            s_sum = s_sum + jnp.sum(jnp.exp2(s_tile - s_max[None]), axis=0)
        acc[xb, 0] = t_max
        acc[xb, 1] = t_sum
        acc[xb, 2] = cross
        acc[xb, 3] = s_max
        acc[xb, 4] = s_sum

    for xb in range(2):
        for kind in range(5):
            start = -jnp.inf if kind in (0, 3) else 0.0
            acc[xb, kind] = jnp.full((8, rows), start, jnp.float32)

    for copy in x_copies:
        copy.start()

    def first_send(j, carry):
        for slot in range(2):
            for to in range(levels):
                @pl.when(source_sends(slot, to))
                def _():
                    for copy in z_copies(slot, j, to):
                        copy.start()
        return carry

    lax.fori_loop(0, chunks, first_send, 0)
    half = chunks // 2

    def arrive(j):
        for slot in range(2):
            @pl.when(z != sources[slot])
            def _():
                for copy in z_copies(slot, j, 1):
                    copy.wait_recv()
                for to in (0, last):
                    @pl.when(forwards(slot, to))
                    def _():
                        for copy in z_copies(slot, j, to):
                            copy.start()

    def gather(k, carry):
        late = k - half
        phase = jnp.where(k < half, 1, late % 3)
        j = jnp.where(k < half, k, late // 3 + jnp.where(phase == 0, 0, half))
        own = phase == 1

        @pl.when(k == 0)
        def _():
            for load in loads:
                load.wait()

        @pl.when(k == half)
        def _():
            for copy in x_copies:
                copy.wait_recv()

        @pl.when(jnp.logical_or(k == 0, k == half))
        def _():
            which = jnp.where(k == 0, 0, 1)
            put_rows(jnp.where(k == 0, x, 1 - x), in_t[which], in_s[which])

        @pl.when(own)
        def _():
            arrive(j)

        relate(jnp.where(own, x, 1 - x), j)
        return carry

    lax.fori_loop(0, 2 * chunks, gather, 0)

    for xb in range(2):
        t_max, s_max = acc[xb, 0], acc[xb, 3]
        t_top = jnp.max(t_max, axis=0, keepdims=True)
        s_top = jnp.max(s_max, axis=0, keepdims=True)
        t_scale = jnp.exp2(t_max - t_top)
        s_scale = jnp.exp2(s_max - s_top)
        t_sum = jnp.sum(acc[xb, 1] * t_scale, axis=0, keepdims=True)
        cross = jnp.sum(acc[xb, 2] * t_scale, axis=0, keepdims=True)
        s_sum = jnp.sum(acc[xb, 4] * s_scale, axis=0, keepdims=True)
        stat_in[place, xb] = jnp.concatenate(
            [t_top, t_sum, cross, s_top, s_sum, jnp.zeros((3, rows), jnp.float32)], axis=0
        )

    def stat_copy(step):
        return pltpu.make_async_remote_copy(
            src_ref=stat_in.at[place], dst_ref=stat_in.at[place],
            send_sem=stat_send.at[step], recv_sem=stat_recv.at[step],
            device_id=planes[step - 1], device_id_type=MESH,
        )

    def stat_wait(step):
        return pltpu.make_async_remote_copy(
            src_ref=stat_in.at[(place - step + 2 * groups) % (2 * groups)],
            dst_ref=stat_in.at[(place - step + 2 * groups) % (2 * groups)],
            send_sem=stat_send.at[step], recv_sem=stat_recv.at[step],
            device_id=planes[step - 1], device_id_type=MESH,
        )

    near = jnp.minimum(z, levels - 1 - z)
    user = jnp.where(seq == 0, near, groups - 1 - near)
    my_slot = jnp.where(z == near, 0, 1)

    def col_copy(xb, step):
        return pltpu.make_async_remote_copy(
            src_ref=stat_in.at[place, xb], dst_ref=stat_col.at[my_slot, place],
            send_sem=col_send.at[xb, step], recv_sem=col_recv.at[my_slot, place],
            device_id=(user * batches + seq, ((z + step) % levels) * 2 + xb), device_id_type=MESH,
        )

    for step in range(1, levels):
        for xb in range(2):
            col_copy(xb, step).start()
    for step in range(1, 2 * groups):
        stat_copy(step).start()
    for slot in range(2):
        high_part, low_part = split((col_s[slot] * (1.0 / math.sqrt(DS))).T)
        q_tr[0:DS, slot * rows:(slot + 1) * rows] = high_part
        q_tr[DS:2 * DS, slot * rows:(slot + 1) * rows] = low_part
    for step in range(1, 2 * groups):
        stat_wait(step).wait_recv()

    def combine(stats):
        t_max = functools.reduce(jnp.maximum, [stat[0:1] for stat in stats])
        s_max = functools.reduce(jnp.maximum, [stat[3:4] for stat in stats])
        t_sum = cross = s_sum = jnp.zeros((1, rows), jnp.float32)
        for stat in stats:
            t_scale = jnp.exp2(stat[0:1] - t_max)
            t_sum = t_sum + stat[1:2] * t_scale
            cross = cross + stat[2:3] * t_scale
            s_sum = s_sum + stat[4:5] * jnp.exp2(stat[3:4] - s_max)
        t_level = t_max + jnp.log2(t_sum)
        s_level = s_max + jnp.log2(s_sum)
        return t_level, s_level, LN2 * (cross / t_sum - t_level + s_level)

    divergence = jnp.zeros((1, rows), jnp.float32)
    for xb in range(2):
        t_level, s_level, share = combine([stat_in[other, xb] for other in range(2 * groups)])
        wide[xb] = jnp.concatenate([t_level, s_level], axis=0)
        divergence = divergence + share
    div_in[z] = jnp.broadcast_to(divergence, (8, rows))

    def div_copy(step, slot):
        return pltpu.make_async_remote_copy(
            src_ref=div_in.at[slot], dst_ref=div_in.at[slot],
            send_sem=div_send.at[step], recv_sem=div_recv.at[step],
            device_id=line[step - 1], device_id_type=MESH,
        )

    for step in range(1, levels):
        div_copy(step, z).start()

    tiles = 2 * rows // TILE

    def row_weights(xb):
        rows_t = wide[xb, 0:1, :]
        rows_s = wide[xb, 1:2, :]

        def tile(j, carry):
            at = pl.ds(pl.multiple_of(j * TILE, TILE), TILE)
            w_row[xb, at, :] = jnp.exp2(s_sc[xb, at, :] - rows_s) - jnp.exp2(t_sc[xb, at, :] - rows_t)
            return carry

        lax.fori_loop(0, tiles, tile, 0)

    def both_weights(xb, carry):
        row_weights(xb)
        return carry

    lax.fori_loop(0, 2, both_weights, 0)
    for slot in range(2):
        @pl.when(z == sources[slot])
        def _():
            for other in range(2 * groups):
                stat_col[slot, other] = stat_in[other, x]

        @pl.when(z != sources[slot])
        def _():
            for other in range(2 * groups):
                pltpu.make_async_remote_copy(
                    src_ref=stat_col.at[slot, other], dst_ref=stat_col.at[slot, other],
                    send_sem=col_send.at[0, 0], recv_sem=col_recv.at[slot, other],
                    device_id=x_device, device_id_type=MESH,
                ).wait_recv()

        t_level, s_level, _ = combine([stat_col[slot, other] for other in range(2 * groups)])
        both = jnp.concatenate([t_level, s_level, jnp.zeros((6, rows), jnp.float32)], axis=0)
        col_level[slot * rows:(slot + 1) * rows, :] = both.T

    blocks = rows // LANES

    def px_copy(b):
        return pltpu.make_async_remote_copy(
            src_ref=part.at[1 - x, b], dst_ref=x_in.at[b],
            send_sem=px_send.at[b], recv_sem=px_recv.at[b],
            device_id=x_device, device_id_type=MESH,
        )

    def py_copy(step, b):
        return pltpu.make_async_remote_copy(
            src_ref=x_sum.at[b], dst_ref=y_in.at[step, b],
            send_sem=py_send.at[step, b], recv_sem=py_recv.at[step, b],
            device_id=(((y + step) % groups) * batches + seq, ka), device_id_type=MESH,
        )

    def out_copy(which, b):
        span = pl.ds(b * LANES, LANES)
        return pltpu.make_async_remote_copy(
            src_ref=out_ref.at[which, span, :], dst_ref=out_ref.at[which, span, :],
            send_sem=out_send.at[b], recv_sem=out_recv.at[b],
            device_id=(mate, ka), device_id_type=MESH,
        )

    def total_copy(which):
        return pltpu.make_async_remote_copy(
            src_ref=total_in.at[which], dst_ref=total_in.at[which],
            send_sem=total_send, recv_sem=total_recv,
            device_id=(mate, ka), device_id_type=MESH,
        )

    def gradient(xb):
        def tile(j, carry):
            at = pl.ds(pl.multiple_of(j * TILE, TILE), TILE)
            col = col_level[at, :]
            weight = (
                w_row[xb, at, :]
                + jnp.exp2(s_sc[xb, at, :] - col[:, 1:2])
                - jnp.exp2(t_sc[xb, at, :] - col[:, 0:1])
            )
            high_part, low_part = split(weight)
            w_high[at, :] = high_part
            w_low[at, :] = low_part
            return carry

        lax.fori_loop(0, tiles, tile, 0)
        first = nn(q_tr[...], w_high[...])
        product = first[:DS] + first[DS:] + nn(q_tr[0:DS, :], w_low[...])
        for b in range(blocks):
            part[xb, b] = product[:, b * LANES:(b + 1) * LANES]

    def both_gradients(step, carry):
        gradient(jnp.where(step == 0, 1 - x, x))

        @pl.when(step == 0)
        def _():
            for b in range(blocks):
                px_copy(b).start()
        return carry

    lax.fori_loop(0, 2, both_gradients, 0)
    for b in range(blocks):
        px_copy(b).wait_recv()
        x_sum[b] = part[x, b] + x_in[b]
        for step in range(1, groups):
            py_copy(step, b).start()
    for step in range(1, levels):
        div_copy(step, (z - step + levels) % levels).wait_recv()
    total = div_in[0, 0:1, :]
    for level in range(1, levels):
        total = total + div_in[level, 0:1, :]
    total_in[seq] = jnp.broadcast_to(total, (8, rows))
    total_copy(seq).start()
    for b in range(blocks):
        result = x_sum[b]
        for step in range(1, groups):
            py_copy(step, b).wait_recv()
            result = result + y_in[step, b]
        out_ref[seq, b * LANES:(b + 1) * LANES, :] = result.T
        out_copy(seq, b).start()
    total_copy(1 - seq).wait_recv()
    loss_ref[0, 0] = jnp.sum(total_in[0, 0:1, :] + total_in[1, 0:1, :]) / (
        batches * HEADS * rows * 2 * levels
    )
    total_copy(seq).wait_send()
    for copy in x_copies:
        copy.wait_send()

    def sent(j, carry):
        for slot in range(2):
            for to in range(levels):
                goes = source_sends(slot, to)
                if to in (0, last):
                    goes = jnp.logical_or(goes, forwards(slot, to))

                @pl.when(goes)
                def _():
                    for copy in z_copies(slot, j, to):
                        copy.wait_send()
        return carry

    lax.fori_loop(0, chunks, sent, 0)
    for step in range(1, 2 * groups):
        stat_copy(step).wait_send()
    for step in range(1, levels):
        div_copy(step, z).wait_send()
        for xb in range(2):
            col_copy(xb, step).wait_send()
    for b in range(blocks):
        px_copy(b).wait_send()
        for step in range(1, groups):
            py_copy(step, b).wait_send()
        out_copy(seq, b).wait_send()
        out_copy(1 - seq, b).wait_recv()


def folded_kernel(
    groups, levels, rows, batches,
    t_hbm, s_hbm, out_ref, loss_ref,
    in_t, in_s, row_n, col_t, col_s, row_t, row_s, t_sc, s_sc, acc,
    row_stat, col_stat, col_part, div_in, wide, col_level, w_row, q_tr, w_high, w_low,
    part, x_in, x_sum, y_in, turned, turned_in, total_in,
    load_sem, slot_sem, x_send, x_recv, z_send, z_recv,
    row_send, row_recv, end_send, end_recv, col_send, col_recv, div_send, div_recv,
    px_send, px_recv, py_send, py_recv, pz_send, pz_recv, out_send, out_recv, total_send, total_recv,
):
    chunks = rows // CHUNK
    pb = lax.axis_index("pb")
    ka = lax.axis_index("ka")
    seq = pb % batches
    y = pb // batches
    z = ka // 2
    x = ka % 2
    place = x * groups + y
    low = jnp.where(seq == 0, y, groups - 1 - y)
    high = levels - 1 - low
    sources = (low, high)
    outer = low == 0
    inner_level = jnp.logical_and(z > 0, z < levels - 1)
    end_level = jnp.logical_not(inner_level)
    active = jnp.logical_or(outer, inner_level)
    turning = jnp.logical_and(outer, inner_level)
    outer_end = jnp.logical_and(outer, end_level)
    y_outer = seq
    y_inner = 1 - seq
    mate = y * batches + (1 - seq)
    x_device = (pb, z * 2 + (1 - x))

    planes = []
    for step in range(1, 2 * groups):
        other = (place + step) % (2 * groups)
        planes.append(((other % groups) * batches + seq, z * 2 + other // groups))
    line = [(pb, ((z + step) % levels) * 2 + x) for step in range(1, levels)]
    barrier = pltpu.get_barrier_semaphore()
    count = 2 * groups * levels
    index = place * levels + z

    def greet(step, told):
        other = (index + step) % count
        spot, level = other // levels, other % levels
        inside = jnp.logical_and(level > 0, level < levels - 1)
        meets = jnp.logical_or(
            level == z,
            jnp.logical_or(
                jnp.logical_and(inside, inner_level), jnp.logical_and(spot % groups == y, outer)
            ),
        )

        @pl.when(meets)
        def _():
            device = ((spot % groups) * batches + seq, level * 2 + spot // groups)
            pl.semaphore_signal(barrier, inc=1, device_id=device, device_id_type=MESH)
        return told + jnp.where(meets, 1, 0)

    greeted = lax.fori_loop(1, count, greet, 0)
    diagonal = (1 - y) * batches + (1 - seq)
    for other in (mate, diagonal):
        pl.semaphore_signal(barrier, inc=1, device_id=(other, ka), device_id_type=MESH)

    loads = [
        pltpu.make_async_copy(t_hbm.at[seq], in_t.at[0], load_sem.at[0]),
        pltpu.make_async_copy(s_hbm.at[seq], in_s.at[0], load_sem.at[1]),
    ]
    for slot in range(2):
        @pl.when(z == sources[slot])
        def _():
            pltpu.make_async_copy(t_hbm.at[seq], col_t.at[slot], slot_sem.at[slot, 0]).start()
            pltpu.make_async_copy(s_hbm.at[seq], col_s.at[slot], slot_sem.at[slot, 1]).start()
    for load in loads:
        load.start()
    pl.semaphore_wait(barrier, greeted + 2)

    y_device = ((1 - y) * batches + seq, ka)

    def piece_copies(q, over_x):
        span = pl.ds(pl.multiple_of(q * CHUNK, CHUNK), CHUNK)
        return [
            pltpu.make_async_remote_copy(
                src_ref=src.at[seq, span, :] if over_x else dst.at[1, span, :], dst_ref=dst.at[1, span, :],
                send_sem=x_send.at[0 if over_x else 1, q, i], recv_sem=x_recv.at[q, i],
                device_id=x_device if over_x else y_device, device_id_type=MESH,
            )
            for i, (src, dst) in enumerate(((t_hbm, in_t), (s_hbm, in_s)))
        ]

    def z_copies(slot, j, to):
        span = pl.ds(pl.multiple_of(j * CHUNK, CHUNK), CHUNK)
        return [
            pltpu.make_async_remote_copy(
                src_ref=buf.at[slot, span, :], dst_ref=buf.at[slot, span, :],
                send_sem=z_send.at[to, slot, j, i], recv_sem=z_recv.at[slot, j, i],
                device_id=(pb, to * 2 + x), device_id_type=MESH,
            )
            for i, buf in enumerate((col_t, col_s))
        ]

    for slot in range(2):
        @pl.when(z == sources[slot])
        def _():
            pltpu.make_async_copy(t_hbm.at[seq], col_t.at[slot], slot_sem.at[slot, 0]).wait()
            pltpu.make_async_copy(s_hbm.at[seq], col_s.at[slot], slot_sem.at[slot, 1]).wait()

    last = levels - 1

    def source_sends(slot, to):
        return jnp.logical_and(z == sources[slot], to != z) if 0 < to < last else None

    def forwards(slot, to):
        beside = 1 if to == 0 else last - 1
        return jnp.logical_and(jnp.logical_and(outer, z == beside), sources[slot] != to)

    def put_rows(xb, teacher, student):
        t_high, t_low = split((teacher * (LOG2E / math.sqrt(DT))).T)
        s_high, s_low = split((student * (LOG2E / math.sqrt(DS))).T)
        row_n[xb] = jnp.concatenate(split(student * (1.0 / math.sqrt(DS))), axis=1)
        for part_index, (t_part, s_part) in enumerate(
            ((t_high, s_high), (t_low, s_low), (t_high, s_high))
        ):
            row_t[xb, part_index * DT:(part_index + 1) * DT, :] = t_part
            row_s[xb, part_index * DS:(part_index + 1) * DS, :] = s_part

    def relate(xb, j):
        span = pl.ds(pl.multiple_of(j * CHUNK, CHUNK), CHUNK)
        t_high, t_low = split(col_t[:, span, :].reshape(2 * CHUNK, DT))
        s_high, s_low = split(col_s[:, span, :].reshape(2 * CHUNK, DS))
        teacher = nn(jnp.concatenate([t_high, t_high, t_low], axis=1), row_t[xb])
        student = nn(jnp.concatenate([s_high, s_high, s_low], axis=1), row_s[xb])
        tiles = []
        for slot in range(2):
            base = slot * rows + j * CHUNK
            at = pl.ds(pl.multiple_of(base, CHUNK), CHUNK)
            t_sc[xb, at, :] = teacher[slot * CHUNK:(slot + 1) * CHUNK]
            s_sc[xb, at, :] = student[slot * CHUNK:(slot + 1) * CHUNK]
            tiles += [pl.ds(pl.multiple_of(base + i * PART, PART), PART) for i in range(CHUNK // PART)]

        def read(ref, at):
            return ref[xb, at, :].reshape(PART // 8, 8, rows)

        t_old, s_old = acc[xb, 0], acc[xb, 3]
        t_max, s_max = t_old, s_old
        for at in tiles:
            t_max = jnp.maximum(t_max, jnp.max(read(t_sc, at), axis=0))
            s_max = jnp.maximum(s_max, jnp.max(read(s_sc, at), axis=0))
        t_scale = jnp.exp2(t_old - t_max)
        s_scale = jnp.exp2(s_old - s_max)
        t_sum, cross, s_sum = acc[xb, 1] * t_scale, acc[xb, 2] * t_scale, acc[xb, 4] * s_scale
        for at in tiles:
            t_tile, s_tile = read(t_sc, at), read(s_sc, at)
            t_exp = jnp.exp2(t_tile - t_max[None])
            t_sum = t_sum + jnp.sum(t_exp, axis=0)
            cross = cross + jnp.sum(t_exp * (t_tile - s_tile), axis=0)
            s_sum = s_sum + jnp.sum(jnp.exp2(s_tile - s_max[None]), axis=0)
        acc[xb, 0] = t_max
        acc[xb, 1] = t_sum
        acc[xb, 2] = cross
        acc[xb, 3] = s_max
        acc[xb, 4] = s_sum

    def turn(j):
        for slot in range(2):
            at = pl.ds(pl.multiple_of(slot * rows + j * CHUNK, PART), CHUNK)
            t_top = jnp.max(jnp.maximum(t_sc[0, at, :], t_sc[1, at, :]), axis=1, keepdims=True)
            s_top = jnp.max(jnp.maximum(s_sc[0, at, :], s_sc[1, at, :]), axis=1, keepdims=True)
            t_all = c_all = s_all = jnp.zeros((CHUNK, rows), jnp.float32)
            for xb in range(2):
                t_exp = jnp.exp2(t_sc[xb, at, :] - t_top)
                t_all = t_all + t_exp
                c_all = c_all + t_exp * (t_sc[xb, at, :] - s_sc[xb, at, :])
                s_all = s_all + jnp.exp2(s_sc[xb, at, :] - s_top)
            sums = [jnp.sum(v, axis=1, keepdims=True) for v in (t_all, c_all, s_all)]
            col_part[at, 0:1] = t_top
            col_part[at, 1:2] = sums[0]
            col_part[at, 2:3] = sums[1]
            col_part[at, 3:4] = s_top
            col_part[at, 4:5] = sums[2]
            col_part[at, 5:8] = jnp.zeros((CHUNK, 3), jnp.float32)

    for xb in range(2):
        for kind in range(5):
            start = -jnp.inf if kind in (0, 3) else 0.0
            acc[xb, kind] = jnp.full((8, rows), start, jnp.float32)

    half = chunks // 2

    @pl.when(active)
    def _():
        for q in range(chunks):
            @pl.when(jnp.logical_or(end_level, q // half == y))
            def _():
                for copy in piece_copies(q, True):
                    copy.start()


    def first_send(j, carry):
        for slot in range(2):
            for to in range(1, last):
                @pl.when(source_sends(slot, to))
                def _():
                    for copy in z_copies(slot, j, to):
                        copy.start()
        return carry

    lax.fori_loop(0, chunks, first_send, 0)
    def arrive(j):
        for slot in range(2):
            @pl.when(z != sources[slot])
            def _():
                for copy in z_copies(slot, j, 1):
                    copy.wait_recv()
                for to in (0, last):
                    @pl.when(forwards(slot, to))
                    def _():
                        for copy in z_copies(slot, j, to):
                            copy.start()

    def gather(k, carry):
        late = k - half
        phase = jnp.where(k < half, 1, late % 3)
        j = jnp.where(k < half, k, late // 3 + jnp.where(phase == 0, 0, half))
        own = phase == 1

        @pl.when(k == half)
        def _():
            for q in range(chunks):
                @pl.when(jnp.logical_or(end_level, q // half != y))
                def _():
                    for copy in piece_copies(q, True):
                        copy.wait_recv()

        @pl.when(jnp.logical_or(k == 0, k == half))
        def _():
            which = jnp.where(k == 0, 0, 1)
            put_rows(jnp.where(k == 0, x, 1 - x), in_t[which], in_s[which])

        @pl.when(own)
        def _():
            arrive(j)

        @pl.when(jnp.logical_and(inner_level, k < half))
        def _():
            for copy in piece_copies(y * half + k, True):
                copy.wait_recv()
            for copy in piece_copies(y * half + k, False):
                copy.start()

        relate(jnp.where(own, x, 1 - x), j)

        @pl.when(jnp.logical_and(turning, jnp.logical_not(own)))
        def _():
            turn(j)
        return carry

    for load in loads:
        load.wait()
    lax.fori_loop(0, jnp.where(active, 2 * chunks, 0), gather, 0)

    mine = jnp.where(inner_level, place, x)

    @pl.when(active)
    def _():
        for xb in range(2):
            t_max, s_max = acc[xb, 0], acc[xb, 3]
            t_top = jnp.max(t_max, axis=0, keepdims=True)
            s_top = jnp.max(s_max, axis=0, keepdims=True)
            t_scale = jnp.exp2(t_max - t_top)
            s_scale = jnp.exp2(s_max - s_top)
            t_sum = jnp.sum(acc[xb, 1] * t_scale, axis=0, keepdims=True)
            cross = jnp.sum(acc[xb, 2] * t_scale, axis=0, keepdims=True)
            s_sum = jnp.sum(acc[xb, 4] * s_scale, axis=0, keepdims=True)
            row_stat[mine, xb] = jnp.concatenate(
                [t_top, t_sum, cross, s_top, s_sum, jnp.zeros((3, rows), jnp.float32)], axis=0
            )

    @pl.when(turning)
    def _():
        for slot in range(2):
            col_stat[slot, 1 + z] = col_part[slot * rows:(slot + 1) * rows, :].T

    def remote(src, dst, send, recv, device):
        return pltpu.make_async_remote_copy(
            src_ref=src, dst_ref=dst, send_sem=send, recv_sem=recv,
            device_id=device, device_id_type=MESH,
        )

    outer_pb = y_outer * batches + seq
    inner_pb = y_inner * batches + seq
    other_inner = last - z
    my_slot = jnp.where(z * 2 < levels, 0, 1)

    def inner_sends():
        copies = [
            remote(row_stat.at[place], row_stat.at[place], row_send.at[step], row_recv.at[place], planes[step - 1])
            for step in range(1, 2 * groups)
        ]
        for xb in range(2):
            copies.append(remote(
                row_stat.at[place, xb], col_stat.at[my_slot, place], col_send.at[xb, 0],
                col_recv.at[my_slot, place], (inner_pb, other_inner * 2 + xb),
            ))
        return copies

    def turning_sends():
        copies = []
        for slot, end in ((0, 0), (1, last)):
            src = col_stat.at[slot, 1 + z]
            for xb in range(2):
                copies.append(remote(
                    src, row_stat.at[1 + z, x], end_send.at[slot, xb], end_recv.at[z - 1, x],
                    (pb, end * 2 + xb),
                ))
            for i, level in enumerate((other_inner, last - end)):
                copies.append(remote(
                    src, col_stat.at[slot, 1 + z], end_send.at[slot, 2 + i], col_recv.at[slot, 1 + z],
                    (pb, level * 2 + x),
                ))
        return copies

    def end_sends():
        copies = [remote(row_stat.at[x], row_stat.at[x], row_send.at[0], row_recv.at[x], x_device)]
        for xb in range(2):
            for i, level in enumerate((1, last - 1, last - z)):
                copies.append(remote(
                    row_stat.at[x, xb], col_stat.at[my_slot, x], col_send.at[xb, 1 + i],
                    col_recv.at[my_slot, x], (pb, level * 2 + xb),
                ))
        return copies

    kinds = ((turning, turning_sends), (inner_level, inner_sends), (outer_end, end_sends))
    for case, sends in kinds:
        @pl.when(case)
        def _():
            for copy in sends():
                copy.start()

    @pl.when(active)
    def _():
        for slot in range(2):
            high_part, low_part = split((col_s[slot] * (1.0 / math.sqrt(DS))).T)
            q_tr[0:DS, slot * rows:(slot + 1) * rows] = high_part
            q_tr[DS:2 * DS, slot * rows:(slot + 1) * rows] = low_part

    def landed(ref, sem):
        remote(ref, ref, row_send.at[0], sem, x_device).wait_recv()

    @pl.when(inner_level)
    def _():
        for step in range(1, 2 * groups):
            other = (place + step) % (2 * groups)
            landed(row_stat.at[other], row_recv.at[other])

    @pl.when(outer_end)
    def _():
        landed(row_stat.at[1 - x], row_recv.at[1 - x])
        for xb in range(2):
            for level in range(2):
                landed(row_stat.at[2 + level, xb], end_recv.at[level, xb])

    def combine(stats):
        t_max = functools.reduce(jnp.maximum, [stat[0:1] for stat in stats])
        s_max = functools.reduce(jnp.maximum, [stat[3:4] for stat in stats])
        t_sum = cross = s_sum = jnp.zeros((1, rows), jnp.float32)
        for stat in stats:
            t_scale = jnp.exp2(stat[0:1] - t_max)
            t_sum = t_sum + stat[1:2] * t_scale
            cross = cross + stat[2:3] * t_scale
            s_sum = s_sum + stat[4:5] * jnp.exp2(stat[3:4] - s_max)
        t_level = t_max + jnp.log2(t_sum)
        s_level = s_max + jnp.log2(s_sum)
        return t_level, s_level, LN2 * (cross / t_sum - t_level + s_level)

    @pl.when(active)
    def _():
        divergence = jnp.zeros((1, rows), jnp.float32)
        for xb in range(2):
            t_level, s_level, share = combine([row_stat[other, xb] for other in range(2 * groups)])
            wide[xb] = jnp.concatenate([t_level, s_level], axis=0)
            divergence = divergence + share
        div_in[z] = jnp.broadcast_to(divergence, (8, rows))

    def div_copy(step, slot):
        return pltpu.make_async_remote_copy(
            src_ref=div_in.at[slot], dst_ref=div_in.at[slot],
            send_sem=div_send.at[step], recv_sem=div_recv.at[step],
            device_id=line[step - 1], device_id_type=MESH,
        )

    @pl.when(outer)
    def _():
        for step in range(1, levels):
            div_copy(step, z).start()

    tiles = 2 * rows // WIDE

    def row_weights(xb):
        rows_t = wide[xb, 0:1, :]
        rows_s = wide[xb, 1:2, :]

        def tile(j, carry):
            at = pl.ds(pl.multiple_of(j * WIDE, WIDE), WIDE)
            w_row[xb, at, :] = jnp.exp2(s_sc[xb, at, :] - rows_s) - jnp.exp2(t_sc[xb, at, :] - rows_t)
            return carry

        lax.fori_loop(0, tiles, tile, 0)

    def both_weights(xb, carry):
        row_weights(xb)
        return carry

    passes = jnp.where(active, 2, 0)
    lax.fori_loop(0, passes, both_weights, 0)
    for slot in range(2):
        @pl.when(jnp.logical_and(active, z == sources[slot]))
        def _():
            for other in range(2 * groups):
                col_stat[slot, other] = row_stat[other, x]

        @pl.when(jnp.logical_and(active, z != sources[slot]))
        def _():
            for other in range(2 * groups):
                @pl.when(jnp.logical_not(jnp.logical_and(turning, other == 1 + z)))
                def _():
                    landed(col_stat.at[slot, other], col_recv.at[slot, other])

    @pl.when(active)
    def _():
        for slot in range(2):
            t_level, s_level, _ = combine([col_stat[slot, other] for other in range(2 * groups)])
            both = jnp.concatenate([t_level, s_level, jnp.zeros((6, rows), jnp.float32)], axis=0)
            col_level[slot * rows:(slot + 1) * rows, :] = both.T

    blocks = rows // LANES

    def px_copy(b):
        return pltpu.make_async_remote_copy(
            src_ref=part.at[1 - x, b], dst_ref=x_in.at[b],
            send_sem=px_send.at[b], recv_sem=px_recv.at[b],
            device_id=x_device, device_id_type=MESH,
        )

    def py_copy(step, b):
        return pltpu.make_async_remote_copy(
            src_ref=x_sum.at[b], dst_ref=y_in.at[step, b],
            send_sem=py_send.at[step, b], recv_sem=py_recv.at[step, b],
            device_id=(((y + step) % groups) * batches + seq, ka), device_id_type=MESH,
        )

    def out_copy(which, b):
        span = pl.ds(b * LANES, LANES)
        return pltpu.make_async_remote_copy(
            src_ref=out_ref.at[which, span, :], dst_ref=out_ref.at[which, span, :],
            send_sem=out_send.at[b], recv_sem=out_recv.at[b],
            device_id=(mate, ka), device_id_type=MESH,
        )

    totals = [(((1 - y) * batches + seq), ka), (mate, ka), (diagonal, ka)]

    def total_copy(i):
        return remote(total_in.at[seq], total_in.at[seq], total_send.at[i], total_recv.at[seq], totals[i])

    def turned_copy(slot, b):
        end = 0 if slot == 0 else last
        return remote(
            turned.at[slot, b], turned_in.at[z - 1, b], pz_send.at[slot, b], pz_recv.at[z - 1, b],
            (pb, end * 2 + x),
        )

    def gradient(xb):
        product = jnp.zeros((DS, rows), jnp.float32)
        for start in range(0, 2 * rows, STEP):
            at = slice(start, start + STEP)
            col = col_level[at, :]
            weight = (
                w_row[xb, at, :]
                + jnp.exp2(s_sc[xb, at, :] - col[:, 1:2])
                - jnp.exp2(t_sc[xb, at, :] - col[:, 0:1])
            )
            high_part, low_part = split(weight)
            w_high[at, :] = high_part
            w_low[at, :] = low_part
            first = nn(q_tr[:, at], high_part)
            product = product + (first[:DS] + first[DS:] + nn(q_tr[0:DS, at], low_part))
        for b in range(blocks):
            part[xb, b] = product[:, b * LANES:(b + 1) * LANES]

    def turn_back(xb):
        back = nn(w_high[...], row_n[xb])
        back = back[:, :DS] + back[:, DS:] + nn(w_low[...], row_n[xb, :, 0:DS])
        for slot in range(2):
            for b in range(blocks):
                start = slot * rows + b * LANES
                piece = back[start:start + LANES]
                turned[slot, b] = jnp.where(xb == x, turned[slot, b] + piece, piece)

    def both_gradients(step, carry):
        xb = jnp.where(step == 0, 1 - x, x)
        gradient(xb)

        @pl.when(step == 0)
        def _():
            for b in range(blocks):
                px_copy(b).start()

        @pl.when(turning)
        def _():
            turn_back(xb)
        return carry

    lax.fori_loop(0, passes, both_gradients, 0)

    @pl.when(turning)
    def _():
        for b in range(blocks):
            for slot in range(2):
                turned_copy(slot, b).start()

    sends_y = jnp.logical_or(inner_level, outer)
    gets_y = jnp.logical_or(inner_level, jnp.logical_not(outer))
    for b in range(blocks):
        @pl.when(active)
        def _():
            px_copy(b).wait_recv()
            x_sum[b] = part[x, b] + x_in[b]

        @pl.when(outer_end)
        def _():
            for level in range(2):
                landed(turned_in.at[level, b], pz_recv.at[level, b])
            x_sum[b] = x_sum[b] + (turned_in[0, b] + turned_in[1, b]).T

        @pl.when(sends_y)
        def _():
            py_copy(1, b).start()

    @pl.when(outer)
    def _():
        for step in range(1, levels):
            div_copy(step, (z - step + levels) % levels).wait_recv()
        total = div_in[0, 0:1, :]
        for level in range(1, levels):
            total = total + div_in[level, 0:1, :]
        total_in[seq] = jnp.broadcast_to(total, (8, rows))
        for i in range(3):
            total_copy(i).start()

    for b in range(blocks):
        span = slice(b * LANES, (b + 1) * LANES)

        @pl.when(gets_y)
        def _():
            py_copy(1, b).wait_recv()

        @pl.when(inner_level)
        def _():
            out_ref[seq, span, :] = (x_sum[b] + y_in[1, b]).T

        @pl.when(outer_end)
        def _():
            out_ref[seq, span, :] = x_sum[b].T

        @pl.when(jnp.logical_not(active))
        def _():
            out_ref[seq, span, :] = y_in[1, b].T
        out_copy(seq, b).start()

    landed(total_in.at[1 - seq], total_recv.at[1 - seq])

    @pl.when(jnp.logical_not(outer))
    def _():
        landed(total_in.at[seq], total_recv.at[seq])
    loss_ref[0, 0] = jnp.sum(total_in[0, 0:1, :] + total_in[1, 0:1, :]) / (
        batches * HEADS * rows * 2 * levels
    )

    @pl.when(outer)
    def _():
        for i in range(3):
            total_copy(i).wait_send()

    @pl.when(active)
    def _():
        for q in range(chunks):
            @pl.when(jnp.logical_or(end_level, q // half == y))
            def _():
                for copy in piece_copies(q, True):
                    copy.wait_send()

            @pl.when(jnp.logical_and(inner_level, q // half == y))
            def _():
                for copy in piece_copies(q, False):
                    copy.wait_send()

    def sent(j, carry):
        for slot in range(2):
            for to in range(levels):
                goes = source_sends(slot, to) if 0 < to < last else forwards(slot, to)

                @pl.when(goes)
                def _():
                    for copy in z_copies(slot, j, to):
                        copy.wait_send()
        return carry

    lax.fori_loop(0, chunks, sent, 0)
    for case, sends in kinds:
        @pl.when(case)
        def _():
            for copy in sends():
                copy.wait_send()

    @pl.when(outer)
    def _():
        for step in range(1, levels):
            div_copy(step, z).wait_send()

    for b in range(blocks):
        @pl.when(active)
        def _():
            px_copy(b).wait_send()

        @pl.when(turning)
        def _():
            for slot in range(2):
                turned_copy(slot, b).wait_send()

        @pl.when(sends_y)
        def _():
            py_copy(1, b).wait_send()
        out_copy(seq, b).wait_send()
        out_copy(1 - seq, b).wait_recv()


def solution(mesh):
    def shards(teacher_q, student_q):
        batches, rows = teacher_q.shape[0], teacher_q.shape[1]
        groups = mesh.shape["pb"] // batches
        levels = mesh.shape["ka"] // 2
        chunks = rows // CHUNK
        blocks = rows // LANES
        f32, bf16 = jnp.float32, jnp.bfloat16
        dma = pltpu.SemaphoreType.DMA
        folds = groups == 2 and levels == 4
        chosen = folded_kernel if folds else kernel
        scratch = [
            pltpu.VMEM((2, rows, DT), f32),
            pltpu.VMEM((2, rows, DS), f32),
            pltpu.VMEM((2, rows, DT), f32),
            pltpu.VMEM((2, rows, DS), f32),
            pltpu.VMEM((2, 3 * DT, rows), bf16),
            pltpu.VMEM((2, 3 * DS, rows), bf16),
            pltpu.VMEM((2, 2 * rows, rows), f32),
            pltpu.VMEM((2, 2 * rows, rows), f32),
            pltpu.VMEM((2, 5, 8, rows), f32),
        ]
        if folds:
            scratch.insert(2, pltpu.VMEM((2, rows, 2 * DS), bf16))
        scratch += [
            pltpu.VMEM((4, 2, 8, rows), f32),
            pltpu.VMEM((2, 4, 8, rows), f32),
            pltpu.VMEM((2 * rows, 8), f32),
            pltpu.VMEM((levels, 8, rows), f32),
            pltpu.VMEM((2, 2, rows), f32),
            pltpu.VMEM((2 * rows, 8), f32),
            pltpu.VMEM((2, 2 * rows, rows), f32),
            pltpu.VMEM((2 * DS, 2 * rows), bf16),
            pltpu.VMEM((2 * rows, rows), bf16),
            pltpu.VMEM((2 * rows, rows), bf16),
            pltpu.VMEM((2, blocks, DS, LANES), f32),
            pltpu.VMEM((blocks, DS, LANES), f32),
            pltpu.VMEM((blocks, DS, LANES), f32),
            pltpu.VMEM((groups, blocks, DS, LANES), f32),
            pltpu.VMEM((2, blocks, LANES, DS), f32),
            pltpu.VMEM((2, blocks, LANES, DS), f32),
            pltpu.VMEM((batches, 8, rows), f32),
            dma((2,)),
            dma((2, 2)),
            dma((2, chunks, 2)),
            dma((chunks, 2)),
            dma((levels, 2, chunks, 2)),
            dma((2, chunks, 2)),
            dma((4,)),
            dma((4,)),
            dma((2, 4)),
            dma((2, 2)),
            dma((2, 4)),
            dma((2, 4)),
            dma((levels,)),
            dma((levels,)),
            dma((blocks,)),
            dma((blocks,)),
            dma((groups, blocks)),
            dma((groups, blocks)),
            dma((2, blocks)),
            dma((2, blocks)),
            dma((blocks,)),
            dma((blocks,)),
            dma((3,)),
            dma((2,)),
        ] if folds else [
            pltpu.VMEM((2 * groups, 2, 8, rows), f32),
            pltpu.VMEM((2, 2 * groups, 8, rows), f32),
            pltpu.VMEM((levels, 8, rows), f32),
            pltpu.VMEM((2, 2, rows), f32),
            pltpu.VMEM((2 * rows, 8), f32),
            pltpu.VMEM((2, 2 * rows, rows), f32),
            pltpu.VMEM((2 * DS, 2 * rows), bf16),
            pltpu.VMEM((2 * rows, rows), bf16),
            pltpu.VMEM((2 * rows, rows), bf16),
            pltpu.VMEM((2, blocks, DS, LANES), f32),
            pltpu.VMEM((blocks, DS, LANES), f32),
            pltpu.VMEM((blocks, DS, LANES), f32),
            pltpu.VMEM((groups, blocks, DS, LANES), f32),
            pltpu.VMEM((batches, 8, rows), f32),
            dma((2,)),
            dma((2, 2)),
            dma((2,)),
            dma((2,)),
            dma((levels, 2, chunks, 2)),
            dma((2, chunks, 2)),
            dma((2 * groups,)),
            dma((2 * groups,)),
            dma((2, levels)),
            dma((2, 2 * groups)),
            dma((levels,)),
            dma((levels,)),
            dma((blocks,)),
            dma((blocks,)),
            dma((groups, blocks)),
            dma((groups, blocks)),
            dma((blocks,)),
            dma((blocks,)),
            dma,
            dma,
        ]
        grad, loss = pl.pallas_call(
            functools.partial(chosen, groups, levels, rows, batches),
            out_shape=(
                jax.ShapeDtypeStruct((batches, rows, DS), f32),
                jax.ShapeDtypeStruct((1, 1), f32),
            ),
            in_specs=[pl.BlockSpec(memory_space=pl.ANY)] * 2,
            out_specs=(
                pl.BlockSpec(memory_space=pltpu.VMEM),
                pl.BlockSpec(memory_space=pltpu.SMEM),
            ),
            scratch_shapes=scratch,
            compiler_params=pltpu.CompilerParams(
                collective_id=1 if folds else 0, has_side_effects=True, vmem_limit_bytes=40 * 1024 * 1024
            ),
        )(pltpu.with_memory_space_constraint(teacher_q, pltpu.HBM), pltpu.with_memory_space_constraint(student_q, pltpu.HBM))
        return grad, loss.reshape(())

    in_specs = (P(None, "ka", None), P(None, "ka", None))
    out_specs = (P(None, "ka", None), P())
    return jax.shard_map(shards, mesh=mesh, in_specs=in_specs, out_specs=out_specs, check_vma=False)
```

```python
import functools
import math

import jax
import jax.numpy as jnp
from jax import lax
from jax.experimental import pallas as pl
from jax.experimental.pallas import tpu as pltpu
from jax.sharding import PartitionSpec as P

HEADS = 1
DT = 256
DS = 128
CHUNK = 96
LANES = 128
TILE = 64
PART = 32
WIDE = 192
STEP = 256
MESH = pl.DeviceIdType.MESH
LOG2E = 1.4426950408889634
LN2 = 0.6931471805599453


def split(values):
    high = values.astype(jnp.bfloat16)
    low = (values - high.astype(jnp.float32)).astype(jnp.bfloat16)
    return high, low


def nn(left, right):
    return jnp.dot(left, right, preferred_element_type=jnp.float32)


def kernel(
    groups, levels, rows, batches,
    t_hbm, s_hbm, out_ref, loss_ref,
    in_t, in_s, col_t, col_s, row_t, row_s, t_sc, s_sc, acc,
    stat_in, stat_col, div_in, wide, col_level, w_row, q_tr, w_high, w_low,
    part, x_in, x_sum, y_in, total_in,
    load_sem, slot_sem, x_send, x_recv, z_send, z_recv,
    stat_send, stat_recv, col_send, col_recv, div_send, div_recv,
    px_send, px_recv, py_send, py_recv, out_send, out_recv, total_send, total_recv,
):
    chunks = rows // CHUNK
    pb = lax.axis_index("pb")
    ka = lax.axis_index("ka")
    seq = pb % batches
    y = pb // batches
    z = ka // 2
    x = ka % 2
    place = x * groups + y
    low = jnp.where(seq == 0, y, groups - 1 - y)
    high = levels - 1 - low
    sources = (low, high)
    mate = y * batches + (1 - seq)
    x_device = (pb, z * 2 + (1 - x))

    planes = []
    for step in range(1, 2 * groups):
        other = (place + step) % (2 * groups)
        planes.append(((other % groups) * batches + seq, z * 2 + other // groups))
    line = [(pb, ((z + step) % levels) * 2 + x) for step in range(1, levels)]
    barrier = pltpu.get_barrier_semaphore()
    count = 2 * groups * levels
    index = place * levels + z

    def greet(step, carry):
        other = (index + step) % count
        spot, level = other // levels, other % levels
        device = ((spot % groups) * batches + seq, level * 2 + spot // groups)
        pl.semaphore_signal(barrier, inc=1, device_id=device, device_id_type=MESH)
        return carry

    lax.fori_loop(1, count, greet, 0)
    pl.semaphore_signal(barrier, inc=1, device_id=(mate, ka), device_id_type=MESH)

    loads = [
        pltpu.make_async_copy(t_hbm.at[seq], in_t.at[0], load_sem.at[0]),
        pltpu.make_async_copy(s_hbm.at[seq], in_s.at[0], load_sem.at[1]),
    ]
    for slot in range(2):
        @pl.when(z == sources[slot])
        def _():
            pltpu.make_async_copy(t_hbm.at[seq], col_t.at[slot], slot_sem.at[slot, 0]).start()
            pltpu.make_async_copy(s_hbm.at[seq], col_s.at[slot], slot_sem.at[slot, 1]).start()
    for load in loads:
        load.start()
    pl.semaphore_wait(barrier, count)

    x_copies = [
        pltpu.make_async_remote_copy(
            src_ref=src.at[seq], dst_ref=dst, send_sem=x_send.at[i], recv_sem=x_recv.at[i],
            device_id=x_device, device_id_type=MESH,
        )
        for i, (src, dst) in enumerate(((t_hbm, in_t.at[1]), (s_hbm, in_s.at[1])))
    ]

    def z_copies(slot, j, to):
        span = pl.ds(pl.multiple_of(j * CHUNK, CHUNK), CHUNK)
        return [
            pltpu.make_async_remote_copy(
                src_ref=buf.at[slot, span, :], dst_ref=buf.at[slot, span, :],
                send_sem=z_send.at[to, slot, j, i], recv_sem=z_recv.at[slot, j, i],
                device_id=(pb, to * 2 + x), device_id_type=MESH,
            )
            for i, buf in enumerate((col_t, col_s))
        ]

    for slot in range(2):
        @pl.when(z == sources[slot])
        def _():
            pltpu.make_async_copy(t_hbm.at[seq], col_t.at[slot], slot_sem.at[slot, 0]).wait()
            pltpu.make_async_copy(s_hbm.at[seq], col_s.at[slot], slot_sem.at[slot, 1]).wait()

    last = levels - 1

    def source_sends(slot, to):
        near = abs(z - to) == 1
        reach = (to != z) if 0 < to < last else near
        return jnp.logical_and(z == sources[slot], reach)

    def forwards(slot, to):
        beside = 1 if to == 0 else last - 1
        waits = jnp.logical_and(sources[slot] != z, sources[slot] != to)
        return jnp.logical_and(z == beside, waits)

    def put_rows(xb, teacher, student):
        t_high, t_low = split((teacher * (LOG2E / math.sqrt(DT))).T)
        s_high, s_low = split((student * (LOG2E / math.sqrt(DS))).T)
        for part_index, (t_part, s_part) in enumerate(
            ((t_high, s_high), (t_low, s_low), (t_high, s_high))
        ):
            row_t[xb, part_index * DT:(part_index + 1) * DT, :] = t_part
            row_s[xb, part_index * DS:(part_index + 1) * DS, :] = s_part

    def relate(xb, j):
        span = pl.ds(pl.multiple_of(j * CHUNK, CHUNK), CHUNK)
        t_high, t_low = split(col_t[:, span, :].reshape(2 * CHUNK, DT))
        s_high, s_low = split(col_s[:, span, :].reshape(2 * CHUNK, DS))
        teacher = nn(jnp.concatenate([t_high, t_high, t_low], axis=1), row_t[xb])
        student = nn(jnp.concatenate([s_high, s_high, s_low], axis=1), row_s[xb])
        tiles = []
        for slot in range(2):
            base = slot * rows + j * CHUNK
            at = pl.ds(pl.multiple_of(base, CHUNK), CHUNK)
            t_sc[xb, at, :] = teacher[slot * CHUNK:(slot + 1) * CHUNK]
            s_sc[xb, at, :] = student[slot * CHUNK:(slot + 1) * CHUNK]
            tiles += [pl.ds(pl.multiple_of(base + i * PART, PART), PART) for i in range(CHUNK // PART)]

        def read(ref, at):
            return ref[xb, at, :].reshape(PART // 8, 8, rows)

        t_old, s_old = acc[xb, 0], acc[xb, 3]
        t_max, s_max = t_old, s_old
        for at in tiles:
            t_max = jnp.maximum(t_max, jnp.max(read(t_sc, at), axis=0))
            s_max = jnp.maximum(s_max, jnp.max(read(s_sc, at), axis=0))
        t_scale = jnp.exp2(t_old - t_max)
        s_scale = jnp.exp2(s_old - s_max)
        t_sum, cross, s_sum = acc[xb, 1] * t_scale, acc[xb, 2] * t_scale, acc[xb, 4] * s_scale
        for at in tiles:
            t_tile, s_tile = read(t_sc, at), read(s_sc, at)
            t_exp = jnp.exp2(t_tile - t_max[None])
            t_sum = t_sum + jnp.sum(t_exp, axis=0)
            cross = cross + jnp.sum(t_exp * (t_tile - s_tile), axis=0)
            s_sum = s_sum + jnp.sum(jnp.exp2(s_tile - s_max[None]), axis=0)
        acc[xb, 0] = t_max
        acc[xb, 1] = t_sum
        acc[xb, 2] = cross
        acc[xb, 3] = s_max
        acc[xb, 4] = s_sum

    for xb in range(2):
        for kind in range(5):
            start = -jnp.inf if kind in (0, 3) else 0.0
            acc[xb, kind] = jnp.full((8, rows), start, jnp.float32)

    for copy in x_copies:
        copy.start()

    def first_send(j, carry):
        for slot in range(2):
            for to in range(levels):
                @pl.when(source_sends(slot, to))
                def _():
                    for copy in z_copies(slot, j, to):
                        copy.start()
        return carry

    lax.fori_loop(0, chunks, first_send, 0)
    half = chunks // 2

    def arrive(j):
        for slot in range(2):
            @pl.when(z != sources[slot])
            def _():
                for copy in z_copies(slot, j, 1):
                    copy.wait_recv()
                for to in (0, last):
                    @pl.when(forwards(slot, to))
                    def _():
                        for copy in z_copies(slot, j, to):
                            copy.start()

    def gather(k, carry):
        late = k - half
        phase = jnp.where(k < half, 1, late % 3)
        j = jnp.where(k < half, k, late // 3 + jnp.where(phase == 0, 0, half))
        own = phase == 1

        @pl.when(k == 0)
        def _():
            for load in loads:
                load.wait()

        @pl.when(k == half)
        def _():
            for copy in x_copies:
                copy.wait_recv()

        @pl.when(jnp.logical_or(k == 0, k == half))
        def _():
            which = jnp.where(k == 0, 0, 1)
            put_rows(jnp.where(k == 0, x, 1 - x), in_t[which], in_s[which])

        @pl.when(own)
        def _():
            arrive(j)

        relate(jnp.where(own, x, 1 - x), j)
        return carry

    lax.fori_loop(0, 2 * chunks, gather, 0)

    for xb in range(2):
        t_max, s_max = acc[xb, 0], acc[xb, 3]
        t_top = jnp.max(t_max, axis=0, keepdims=True)
        s_top = jnp.max(s_max, axis=0, keepdims=True)
        t_scale = jnp.exp2(t_max - t_top)
        s_scale = jnp.exp2(s_max - s_top)
        t_sum = jnp.sum(acc[xb, 1] * t_scale, axis=0, keepdims=True)
        cross = jnp.sum(acc[xb, 2] * t_scale, axis=0, keepdims=True)
        s_sum = jnp.sum(acc[xb, 4] * s_scale, axis=0, keepdims=True)
        stat_in[place, xb] = jnp.concatenate(
            [t_top, t_sum, cross, s_top, s_sum, jnp.zeros((3, rows), jnp.float32)], axis=0
        )

    def stat_copy(step):
        return pltpu.make_async_remote_copy(
            src_ref=stat_in.at[place], dst_ref=stat_in.at[place],
            send_sem=stat_send.at[step], recv_sem=stat_recv.at[step],
            device_id=planes[step - 1], device_id_type=MESH,
        )

    def stat_wait(step):
        return pltpu.make_async_remote_copy(
            src_ref=stat_in.at[(place - step + 2 * groups) % (2 * groups)],
            dst_ref=stat_in.at[(place - step + 2 * groups) % (2 * groups)],
            send_sem=stat_send.at[step], recv_sem=stat_recv.at[step],
            device_id=planes[step - 1], device_id_type=MESH,
        )

    near = jnp.minimum(z, levels - 1 - z)
    user = jnp.where(seq == 0, near, groups - 1 - near)
    my_slot = jnp.where(z == near, 0, 1)

    def col_copy(xb, step):
        return pltpu.make_async_remote_copy(
            src_ref=stat_in.at[place, xb], dst_ref=stat_col.at[my_slot, place],
            send_sem=col_send.at[xb, step], recv_sem=col_recv.at[my_slot, place],
            device_id=(user * batches + seq, ((z + step) % levels) * 2 + xb), device_id_type=MESH,
        )

    for step in range(1, levels):
        for xb in range(2):
            col_copy(xb, step).start()
    for step in range(1, 2 * groups):
        stat_copy(step).start()
    for slot in range(2):
        high_part, low_part = split((col_s[slot] * (1.0 / math.sqrt(DS))).T)
        q_tr[0:DS, slot * rows:(slot + 1) * rows] = high_part
        q_tr[DS:2 * DS, slot * rows:(slot + 1) * rows] = low_part
    for step in range(1, 2 * groups):
        stat_wait(step).wait_recv()

    def combine(stats):
        t_max = functools.reduce(jnp.maximum, [stat[0:1] for stat in stats])
        s_max = functools.reduce(jnp.maximum, [stat[3:4] for stat in stats])
        t_sum = cross = s_sum = jnp.zeros((1, rows), jnp.float32)
        for stat in stats:
            t_scale = jnp.exp2(stat[0:1] - t_max)
            t_sum = t_sum + stat[1:2] * t_scale
            cross = cross + stat[2:3] * t_scale
            s_sum = s_sum + stat[4:5] * jnp.exp2(stat[3:4] - s_max)
        t_level = t_max + jnp.log2(t_sum)
        s_level = s_max + jnp.log2(s_sum)
        return t_level, s_level, LN2 * (cross / t_sum - t_level + s_level)

    divergence = jnp.zeros((1, rows), jnp.float32)
    for xb in range(2):
        t_level, s_level, share = combine([stat_in[other, xb] for other in range(2 * groups)])
        wide[xb] = jnp.concatenate([t_level, s_level], axis=0)
        divergence = divergence + share
    div_in[z] = jnp.broadcast_to(divergence, (8, rows))

    def div_copy(step, slot):
        return pltpu.make_async_remote_copy(
            src_ref=div_in.at[slot], dst_ref=div_in.at[slot],
            send_sem=div_send.at[step], recv_sem=div_recv.at[step],
            device_id=line[step - 1], device_id_type=MESH,
        )

    for step in range(1, levels):
        div_copy(step, z).start()

    tiles = 2 * rows // TILE

    def row_weights(xb):
        rows_t = wide[xb, 0:1, :]
        rows_s = wide[xb, 1:2, :]

        def tile(j, carry):
            at = pl.ds(pl.multiple_of(j * TILE, TILE), TILE)
            w_row[xb, at, :] = jnp.exp2(s_sc[xb, at, :] - rows_s) - jnp.exp2(t_sc[xb, at, :] - rows_t)
            return carry

        lax.fori_loop(0, tiles, tile, 0)

    def both_weights(xb, carry):
        row_weights(xb)
        return carry

    lax.fori_loop(0, 2, both_weights, 0)
    for slot in range(2):
        @pl.when(z == sources[slot])
        def _():
            for other in range(2 * groups):
                stat_col[slot, other] = stat_in[other, x]

        @pl.when(z != sources[slot])
        def _():
            for other in range(2 * groups):
                pltpu.make_async_remote_copy(
                    src_ref=stat_col.at[slot, other], dst_ref=stat_col.at[slot, other],
                    send_sem=col_send.at[0, 0], recv_sem=col_recv.at[slot, other],
                    device_id=x_device, device_id_type=MESH,
                ).wait_recv()

        t_level, s_level, _ = combine([stat_col[slot, other] for other in range(2 * groups)])
        both = jnp.concatenate([t_level, s_level, jnp.zeros((6, rows), jnp.float32)], axis=0)
        col_level[slot * rows:(slot + 1) * rows, :] = both.T

    blocks = rows // LANES

    def px_copy(b):
        return pltpu.make_async_remote_copy(
            src_ref=part.at[1 - x, b], dst_ref=x_in.at[b],
            send_sem=px_send.at[b], recv_sem=px_recv.at[b],
            device_id=x_device, device_id_type=MESH,
        )

    def py_copy(step, b):
        return pltpu.make_async_remote_copy(
            src_ref=x_sum.at[b], dst_ref=y_in.at[step, b],
            send_sem=py_send.at[step, b], recv_sem=py_recv.at[step, b],
            device_id=(((y + step) % groups) * batches + seq, ka), device_id_type=MESH,
        )

    def out_copy(which, b):
        span = pl.ds(b * LANES, LANES)
        return pltpu.make_async_remote_copy(
            src_ref=out_ref.at[which, span, :], dst_ref=out_ref.at[which, span, :],
            send_sem=out_send.at[b], recv_sem=out_recv.at[b],
            device_id=(mate, ka), device_id_type=MESH,
        )

    def total_copy(which):
        return pltpu.make_async_remote_copy(
            src_ref=total_in.at[which], dst_ref=total_in.at[which],
            send_sem=total_send, recv_sem=total_recv,
            device_id=(mate, ka), device_id_type=MESH,
        )

    def gradient(xb):
        def tile(j, carry):
            at = pl.ds(pl.multiple_of(j * TILE, TILE), TILE)
            col = col_level[at, :]
            weight = (
                w_row[xb, at, :]
                + jnp.exp2(s_sc[xb, at, :] - col[:, 1:2])
                - jnp.exp2(t_sc[xb, at, :] - col[:, 0:1])
            )
            high_part, low_part = split(weight)
            w_high[at, :] = high_part
            w_low[at, :] = low_part
            return carry

        lax.fori_loop(0, tiles, tile, 0)
        first = nn(q_tr[...], w_high[...])
        product = first[:DS] + first[DS:] + nn(q_tr[0:DS, :], w_low[...])
        for b in range(blocks):
            part[xb, b] = product[:, b * LANES:(b + 1) * LANES]

    def both_gradients(step, carry):
        gradient(jnp.where(step == 0, 1 - x, x))

        @pl.when(step == 0)
        def _():
            for b in range(blocks):
                px_copy(b).start()
        return carry

    lax.fori_loop(0, 2, both_gradients, 0)
    for b in range(blocks):
        px_copy(b).wait_recv()
        x_sum[b] = part[x, b] + x_in[b]
        for step in range(1, groups):
            py_copy(step, b).start()
    for step in range(1, levels):
        div_copy(step, (z - step + levels) % levels).wait_recv()
    total = div_in[0, 0:1, :]
    for level in range(1, levels):
        total = total + div_in[level, 0:1, :]
    total_in[seq] = jnp.broadcast_to(total, (8, rows))
    total_copy(seq).start()
    for b in range(blocks):
        result = x_sum[b]
        for step in range(1, groups):
            py_copy(step, b).wait_recv()
            result = result + y_in[step, b]
        out_ref[seq, b * LANES:(b + 1) * LANES, :] = result.T
        out_copy(seq, b).start()
    total_copy(1 - seq).wait_recv()
    loss_ref[0, 0] = jnp.sum(total_in[0, 0:1, :] + total_in[1, 0:1, :]) / (
        batches * HEADS * rows * 2 * levels
    )
    total_copy(seq).wait_send()
    for copy in x_copies:
        copy.wait_send()

    def sent(j, carry):
        for slot in range(2):
            for to in range(levels):
                goes = source_sends(slot, to)
                if to in (0, last):
                    goes = jnp.logical_or(goes, forwards(slot, to))

                @pl.when(goes)
                def _():
                    for copy in z_copies(slot, j, to):
                        copy.wait_send()
        return carry

    lax.fori_loop(0, chunks, sent, 0)
    for step in range(1, 2 * groups):
        stat_copy(step).wait_send()
    for step in range(1, levels):
        div_copy(step, z).wait_send()
        for xb in range(2):
            col_copy(xb, step).wait_send()
    for b in range(blocks):
        px_copy(b).wait_send()
        for step in range(1, groups):
            py_copy(step, b).wait_send()
        out_copy(seq, b).wait_send()
        out_copy(1 - seq, b).wait_recv()


def folded_kernel(
    groups, levels, rows, batches,
    t_hbm, s_hbm, out_ref, loss_ref,
    in_t, in_s, row_n, col_t, col_s, row_t, row_s, t_sc, s_sc, acc,
    row_stat, col_stat, col_part, div_in, wide, col_level, w_row, q_tr, w_high, w_low,
    part, x_in, x_sum, y_in, turned, turned_in, total_in,
    load_sem, slot_sem, x_send, x_recv, z_send, z_recv,
    row_send, row_recv, end_send, end_recv, col_send, col_recv, div_send, div_recv,
    px_send, px_recv, py_send, py_recv, pz_send, pz_recv, out_send, out_recv, total_send, total_recv,
):
    chunks = rows // CHUNK
    pb = lax.axis_index("pb")
    ka = lax.axis_index("ka")
    seq = pb % batches
    y = pb // batches
    z = ka // 2
    x = ka % 2
    place = x * groups + y
    low = jnp.where(seq == 0, y, groups - 1 - y)
    high = levels - 1 - low
    sources = (low, high)
    outer = low == 0
    inner_level = jnp.logical_and(z > 0, z < levels - 1)
    end_level = jnp.logical_not(inner_level)
    active = jnp.logical_or(outer, inner_level)
    turning = jnp.logical_and(outer, inner_level)
    outer_end = jnp.logical_and(outer, end_level)
    y_outer = seq
    y_inner = 1 - seq
    mate = y * batches + (1 - seq)
    x_device = (pb, z * 2 + (1 - x))

    planes = []
    for step in range(1, 2 * groups):
        other = (place + step) % (2 * groups)
        planes.append(((other % groups) * batches + seq, z * 2 + other // groups))
    line = [(pb, ((z + step) % levels) * 2 + x) for step in range(1, levels)]
    barrier = pltpu.get_barrier_semaphore()
    count = 2 * groups * levels
    index = place * levels + z

    def greet(step, told):
        other = (index + step) % count
        spot, level = other // levels, other % levels
        inside = jnp.logical_and(level > 0, level < levels - 1)
        meets = jnp.logical_or(
            level == z,
            jnp.logical_or(
                jnp.logical_and(inside, inner_level), jnp.logical_and(spot % groups == y, outer)
            ),
        )

        @pl.when(meets)
        def _():
            device = ((spot % groups) * batches + seq, level * 2 + spot // groups)
            pl.semaphore_signal(barrier, inc=1, device_id=device, device_id_type=MESH)
        return told + jnp.where(meets, 1, 0)

    greeted = lax.fori_loop(1, count, greet, 0)
    diagonal = (1 - y) * batches + (1 - seq)
    for other in (mate, diagonal):
        pl.semaphore_signal(barrier, inc=1, device_id=(other, ka), device_id_type=MESH)

    loads = [
        pltpu.make_async_copy(t_hbm.at[seq], in_t.at[0], load_sem.at[0]),
        pltpu.make_async_copy(s_hbm.at[seq], in_s.at[0], load_sem.at[1]),
    ]
    for slot in range(2):
        @pl.when(z == sources[slot])
        def _():
            pltpu.make_async_copy(t_hbm.at[seq], col_t.at[slot], slot_sem.at[slot, 0]).start()
            pltpu.make_async_copy(s_hbm.at[seq], col_s.at[slot], slot_sem.at[slot, 1]).start()
    for load in loads:
        load.start()
    pl.semaphore_wait(barrier, greeted + 2)

    y_device = ((1 - y) * batches + seq, ka)

    def piece_copies(q, over_x):
        span = pl.ds(pl.multiple_of(q * CHUNK, CHUNK), CHUNK)
        return [
            pltpu.make_async_remote_copy(
                src_ref=src.at[seq, span, :] if over_x else dst.at[1, span, :], dst_ref=dst.at[1, span, :],
                send_sem=x_send.at[0 if over_x else 1, q, i], recv_sem=x_recv.at[q, i],
                device_id=x_device if over_x else y_device, device_id_type=MESH,
            )
            for i, (src, dst) in enumerate(((t_hbm, in_t), (s_hbm, in_s)))
        ]

    def z_copies(slot, j, to):
        span = pl.ds(pl.multiple_of(j * CHUNK, CHUNK), CHUNK)
        return [
            pltpu.make_async_remote_copy(
                src_ref=buf.at[slot, span, :], dst_ref=buf.at[slot, span, :],
                send_sem=z_send.at[to, slot, j, i], recv_sem=z_recv.at[slot, j, i],
                device_id=(pb, to * 2 + x), device_id_type=MESH,
            )
            for i, buf in enumerate((col_t, col_s))
        ]

    for slot in range(2):
        @pl.when(z == sources[slot])
        def _():
            pltpu.make_async_copy(t_hbm.at[seq], col_t.at[slot], slot_sem.at[slot, 0]).wait()
            pltpu.make_async_copy(s_hbm.at[seq], col_s.at[slot], slot_sem.at[slot, 1]).wait()

    last = levels - 1

    def source_sends(slot, to):
        return jnp.logical_and(z == sources[slot], to != z) if 0 < to < last else None

    def forwards(slot, to):
        beside = 1 if to == 0 else last - 1
        return jnp.logical_and(jnp.logical_and(outer, z == beside), sources[slot] != to)

    def put_rows(xb, teacher, student):
        t_high, t_low = split((teacher * (LOG2E / math.sqrt(DT))).T)
        s_high, s_low = split((student * (LOG2E / math.sqrt(DS))).T)
        row_n[xb] = jnp.concatenate(split(student * (1.0 / math.sqrt(DS))), axis=1)
        for part_index, (t_part, s_part) in enumerate(
            ((t_high, s_high), (t_low, s_low), (t_high, s_high))
        ):
            row_t[xb, part_index * DT:(part_index + 1) * DT, :] = t_part
            row_s[xb, part_index * DS:(part_index + 1) * DS, :] = s_part

    def relate(xb, j):
        span = pl.ds(pl.multiple_of(j * CHUNK, CHUNK), CHUNK)
        t_high, t_low = split(col_t[:, span, :].reshape(2 * CHUNK, DT))
        s_high, s_low = split(col_s[:, span, :].reshape(2 * CHUNK, DS))
        teacher = nn(jnp.concatenate([t_high, t_high, t_low], axis=1), row_t[xb])
        student = nn(jnp.concatenate([s_high, s_high, s_low], axis=1), row_s[xb])
        for slot in range(2):
            at = pl.ds(pl.multiple_of(slot * rows + j * CHUNK, PART), CHUNK)
            t_sc[xb, at, :] = teacher[slot * CHUNK:(slot + 1) * CHUNK]
            s_sc[xb, at, :] = student[slot * CHUNK:(slot + 1) * CHUNK]
        tiles = range(0, 2 * CHUNK, PART)

        def read(values, at):
            return values[at:at + PART].reshape(PART // 8, 8, rows)

        t_old, s_old = acc[xb, 0], acc[xb, 3]
        t_max, s_max = t_old, s_old
        for at in tiles:
            t_max = jnp.maximum(t_max, jnp.max(read(teacher, at), axis=0))
            s_max = jnp.maximum(s_max, jnp.max(read(student, at), axis=0))
        t_scale = jnp.exp2(t_old - t_max)
        s_scale = jnp.exp2(s_old - s_max)
        t_sum, cross, s_sum = acc[xb, 1] * t_scale, acc[xb, 2] * t_scale, acc[xb, 4] * s_scale
        for at in tiles:
            t_tile, s_tile = read(teacher, at), read(student, at)
            t_exp = jnp.exp2(t_tile - t_max[None])
            t_sum = t_sum + jnp.sum(t_exp, axis=0)
            cross = cross + jnp.sum(t_exp * (t_tile - s_tile), axis=0)
            s_sum = s_sum + jnp.sum(jnp.exp2(s_tile - s_max[None]), axis=0)
        acc[xb, 0] = t_max
        acc[xb, 1] = t_sum
        acc[xb, 2] = cross
        acc[xb, 3] = s_max
        acc[xb, 4] = s_sum

    def turn(j):
        for slot in range(2):
            at = pl.ds(pl.multiple_of(slot * rows + j * CHUNK, PART), CHUNK)
            t_top = jnp.max(jnp.maximum(t_sc[0, at, :], t_sc[1, at, :]), axis=1, keepdims=True)
            s_top = jnp.max(jnp.maximum(s_sc[0, at, :], s_sc[1, at, :]), axis=1, keepdims=True)
            t_all = c_all = s_all = jnp.zeros((CHUNK, rows), jnp.float32)
            for xb in range(2):
                t_exp = jnp.exp2(t_sc[xb, at, :] - t_top)
                t_all = t_all + t_exp
                c_all = c_all + t_exp * (t_sc[xb, at, :] - s_sc[xb, at, :])
                s_all = s_all + jnp.exp2(s_sc[xb, at, :] - s_top)
            sums = [jnp.sum(v, axis=1, keepdims=True) for v in (t_all, c_all, s_all)]
            col_part[at, 0:1] = t_top
            col_part[at, 1:2] = sums[0]
            col_part[at, 2:3] = sums[1]
            col_part[at, 3:4] = s_top
            col_part[at, 4:5] = sums[2]
            col_part[at, 5:8] = jnp.zeros((CHUNK, 3), jnp.float32)

    for xb in range(2):
        for kind in range(5):
            start = -jnp.inf if kind in (0, 3) else 0.0
            acc[xb, kind] = jnp.full((8, rows), start, jnp.float32)

    half = chunks // 2

    @pl.when(active)
    def _():
        for q in range(chunks):
            @pl.when(jnp.logical_or(end_level, q // half == y))
            def _():
                for copy in piece_copies(q, True):
                    copy.start()


    def first_send(j, carry):
        for slot in range(2):
            for to in range(1, last):
                @pl.when(source_sends(slot, to))
                def _():
                    for copy in z_copies(slot, j, to):
                        copy.start()
        return carry

    lax.fori_loop(0, chunks, first_send, 0)
    def arrive(j):
        for slot in range(2):
            @pl.when(z != sources[slot])
            def _():
                for copy in z_copies(slot, j, 1):
                    copy.wait_recv()
                for to in (0, last):
                    @pl.when(forwards(slot, to))
                    def _():
                        for copy in z_copies(slot, j, to):
                            copy.start()

    def gather(k, carry):
        late = k - half
        phase = jnp.where(k < half, 1, late % 3)
        j = jnp.where(k < half, k, late // 3 + jnp.where(phase == 0, 0, half))
        own = phase == 1

        @pl.when(k == half)
        def _():
            for q in range(chunks):
                @pl.when(jnp.logical_or(end_level, q // half != y))
                def _():
                    for copy in piece_copies(q, True):
                        copy.wait_recv()

        @pl.when(jnp.logical_or(k == 0, k == half))
        def _():
            which = jnp.where(k == 0, 0, 1)
            put_rows(jnp.where(k == 0, x, 1 - x), in_t[which], in_s[which])

        @pl.when(own)
        def _():
            arrive(j)

        @pl.when(jnp.logical_and(inner_level, k < half))
        def _():
            for copy in piece_copies(y * half + k, True):
                copy.wait_recv()
            for copy in piece_copies(y * half + k, False):
                copy.start()

        relate(jnp.where(own, x, 1 - x), j)

        @pl.when(jnp.logical_and(turning, jnp.logical_not(own)))
        def _():
            turn(j)
        return carry

    for load in loads:
        load.wait()
    lax.fori_loop(0, jnp.where(active, 2 * chunks, 0), gather, 0)

    mine = jnp.where(inner_level, place, x)

    @pl.when(active)
    def _():
        for xb in range(2):
            t_max, s_max = acc[xb, 0], acc[xb, 3]
            t_top = jnp.max(t_max, axis=0, keepdims=True)
            s_top = jnp.max(s_max, axis=0, keepdims=True)
            t_scale = jnp.exp2(t_max - t_top)
            s_scale = jnp.exp2(s_max - s_top)
            t_sum = jnp.sum(acc[xb, 1] * t_scale, axis=0, keepdims=True)
            cross = jnp.sum(acc[xb, 2] * t_scale, axis=0, keepdims=True)
            s_sum = jnp.sum(acc[xb, 4] * s_scale, axis=0, keepdims=True)
            row_stat[mine, xb] = jnp.concatenate(
                [t_top, t_sum, cross, s_top, s_sum, jnp.zeros((3, rows), jnp.float32)], axis=0
            )

    @pl.when(turning)
    def _():
        for slot in range(2):
            col_stat[slot, 1 + z] = col_part[slot * rows:(slot + 1) * rows, :].T

    def remote(src, dst, send, recv, device):
        return pltpu.make_async_remote_copy(
            src_ref=src, dst_ref=dst, send_sem=send, recv_sem=recv,
            device_id=device, device_id_type=MESH,
        )

    outer_pb = y_outer * batches + seq
    inner_pb = y_inner * batches + seq
    other_inner = last - z
    my_slot = jnp.where(z * 2 < levels, 0, 1)

    def inner_sends():
        copies = [
            remote(row_stat.at[place], row_stat.at[place], row_send.at[step], row_recv.at[place], planes[step - 1])
            for step in range(1, 2 * groups)
        ]
        for xb in range(2):
            copies.append(remote(
                row_stat.at[place, xb], col_stat.at[my_slot, place], col_send.at[xb, 0],
                col_recv.at[my_slot, place], (inner_pb, other_inner * 2 + xb),
            ))
        return copies

    def turning_sends():
        copies = []
        for slot, end in ((0, 0), (1, last)):
            src = col_stat.at[slot, 1 + z]
            for xb in range(2):
                copies.append(remote(
                    src, row_stat.at[1 + z, x], end_send.at[slot, xb], end_recv.at[z - 1, x],
                    (pb, end * 2 + xb),
                ))
            for i, level in enumerate((other_inner, last - end)):
                copies.append(remote(
                    src, col_stat.at[slot, 1 + z], end_send.at[slot, 2 + i], col_recv.at[slot, 1 + z],
                    (pb, level * 2 + x),
                ))
        return copies

    def end_sends():
        copies = [remote(row_stat.at[x], row_stat.at[x], row_send.at[0], row_recv.at[x], x_device)]
        for xb in range(2):
            for i, level in enumerate((1, last - 1, last - z)):
                copies.append(remote(
                    row_stat.at[x, xb], col_stat.at[my_slot, x], col_send.at[xb, 1 + i],
                    col_recv.at[my_slot, x], (pb, level * 2 + xb),
                ))
        return copies

    kinds = ((turning, turning_sends), (inner_level, inner_sends), (outer_end, end_sends))
    for case, sends in kinds:
        @pl.when(case)
        def _():
            for copy in sends():
                copy.start()

    @pl.when(active)
    def _():
        for slot in range(2):
            high_part, low_part = split((col_s[slot] * (1.0 / math.sqrt(DS))).T)
            q_tr[0:DS, slot * rows:(slot + 1) * rows] = high_part
            q_tr[DS:2 * DS, slot * rows:(slot + 1) * rows] = low_part

    def landed(ref, sem):
        remote(ref, ref, row_send.at[0], sem, x_device).wait_recv()

    @pl.when(inner_level)
    def _():
        for step in range(1, 2 * groups):
            other = (place + step) % (2 * groups)
            landed(row_stat.at[other], row_recv.at[other])

    @pl.when(outer_end)
    def _():
        landed(row_stat.at[1 - x], row_recv.at[1 - x])
        for xb in range(2):
            for level in range(2):
                landed(row_stat.at[2 + level, xb], end_recv.at[level, xb])

    def combine(stats):
        t_max = functools.reduce(jnp.maximum, [stat[0:1] for stat in stats])
        s_max = functools.reduce(jnp.maximum, [stat[3:4] for stat in stats])
        t_sum = cross = s_sum = jnp.zeros((1, rows), jnp.float32)
        for stat in stats:
            t_scale = jnp.exp2(stat[0:1] - t_max)
            t_sum = t_sum + stat[1:2] * t_scale
            cross = cross + stat[2:3] * t_scale
            s_sum = s_sum + stat[4:5] * jnp.exp2(stat[3:4] - s_max)
        t_level = t_max + jnp.log2(t_sum)
        s_level = s_max + jnp.log2(s_sum)
        return t_level, s_level, LN2 * (cross / t_sum - t_level + s_level)

    @pl.when(active)
    def _():
        divergence = jnp.zeros((1, rows), jnp.float32)
        for xb in range(2):
            t_level, s_level, share = combine([row_stat[other, xb] for other in range(2 * groups)])
            wide[xb] = jnp.concatenate([t_level, s_level], axis=0)
            divergence = divergence + share
        div_in[z] = jnp.broadcast_to(divergence, (8, rows))

    def div_copy(step, slot):
        return pltpu.make_async_remote_copy(
            src_ref=div_in.at[slot], dst_ref=div_in.at[slot],
            send_sem=div_send.at[step], recv_sem=div_recv.at[step],
            device_id=line[step - 1], device_id_type=MESH,
        )

    @pl.when(outer)
    def _():
        for step in range(1, levels):
            div_copy(step, z).start()

    tiles = 2 * rows // WIDE

    def row_weights(xb):
        rows_t = wide[xb, 0:1, :]
        rows_s = wide[xb, 1:2, :]

        def tile(j, carry):
            at = pl.ds(pl.multiple_of(j * WIDE, WIDE), WIDE)
            w_row[xb, at, :] = jnp.exp2(s_sc[xb, at, :] - rows_s) - jnp.exp2(t_sc[xb, at, :] - rows_t)
            return carry

        lax.fori_loop(0, tiles, tile, 0)

    def both_weights(xb, carry):
        row_weights(xb)
        return carry

    passes = jnp.where(active, 2, 0)
    lax.fori_loop(0, passes, both_weights, 0)
    for slot in range(2):
        @pl.when(jnp.logical_and(active, z == sources[slot]))
        def _():
            for other in range(2 * groups):
                col_stat[slot, other] = row_stat[other, x]

        @pl.when(jnp.logical_and(active, z != sources[slot]))
        def _():
            for other in range(2 * groups):
                @pl.when(jnp.logical_not(jnp.logical_and(turning, other == 1 + z)))
                def _():
                    landed(col_stat.at[slot, other], col_recv.at[slot, other])

    @pl.when(active)
    def _():
        for slot in range(2):
            t_level, s_level, _ = combine([col_stat[slot, other] for other in range(2 * groups)])
            both = jnp.concatenate([t_level, s_level, jnp.zeros((6, rows), jnp.float32)], axis=0)
            col_level[slot * rows:(slot + 1) * rows, :] = both.T

    blocks = rows // LANES

    def px_copy(b):
        return pltpu.make_async_remote_copy(
            src_ref=part.at[1 - x, b], dst_ref=x_in.at[b],
            send_sem=px_send.at[b], recv_sem=px_recv.at[b],
            device_id=x_device, device_id_type=MESH,
        )

    def py_copy(step, b):
        return pltpu.make_async_remote_copy(
            src_ref=x_sum.at[b], dst_ref=y_in.at[step, b],
            send_sem=py_send.at[step, b], recv_sem=py_recv.at[step, b],
            device_id=(((y + step) % groups) * batches + seq, ka), device_id_type=MESH,
        )

    def out_copy(which, b):
        span = pl.ds(b * LANES, LANES)
        return pltpu.make_async_remote_copy(
            src_ref=out_ref.at[which, span, :], dst_ref=out_ref.at[which, span, :],
            send_sem=out_send.at[b], recv_sem=out_recv.at[b],
            device_id=(mate, ka), device_id_type=MESH,
        )

    totals = [(((1 - y) * batches + seq), ka), (mate, ka), (diagonal, ka)]

    def total_copy(i):
        return remote(total_in.at[seq], total_in.at[seq], total_send.at[i], total_recv.at[seq], totals[i])

    def turned_copy(slot, b):
        end = 0 if slot == 0 else last
        return remote(
            turned.at[slot, b], turned_in.at[z - 1, b], pz_send.at[slot, b], pz_recv.at[z - 1, b],
            (pb, end * 2 + x),
        )

    def gradient(xb):
        product = jnp.zeros((DS, rows), jnp.float32)
        for start in range(0, 2 * rows, STEP):
            at = slice(start, start + STEP)
            col = col_level[at, :]
            weight = (
                w_row[xb, at, :]
                + jnp.exp2(s_sc[xb, at, :] - col[:, 1:2])
                - jnp.exp2(t_sc[xb, at, :] - col[:, 0:1])
            )
            high_part, low_part = split(weight)
            w_high[at, :] = high_part
            w_low[at, :] = low_part
            first = nn(q_tr[:, at], high_part)
            product = product + (first[:DS] + first[DS:] + nn(q_tr[0:DS, at], low_part))
        for b in range(blocks):
            part[xb, b] = product[:, b * LANES:(b + 1) * LANES]

    def turn_back(xb):
        back = nn(w_high[...], row_n[xb])
        back = back[:, :DS] + back[:, DS:] + nn(w_low[...], row_n[xb, :, 0:DS])
        for slot in range(2):
            for b in range(blocks):
                start = slot * rows + b * LANES
                piece = back[start:start + LANES]
                turned[slot, b] = jnp.where(xb == x, turned[slot, b] + piece, piece)

    def both_gradients(step, carry):
        xb = jnp.where(step == 0, 1 - x, x)
        gradient(xb)

        @pl.when(step == 0)
        def _():
            for b in range(blocks):
                px_copy(b).start()

        @pl.when(turning)
        def _():
            turn_back(xb)
        return carry

    lax.fori_loop(0, passes, both_gradients, 0)

    @pl.when(turning)
    def _():
        for b in range(blocks):
            for slot in range(2):
                turned_copy(slot, b).start()

    sends_y = jnp.logical_or(inner_level, outer)
    gets_y = jnp.logical_or(inner_level, jnp.logical_not(outer))
    for b in range(blocks):
        @pl.when(active)
        def _():
            px_copy(b).wait_recv()
            x_sum[b] = part[x, b] + x_in[b]

        @pl.when(outer_end)
        def _():
            for level in range(2):
                landed(turned_in.at[level, b], pz_recv.at[level, b])
            x_sum[b] = x_sum[b] + (turned_in[0, b] + turned_in[1, b]).T

        @pl.when(sends_y)
        def _():
            py_copy(1, b).start()

    @pl.when(outer)
    def _():
        for step in range(1, levels):
            div_copy(step, (z - step + levels) % levels).wait_recv()
        total = div_in[0, 0:1, :]
        for level in range(1, levels):
            total = total + div_in[level, 0:1, :]
        total_in[seq] = jnp.broadcast_to(total, (8, rows))
        for i in range(3):
            total_copy(i).start()

    for b in range(blocks):
        span = slice(b * LANES, (b + 1) * LANES)

        @pl.when(gets_y)
        def _():
            py_copy(1, b).wait_recv()

        @pl.when(inner_level)
        def _():
            out_ref[seq, span, :] = (x_sum[b] + y_in[1, b]).T

        @pl.when(outer_end)
        def _():
            out_ref[seq, span, :] = x_sum[b].T

        @pl.when(jnp.logical_not(active))
        def _():
            out_ref[seq, span, :] = y_in[1, b].T
        out_copy(seq, b).start()

    landed(total_in.at[1 - seq], total_recv.at[1 - seq])

    @pl.when(jnp.logical_not(outer))
    def _():
        landed(total_in.at[seq], total_recv.at[seq])
    loss_ref[0, 0] = jnp.sum(total_in[0, 0:1, :] + total_in[1, 0:1, :]) / (
        batches * HEADS * rows * 2 * levels
    )

    @pl.when(outer)
    def _():
        for i in range(3):
            total_copy(i).wait_send()

    @pl.when(active)
    def _():
        for q in range(chunks):
            @pl.when(jnp.logical_or(end_level, q // half == y))
            def _():
                for copy in piece_copies(q, True):
                    copy.wait_send()

            @pl.when(jnp.logical_and(inner_level, q // half == y))
            def _():
                for copy in piece_copies(q, False):
                    copy.wait_send()

    def sent(j, carry):
        for slot in range(2):
            for to in range(levels):
                goes = source_sends(slot, to) if 0 < to < last else forwards(slot, to)

                @pl.when(goes)
                def _():
                    for copy in z_copies(slot, j, to):
                        copy.wait_send()
        return carry

    lax.fori_loop(0, chunks, sent, 0)
    for case, sends in kinds:
        @pl.when(case)
        def _():
            for copy in sends():
                copy.wait_send()

    @pl.when(outer)
    def _():
        for step in range(1, levels):
            div_copy(step, z).wait_send()

    for b in range(blocks):
        @pl.when(active)
        def _():
            px_copy(b).wait_send()

        @pl.when(turning)
        def _():
            for slot in range(2):
                turned_copy(slot, b).wait_send()

        @pl.when(sends_y)
        def _():
            py_copy(1, b).wait_send()
        out_copy(seq, b).wait_send()
        out_copy(1 - seq, b).wait_recv()


def solution(mesh):
    def shards(teacher_q, student_q):
        batches, rows = teacher_q.shape[0], teacher_q.shape[1]
        groups = mesh.shape["pb"] // batches
        levels = mesh.shape["ka"] // 2
        chunks = rows // CHUNK
        blocks = rows // LANES
        f32, bf16 = jnp.float32, jnp.bfloat16
        dma = pltpu.SemaphoreType.DMA
        folds = groups == 2 and levels == 4
        chosen = folded_kernel if folds else kernel
        scratch = [
            pltpu.VMEM((2, rows, DT), f32),
            pltpu.VMEM((2, rows, DS), f32),
            pltpu.VMEM((2, rows, DT), f32),
            pltpu.VMEM((2, rows, DS), f32),
            pltpu.VMEM((2, 3 * DT, rows), bf16),
            pltpu.VMEM((2, 3 * DS, rows), bf16),
            pltpu.VMEM((2, 2 * rows, rows), f32),
            pltpu.VMEM((2, 2 * rows, rows), f32),
            pltpu.VMEM((2, 5, 8, rows), f32),
        ]
        if folds:
            scratch.insert(2, pltpu.VMEM((2, rows, 2 * DS), bf16))
        scratch += [
            pltpu.VMEM((4, 2, 8, rows), f32),
            pltpu.VMEM((2, 4, 8, rows), f32),
            pltpu.VMEM((2 * rows, 8), f32),
            pltpu.VMEM((levels, 8, rows), f32),
            pltpu.VMEM((2, 2, rows), f32),
            pltpu.VMEM((2 * rows, 8), f32),
            pltpu.VMEM((2, 2 * rows, rows), f32),
            pltpu.VMEM((2 * DS, 2 * rows), bf16),
            pltpu.VMEM((2 * rows, rows), bf16),
            pltpu.VMEM((2 * rows, rows), bf16),
            pltpu.VMEM((2, blocks, DS, LANES), f32),
            pltpu.VMEM((blocks, DS, LANES), f32),
            pltpu.VMEM((blocks, DS, LANES), f32),
            pltpu.VMEM((groups, blocks, DS, LANES), f32),
            pltpu.VMEM((2, blocks, LANES, DS), f32),
            pltpu.VMEM((2, blocks, LANES, DS), f32),
            pltpu.VMEM((batches, 8, rows), f32),
            dma((2,)),
            dma((2, 2)),
            dma((2, chunks, 2)),
            dma((chunks, 2)),
            dma((levels, 2, chunks, 2)),
            dma((2, chunks, 2)),
            dma((4,)),
            dma((4,)),
            dma((2, 4)),
            dma((2, 2)),
            dma((2, 4)),
            dma((2, 4)),
            dma((levels,)),
            dma((levels,)),
            dma((blocks,)),
            dma((blocks,)),
            dma((groups, blocks)),
            dma((groups, blocks)),
            dma((2, blocks)),
            dma((2, blocks)),
            dma((blocks,)),
            dma((blocks,)),
            dma((3,)),
            dma((2,)),
        ] if folds else [
            pltpu.VMEM((2 * groups, 2, 8, rows), f32),
            pltpu.VMEM((2, 2 * groups, 8, rows), f32),
            pltpu.VMEM((levels, 8, rows), f32),
            pltpu.VMEM((2, 2, rows), f32),
            pltpu.VMEM((2 * rows, 8), f32),
            pltpu.VMEM((2, 2 * rows, rows), f32),
            pltpu.VMEM((2 * DS, 2 * rows), bf16),
            pltpu.VMEM((2 * rows, rows), bf16),
            pltpu.VMEM((2 * rows, rows), bf16),
            pltpu.VMEM((2, blocks, DS, LANES), f32),
            pltpu.VMEM((blocks, DS, LANES), f32),
            pltpu.VMEM((blocks, DS, LANES), f32),
            pltpu.VMEM((groups, blocks, DS, LANES), f32),
            pltpu.VMEM((batches, 8, rows), f32),
            dma((2,)),
            dma((2, 2)),
            dma((2,)),
            dma((2,)),
            dma((levels, 2, chunks, 2)),
            dma((2, chunks, 2)),
            dma((2 * groups,)),
            dma((2 * groups,)),
            dma((2, levels)),
            dma((2, 2 * groups)),
            dma((levels,)),
            dma((levels,)),
            dma((blocks,)),
            dma((blocks,)),
            dma((groups, blocks)),
            dma((groups, blocks)),
            dma((blocks,)),
            dma((blocks,)),
            dma,
            dma,
        ]
        grad, loss = pl.pallas_call(
            functools.partial(chosen, groups, levels, rows, batches),
            out_shape=(
                jax.ShapeDtypeStruct((batches, rows, DS), f32),
                jax.ShapeDtypeStruct((1, 1), f32),
            ),
            in_specs=[pl.BlockSpec(memory_space=pl.ANY)] * 2,
            out_specs=(
                pl.BlockSpec(memory_space=pltpu.VMEM),
                pl.BlockSpec(memory_space=pltpu.SMEM),
            ),
            scratch_shapes=scratch,
            compiler_params=pltpu.CompilerParams(
                collective_id=1 if folds else 0, has_side_effects=True, vmem_limit_bytes=40 * 1024 * 1024
            ),
        )(pltpu.with_memory_space_constraint(teacher_q, pltpu.HBM), pltpu.with_memory_space_constraint(student_q, pltpu.HBM))
        return grad, loss.reshape(())

    in_specs = (P(None, "ka", None), P(None, "ka", None))
    out_specs = (P(None, "ka", None), P())
    return jax.shard_map(shards, mesh=mesh, in_specs=in_specs, out_specs=out_specs, check_vma=False)
```

```python
import functools
import math

import jax
import jax.numpy as jnp
from jax import lax
from jax.experimental import pallas as pl
from jax.experimental.pallas import tpu as pltpu
from jax.sharding import PartitionSpec as P

HEADS = 1
DT = 256
DS = 128
CHUNK = 96
LANES = 128
TILE = 64
PART = 32
WIDE = 192
STEP = 256
MESH = pl.DeviceIdType.MESH
LOG2E = 1.4426950408889634
LN2 = 0.6931471805599453


def split(values):
    high = values.astype(jnp.bfloat16)
    low = (values - high.astype(jnp.float32)).astype(jnp.bfloat16)
    return high, low


def nn(left, right):
    return jnp.dot(left, right, preferred_element_type=jnp.float32)


def kernel(
    groups, levels, rows, batches,
    t_hbm, s_hbm, out_ref, loss_ref,
    in_t, in_s, col_t, col_s, row_t, row_s, t_sc, s_sc, acc,
    stat_in, stat_col, div_in, wide, col_level, w_row, q_tr, w_high, w_low,
    part, x_in, x_sum, y_in, total_in,
    load_sem, slot_sem, x_send, x_recv, z_send, z_recv,
    stat_send, stat_recv, col_send, col_recv, div_send, div_recv,
    px_send, px_recv, py_send, py_recv, out_send, out_recv, total_send, total_recv,
):
    chunks = rows // CHUNK
    pb = lax.axis_index("pb")
    ka = lax.axis_index("ka")
    seq = pb % batches
    y = pb // batches
    z = ka // 2
    x = ka % 2
    place = x * groups + y
    low = jnp.where(seq == 0, y, groups - 1 - y)
    high = levels - 1 - low
    sources = (low, high)
    mate = y * batches + (1 - seq)
    x_device = (pb, z * 2 + (1 - x))

    planes = []
    for step in range(1, 2 * groups):
        other = (place + step) % (2 * groups)
        planes.append(((other % groups) * batches + seq, z * 2 + other // groups))
    line = [(pb, ((z + step) % levels) * 2 + x) for step in range(1, levels)]
    barrier = pltpu.get_barrier_semaphore()
    count = 2 * groups * levels
    index = place * levels + z

    def greet(step, carry):
        other = (index + step) % count
        spot, level = other // levels, other % levels
        device = ((spot % groups) * batches + seq, level * 2 + spot // groups)
        pl.semaphore_signal(barrier, inc=1, device_id=device, device_id_type=MESH)
        return carry

    lax.fori_loop(1, count, greet, 0)
    pl.semaphore_signal(barrier, inc=1, device_id=(mate, ka), device_id_type=MESH)

    loads = [
        pltpu.make_async_copy(t_hbm.at[seq], in_t.at[0], load_sem.at[0]),
        pltpu.make_async_copy(s_hbm.at[seq], in_s.at[0], load_sem.at[1]),
    ]
    for slot in range(2):
        @pl.when(z == sources[slot])
        def _():
            pltpu.make_async_copy(t_hbm.at[seq], col_t.at[slot], slot_sem.at[slot, 0]).start()
            pltpu.make_async_copy(s_hbm.at[seq], col_s.at[slot], slot_sem.at[slot, 1]).start()
    for load in loads:
        load.start()
    pl.semaphore_wait(barrier, count)

    x_copies = [
        pltpu.make_async_remote_copy(
            src_ref=src.at[seq], dst_ref=dst, send_sem=x_send.at[i], recv_sem=x_recv.at[i],
            device_id=x_device, device_id_type=MESH,
        )
        for i, (src, dst) in enumerate(((t_hbm, in_t.at[1]), (s_hbm, in_s.at[1])))
    ]

    def z_copies(slot, j, to):
        span = pl.ds(pl.multiple_of(j * CHUNK, CHUNK), CHUNK)
        return [
            pltpu.make_async_remote_copy(
                src_ref=buf.at[slot, span, :], dst_ref=buf.at[slot, span, :],
                send_sem=z_send.at[to, slot, j, i], recv_sem=z_recv.at[slot, j, i],
                device_id=(pb, to * 2 + x), device_id_type=MESH,
            )
            for i, buf in enumerate((col_t, col_s))
        ]

    for slot in range(2):
        @pl.when(z == sources[slot])
        def _():
            pltpu.make_async_copy(t_hbm.at[seq], col_t.at[slot], slot_sem.at[slot, 0]).wait()
            pltpu.make_async_copy(s_hbm.at[seq], col_s.at[slot], slot_sem.at[slot, 1]).wait()

    last = levels - 1

    def source_sends(slot, to):
        near = abs(z - to) == 1
        reach = (to != z) if 0 < to < last else near
        return jnp.logical_and(z == sources[slot], reach)

    def forwards(slot, to):
        beside = 1 if to == 0 else last - 1
        waits = jnp.logical_and(sources[slot] != z, sources[slot] != to)
        return jnp.logical_and(z == beside, waits)

    def put_rows(xb, teacher, student):
        t_high, t_low = split((teacher * (LOG2E / math.sqrt(DT))).T)
        s_high, s_low = split((student * (LOG2E / math.sqrt(DS))).T)
        for part_index, (t_part, s_part) in enumerate(
            ((t_high, s_high), (t_low, s_low), (t_high, s_high))
        ):
            row_t[xb, part_index * DT:(part_index + 1) * DT, :] = t_part
            row_s[xb, part_index * DS:(part_index + 1) * DS, :] = s_part

    def relate(xb, j):
        span = pl.ds(pl.multiple_of(j * CHUNK, CHUNK), CHUNK)
        t_high, t_low = split(col_t[:, span, :].reshape(2 * CHUNK, DT))
        s_high, s_low = split(col_s[:, span, :].reshape(2 * CHUNK, DS))
        teacher = nn(jnp.concatenate([t_high, t_high, t_low], axis=1), row_t[xb])
        student = nn(jnp.concatenate([s_high, s_high, s_low], axis=1), row_s[xb])
        tiles = []
        for slot in range(2):
            base = slot * rows + j * CHUNK
            at = pl.ds(pl.multiple_of(base, CHUNK), CHUNK)
            t_sc[xb, at, :] = teacher[slot * CHUNK:(slot + 1) * CHUNK]
            s_sc[xb, at, :] = student[slot * CHUNK:(slot + 1) * CHUNK]
            tiles += [pl.ds(pl.multiple_of(base + i * PART, PART), PART) for i in range(CHUNK // PART)]

        def read(ref, at):
            return ref[xb, at, :].reshape(PART // 8, 8, rows)

        t_old, s_old = acc[xb, 0], acc[xb, 3]
        t_max, s_max = t_old, s_old
        for at in tiles:
            t_max = jnp.maximum(t_max, jnp.max(read(t_sc, at), axis=0))
            s_max = jnp.maximum(s_max, jnp.max(read(s_sc, at), axis=0))
        t_scale = jnp.exp2(t_old - t_max)
        s_scale = jnp.exp2(s_old - s_max)
        t_sum, cross, s_sum = acc[xb, 1] * t_scale, acc[xb, 2] * t_scale, acc[xb, 4] * s_scale
        for at in tiles:
            t_tile, s_tile = read(t_sc, at), read(s_sc, at)
            t_exp = jnp.exp2(t_tile - t_max[None])
            t_sum = t_sum + jnp.sum(t_exp, axis=0)
            cross = cross + jnp.sum(t_exp * (t_tile - s_tile), axis=0)
            s_sum = s_sum + jnp.sum(jnp.exp2(s_tile - s_max[None]), axis=0)
        acc[xb, 0] = t_max
        acc[xb, 1] = t_sum
        acc[xb, 2] = cross
        acc[xb, 3] = s_max
        acc[xb, 4] = s_sum

    for xb in range(2):
        for kind in range(5):
            start = -jnp.inf if kind in (0, 3) else 0.0
            acc[xb, kind] = jnp.full((8, rows), start, jnp.float32)

    for copy in x_copies:
        copy.start()

    def first_send(j, carry):
        for slot in range(2):
            for to in range(levels):
                @pl.when(source_sends(slot, to))
                def _():
                    for copy in z_copies(slot, j, to):
                        copy.start()
        return carry

    lax.fori_loop(0, chunks, first_send, 0)
    half = chunks // 2

    def arrive(j):
        for slot in range(2):
            @pl.when(z != sources[slot])
            def _():
                for copy in z_copies(slot, j, 1):
                    copy.wait_recv()
                for to in (0, last):
                    @pl.when(forwards(slot, to))
                    def _():
                        for copy in z_copies(slot, j, to):
                            copy.start()

    def gather(k, carry):
        late = k - half
        phase = jnp.where(k < half, 1, late % 3)
        j = jnp.where(k < half, k, late // 3 + jnp.where(phase == 0, 0, half))
        own = phase == 1

        @pl.when(k == 0)
        def _():
            for load in loads:
                load.wait()

        @pl.when(k == half)
        def _():
            for copy in x_copies:
                copy.wait_recv()

        @pl.when(jnp.logical_or(k == 0, k == half))
        def _():
            which = jnp.where(k == 0, 0, 1)
            put_rows(jnp.where(k == 0, x, 1 - x), in_t[which], in_s[which])

        @pl.when(own)
        def _():
            arrive(j)

        relate(jnp.where(own, x, 1 - x), j)
        return carry

    lax.fori_loop(0, 2 * chunks, gather, 0)

    for xb in range(2):
        t_max, s_max = acc[xb, 0], acc[xb, 3]
        t_top = jnp.max(t_max, axis=0, keepdims=True)
        s_top = jnp.max(s_max, axis=0, keepdims=True)
        t_scale = jnp.exp2(t_max - t_top)
        s_scale = jnp.exp2(s_max - s_top)
        t_sum = jnp.sum(acc[xb, 1] * t_scale, axis=0, keepdims=True)
        cross = jnp.sum(acc[xb, 2] * t_scale, axis=0, keepdims=True)
        s_sum = jnp.sum(acc[xb, 4] * s_scale, axis=0, keepdims=True)
        stat_in[place, xb] = jnp.concatenate(
            [t_top, t_sum, cross, s_top, s_sum, jnp.zeros((3, rows), jnp.float32)], axis=0
        )

    def stat_copy(step):
        return pltpu.make_async_remote_copy(
            src_ref=stat_in.at[place], dst_ref=stat_in.at[place],
            send_sem=stat_send.at[step], recv_sem=stat_recv.at[step],
            device_id=planes[step - 1], device_id_type=MESH,
        )

    def stat_wait(step):
        return pltpu.make_async_remote_copy(
            src_ref=stat_in.at[(place - step + 2 * groups) % (2 * groups)],
            dst_ref=stat_in.at[(place - step + 2 * groups) % (2 * groups)],
            send_sem=stat_send.at[step], recv_sem=stat_recv.at[step],
            device_id=planes[step - 1], device_id_type=MESH,
        )

    near = jnp.minimum(z, levels - 1 - z)
    user = jnp.where(seq == 0, near, groups - 1 - near)
    my_slot = jnp.where(z == near, 0, 1)

    def col_copy(xb, step):
        return pltpu.make_async_remote_copy(
            src_ref=stat_in.at[place, xb], dst_ref=stat_col.at[my_slot, place],
            send_sem=col_send.at[xb, step], recv_sem=col_recv.at[my_slot, place],
            device_id=(user * batches + seq, ((z + step) % levels) * 2 + xb), device_id_type=MESH,
        )

    for step in range(1, levels):
        for xb in range(2):
            col_copy(xb, step).start()
    for step in range(1, 2 * groups):
        stat_copy(step).start()
    for slot in range(2):
        high_part, low_part = split((col_s[slot] * (1.0 / math.sqrt(DS))).T)
        q_tr[0:DS, slot * rows:(slot + 1) * rows] = high_part
        q_tr[DS:2 * DS, slot * rows:(slot + 1) * rows] = low_part
    for step in range(1, 2 * groups):
        stat_wait(step).wait_recv()

    def combine(stats):
        t_max = functools.reduce(jnp.maximum, [stat[0:1] for stat in stats])
        s_max = functools.reduce(jnp.maximum, [stat[3:4] for stat in stats])
        t_sum = cross = s_sum = jnp.zeros((1, rows), jnp.float32)
        for stat in stats:
            t_scale = jnp.exp2(stat[0:1] - t_max)
            t_sum = t_sum + stat[1:2] * t_scale
            cross = cross + stat[2:3] * t_scale
            s_sum = s_sum + stat[4:5] * jnp.exp2(stat[3:4] - s_max)
        t_level = t_max + jnp.log2(t_sum)
        s_level = s_max + jnp.log2(s_sum)
        return t_level, s_level, LN2 * (cross / t_sum - t_level + s_level)

    divergence = jnp.zeros((1, rows), jnp.float32)
    for xb in range(2):
        t_level, s_level, share = combine([stat_in[other, xb] for other in range(2 * groups)])
        wide[xb] = jnp.concatenate([t_level, s_level], axis=0)
        divergence = divergence + share
    div_in[z] = jnp.broadcast_to(divergence, (8, rows))

    def div_copy(step, slot):
        return pltpu.make_async_remote_copy(
            src_ref=div_in.at[slot], dst_ref=div_in.at[slot],
            send_sem=div_send.at[step], recv_sem=div_recv.at[step],
            device_id=line[step - 1], device_id_type=MESH,
        )

    for step in range(1, levels):
        div_copy(step, z).start()

    tiles = 2 * rows // TILE

    def row_weights(xb):
        rows_t = wide[xb, 0:1, :]
        rows_s = wide[xb, 1:2, :]

        def tile(j, carry):
            at = pl.ds(pl.multiple_of(j * TILE, TILE), TILE)
            w_row[xb, at, :] = jnp.exp2(s_sc[xb, at, :] - rows_s) - jnp.exp2(t_sc[xb, at, :] - rows_t)
            return carry

        lax.fori_loop(0, tiles, tile, 0)

    def both_weights(xb, carry):
        row_weights(xb)
        return carry

    lax.fori_loop(0, 2, both_weights, 0)
    for slot in range(2):
        @pl.when(z == sources[slot])
        def _():
            for other in range(2 * groups):
                stat_col[slot, other] = stat_in[other, x]

        @pl.when(z != sources[slot])
        def _():
            for other in range(2 * groups):
                pltpu.make_async_remote_copy(
                    src_ref=stat_col.at[slot, other], dst_ref=stat_col.at[slot, other],
                    send_sem=col_send.at[0, 0], recv_sem=col_recv.at[slot, other],
                    device_id=x_device, device_id_type=MESH,
                ).wait_recv()

        t_level, s_level, _ = combine([stat_col[slot, other] for other in range(2 * groups)])
        both = jnp.concatenate([t_level, s_level, jnp.zeros((6, rows), jnp.float32)], axis=0)
        col_level[slot * rows:(slot + 1) * rows, :] = both.T

    blocks = rows // LANES

    def px_copy(b):
        return pltpu.make_async_remote_copy(
            src_ref=part.at[1 - x, b], dst_ref=x_in.at[b],
            send_sem=px_send.at[b], recv_sem=px_recv.at[b],
            device_id=x_device, device_id_type=MESH,
        )

    def py_copy(step, b):
        return pltpu.make_async_remote_copy(
            src_ref=x_sum.at[b], dst_ref=y_in.at[step, b],
            send_sem=py_send.at[step, b], recv_sem=py_recv.at[step, b],
            device_id=(((y + step) % groups) * batches + seq, ka), device_id_type=MESH,
        )

    def out_copy(which, b):
        span = pl.ds(b * LANES, LANES)
        return pltpu.make_async_remote_copy(
            src_ref=out_ref.at[which, span, :], dst_ref=out_ref.at[which, span, :],
            send_sem=out_send.at[b], recv_sem=out_recv.at[b],
            device_id=(mate, ka), device_id_type=MESH,
        )

    def total_copy(which):
        return pltpu.make_async_remote_copy(
            src_ref=total_in.at[which], dst_ref=total_in.at[which],
            send_sem=total_send, recv_sem=total_recv,
            device_id=(mate, ka), device_id_type=MESH,
        )

    def gradient(xb):
        def tile(j, carry):
            at = pl.ds(pl.multiple_of(j * TILE, TILE), TILE)
            col = col_level[at, :]
            weight = (
                w_row[xb, at, :]
                + jnp.exp2(s_sc[xb, at, :] - col[:, 1:2])
                - jnp.exp2(t_sc[xb, at, :] - col[:, 0:1])
            )
            high_part, low_part = split(weight)
            w_high[at, :] = high_part
            w_low[at, :] = low_part
            return carry

        lax.fori_loop(0, tiles, tile, 0)
        first = nn(q_tr[...], w_high[...])
        product = first[:DS] + first[DS:] + nn(q_tr[0:DS, :], w_low[...])
        for b in range(blocks):
            part[xb, b] = product[:, b * LANES:(b + 1) * LANES]

    def both_gradients(step, carry):
        gradient(jnp.where(step == 0, 1 - x, x))

        @pl.when(step == 0)
        def _():
            for b in range(blocks):
                px_copy(b).start()
        return carry

    lax.fori_loop(0, 2, both_gradients, 0)
    for b in range(blocks):
        px_copy(b).wait_recv()
        x_sum[b] = part[x, b] + x_in[b]
        for step in range(1, groups):
            py_copy(step, b).start()
    for step in range(1, levels):
        div_copy(step, (z - step + levels) % levels).wait_recv()
    total = div_in[0, 0:1, :]
    for level in range(1, levels):
        total = total + div_in[level, 0:1, :]
    total_in[seq] = jnp.broadcast_to(total, (8, rows))
    total_copy(seq).start()
    for b in range(blocks):
        result = x_sum[b]
        for step in range(1, groups):
            py_copy(step, b).wait_recv()
            result = result + y_in[step, b]
        out_ref[seq, b * LANES:(b + 1) * LANES, :] = result.T
        out_copy(seq, b).start()
    total_copy(1 - seq).wait_recv()
    loss_ref[0, 0] = jnp.sum(total_in[0, 0:1, :] + total_in[1, 0:1, :]) / (
        batches * HEADS * rows * 2 * levels
    )
    total_copy(seq).wait_send()
    for copy in x_copies:
        copy.wait_send()

    def sent(j, carry):
        for slot in range(2):
            for to in range(levels):
                goes = source_sends(slot, to)
                if to in (0, last):
                    goes = jnp.logical_or(goes, forwards(slot, to))

                @pl.when(goes)
                def _():
                    for copy in z_copies(slot, j, to):
                        copy.wait_send()
        return carry

    lax.fori_loop(0, chunks, sent, 0)
    for step in range(1, 2 * groups):
        stat_copy(step).wait_send()
    for step in range(1, levels):
        div_copy(step, z).wait_send()
        for xb in range(2):
            col_copy(xb, step).wait_send()
    for b in range(blocks):
        px_copy(b).wait_send()
        for step in range(1, groups):
            py_copy(step, b).wait_send()
        out_copy(seq, b).wait_send()
        out_copy(1 - seq, b).wait_recv()


def folded_kernel(
    groups, levels, rows, batches,
    t_hbm, s_hbm, out_ref, loss_ref,
    in_t, in_s, row_n, col_t, col_s, row_t, row_s, t_sc, s_sc, acc,
    row_stat, col_stat, col_part, div_in, wide, col_level, w_row, q_tr, w_high, w_low,
    part, x_in, x_sum, y_in, turned, turned_in, total_in,
    load_sem, slot_sem, x_send, x_recv, z_send, z_recv,
    row_send, row_recv, end_send, end_recv, col_send, col_recv, div_send, div_recv,
    px_send, px_recv, py_send, py_recv, pz_send, pz_recv, out_send, out_recv, total_send, total_recv,
):
    chunks = rows // CHUNK
    pb = lax.axis_index("pb")
    ka = lax.axis_index("ka")
    seq = pb % batches
    y = pb // batches
    z = ka // 2
    x = ka % 2
    place = x * groups + y
    low = jnp.where(seq == 0, y, groups - 1 - y)
    high = levels - 1 - low
    sources = (low, high)
    outer = low == 0
    inner_level = jnp.logical_and(z > 0, z < levels - 1)
    end_level = jnp.logical_not(inner_level)
    active = jnp.logical_or(outer, inner_level)
    turning = jnp.logical_and(outer, inner_level)
    outer_end = jnp.logical_and(outer, end_level)
    y_outer = seq
    y_inner = 1 - seq
    mate = y * batches + (1 - seq)
    x_device = (pb, z * 2 + (1 - x))

    planes = []
    for step in range(1, 2 * groups):
        other = (place + step) % (2 * groups)
        planes.append(((other % groups) * batches + seq, z * 2 + other // groups))
    line = [(pb, ((z + step) % levels) * 2 + x) for step in range(1, levels)]
    barrier = pltpu.get_barrier_semaphore()
    count = 2 * groups * levels
    index = place * levels + z

    def greet(step, told):
        other = (index + step) % count
        spot, level = other // levels, other % levels
        inside = jnp.logical_and(level > 0, level < levels - 1)
        meets = jnp.logical_or(
            level == z,
            jnp.logical_or(
                jnp.logical_and(inside, inner_level), jnp.logical_and(spot % groups == y, outer)
            ),
        )

        @pl.when(meets)
        def _():
            device = ((spot % groups) * batches + seq, level * 2 + spot // groups)
            pl.semaphore_signal(barrier, inc=1, device_id=device, device_id_type=MESH)
        return told + jnp.where(meets, 1, 0)

    greeted = lax.fori_loop(1, count, greet, 0)
    diagonal = (1 - y) * batches + (1 - seq)
    for other in (mate, diagonal):
        pl.semaphore_signal(barrier, inc=1, device_id=(other, ka), device_id_type=MESH)

    loads = [
        pltpu.make_async_copy(t_hbm.at[seq], in_t.at[0], load_sem.at[0]),
        pltpu.make_async_copy(s_hbm.at[seq], in_s.at[0], load_sem.at[1]),
    ]
    for slot in range(2):
        @pl.when(z == sources[slot])
        def _():
            pltpu.make_async_copy(t_hbm.at[seq], col_t.at[slot], slot_sem.at[slot, 0]).start()
            pltpu.make_async_copy(s_hbm.at[seq], col_s.at[slot], slot_sem.at[slot, 1]).start()
    for load in loads:
        load.start()
    pl.semaphore_wait(barrier, greeted + 2)

    y_device = ((1 - y) * batches + seq, ka)

    def piece_copies(q, over_x):
        span = pl.ds(pl.multiple_of(q * CHUNK, CHUNK), CHUNK)
        return [
            pltpu.make_async_remote_copy(
                src_ref=src.at[seq, span, :] if over_x else dst.at[1, span, :], dst_ref=dst.at[1, span, :],
                send_sem=x_send.at[0 if over_x else 1, q, i], recv_sem=x_recv.at[q, i],
                device_id=x_device if over_x else y_device, device_id_type=MESH,
            )
            for i, (src, dst) in enumerate(((t_hbm, in_t), (s_hbm, in_s)))
        ]

    def z_copies(slot, j, to):
        span = pl.ds(pl.multiple_of(j * CHUNK, CHUNK), CHUNK)
        return [
            pltpu.make_async_remote_copy(
                src_ref=buf.at[slot, span, :], dst_ref=buf.at[slot, span, :],
                send_sem=z_send.at[to, slot, j, i], recv_sem=z_recv.at[slot, j, i],
                device_id=(pb, to * 2 + x), device_id_type=MESH,
            )
            for i, buf in enumerate((col_t, col_s))
        ]

    for slot in range(2):
        @pl.when(z == sources[slot])
        def _():
            pltpu.make_async_copy(t_hbm.at[seq], col_t.at[slot], slot_sem.at[slot, 0]).wait()
            pltpu.make_async_copy(s_hbm.at[seq], col_s.at[slot], slot_sem.at[slot, 1]).wait()

    last = levels - 1

    def source_sends(slot, to):
        return jnp.logical_and(z == sources[slot], to != z) if 0 < to < last else None

    def forwards(slot, to):
        beside = 1 if to == 0 else last - 1
        return jnp.logical_and(jnp.logical_and(outer, z == beside), sources[slot] != to)

    def put_rows(xb, teacher, student):
        t_high, t_low = split((teacher * (LOG2E / math.sqrt(DT))).T)
        s_high, s_low = split((student * (LOG2E / math.sqrt(DS))).T)
        row_n[xb] = jnp.concatenate(split(student * (1.0 / math.sqrt(DS))), axis=1)
        for part_index, (t_part, s_part) in enumerate(
            ((t_high, s_high), (t_low, s_low), (t_high, s_high))
        ):
            row_t[xb, part_index * DT:(part_index + 1) * DT, :] = t_part
            row_s[xb, part_index * DS:(part_index + 1) * DS, :] = s_part

    def relate(xb, j):
        span = pl.ds(pl.multiple_of(j * CHUNK, CHUNK), CHUNK)
        t_high, t_low = split(col_t[:, span, :].reshape(2 * CHUNK, DT))
        s_high, s_low = split(col_s[:, span, :].reshape(2 * CHUNK, DS))
        teacher = nn(jnp.concatenate([t_high, t_high, t_low], axis=1), row_t[xb])
        student = nn(jnp.concatenate([s_high, s_high, s_low], axis=1), row_s[xb])
        for slot in range(2):
            at = pl.ds(pl.multiple_of(slot * rows + j * CHUNK, PART), CHUNK)
            t_sc[xb, at, :] = teacher[slot * CHUNK:(slot + 1) * CHUNK]
            s_sc[xb, at, :] = student[slot * CHUNK:(slot + 1) * CHUNK]
        tiles = range(0, 2 * CHUNK, PART)

        def read(values, at):
            return values[at:at + PART].reshape(PART // 8, 8, rows)

        t_old, s_old = acc[xb, 0], acc[xb, 3]
        t_max, s_max = t_old, s_old
        for at in tiles:
            t_max = jnp.maximum(t_max, jnp.max(read(teacher, at), axis=0))
            s_max = jnp.maximum(s_max, jnp.max(read(student, at), axis=0))
        t_scale = jnp.exp2(t_old - t_max)
        s_scale = jnp.exp2(s_old - s_max)
        t_sum, cross, s_sum = acc[xb, 1] * t_scale, acc[xb, 2] * t_scale, acc[xb, 4] * s_scale
        for at in tiles:
            t_tile, s_tile = read(teacher, at), read(student, at)
            t_exp = jnp.exp2(t_tile - t_max[None])
            t_sum = t_sum + jnp.sum(t_exp, axis=0)
            cross = cross + jnp.sum(t_exp * (t_tile - s_tile), axis=0)
            s_sum = s_sum + jnp.sum(jnp.exp2(s_tile - s_max[None]), axis=0)
        acc[xb, 0] = t_max
        acc[xb, 1] = t_sum
        acc[xb, 2] = cross
        acc[xb, 3] = s_max
        acc[xb, 4] = s_sum

    def turn(j):
        for slot in range(2):
            at = pl.ds(pl.multiple_of(slot * rows + j * CHUNK, PART), CHUNK)
            t_top = jnp.max(jnp.maximum(t_sc[0, at, :], t_sc[1, at, :]), axis=1, keepdims=True)
            s_top = jnp.max(jnp.maximum(s_sc[0, at, :], s_sc[1, at, :]), axis=1, keepdims=True)
            t_all = c_all = s_all = jnp.zeros((CHUNK, rows), jnp.float32)
            for xb in range(2):
                t_exp = jnp.exp2(t_sc[xb, at, :] - t_top)
                t_all = t_all + t_exp
                c_all = c_all + t_exp * (t_sc[xb, at, :] - s_sc[xb, at, :])
                s_all = s_all + jnp.exp2(s_sc[xb, at, :] - s_top)
            sums = [jnp.sum(v, axis=1, keepdims=True) for v in (t_all, c_all, s_all)]
            col_part[at, 0:1] = t_top
            col_part[at, 1:2] = sums[0]
            col_part[at, 2:3] = sums[1]
            col_part[at, 3:4] = s_top
            col_part[at, 4:5] = sums[2]
            col_part[at, 5:8] = jnp.zeros((CHUNK, 3), jnp.float32)

    for xb in range(2):
        for kind in range(5):
            start = -jnp.inf if kind in (0, 3) else 0.0
            acc[xb, kind] = jnp.full((8, rows), start, jnp.float32)

    half = chunks // 2

    @pl.when(active)
    def _():
        for q in range(chunks):
            @pl.when(jnp.logical_or(end_level, q // half == y))
            def _():
                for copy in piece_copies(q, True):
                    copy.start()


    def first_send(j, carry):
        for slot in range(2):
            for to in range(1, last):
                @pl.when(source_sends(slot, to))
                def _():
                    for copy in z_copies(slot, j, to):
                        copy.start()
        return carry

    lax.fori_loop(0, chunks, first_send, 0)
    def arrive(j):
        for slot in range(2):
            @pl.when(z != sources[slot])
            def _():
                for copy in z_copies(slot, j, 1):
                    copy.wait_recv()
                for to in (0, last):
                    @pl.when(forwards(slot, to))
                    def _():
                        for copy in z_copies(slot, j, to):
                            copy.start()

    def gather(k, carry):
        late = k - half
        phase = jnp.where(k < half, 1, late % 3)
        j = jnp.where(k < half, k, late // 3 + jnp.where(phase == 0, 0, half))
        own = phase == 1

        @pl.when(k == half)
        def _():
            for q in range(chunks):
                @pl.when(jnp.logical_or(end_level, q // half != y))
                def _():
                    for copy in piece_copies(q, True):
                        copy.wait_recv()

        @pl.when(jnp.logical_or(k == 0, k == half))
        def _():
            which = jnp.where(k == 0, 0, 1)
            put_rows(jnp.where(k == 0, x, 1 - x), in_t[which], in_s[which])

        @pl.when(own)
        def _():
            arrive(j)

        @pl.when(jnp.logical_and(inner_level, k < half))
        def _():
            for copy in piece_copies(y * half + k, True):
                copy.wait_recv()
            for copy in piece_copies(y * half + k, False):
                copy.start()

        relate(jnp.where(own, x, 1 - x), j)

        @pl.when(jnp.logical_and(turning, jnp.logical_not(own)))
        def _():
            turn(j)
        return carry

    for load in loads:
        load.wait()
    lax.fori_loop(0, jnp.where(active, 2 * chunks, 0), gather, 0)

    mine = jnp.where(inner_level, place, x)

    @pl.when(active)
    def _():
        for xb in range(2):
            t_max, s_max = acc[xb, 0], acc[xb, 3]
            t_top = jnp.max(t_max, axis=0, keepdims=True)
            s_top = jnp.max(s_max, axis=0, keepdims=True)
            t_scale = jnp.exp2(t_max - t_top)
            s_scale = jnp.exp2(s_max - s_top)
            t_sum = jnp.sum(acc[xb, 1] * t_scale, axis=0, keepdims=True)
            cross = jnp.sum(acc[xb, 2] * t_scale, axis=0, keepdims=True)
            s_sum = jnp.sum(acc[xb, 4] * s_scale, axis=0, keepdims=True)
            row_stat[mine, xb] = jnp.concatenate(
                [t_top, t_sum, cross, s_top, s_sum, jnp.zeros((3, rows), jnp.float32)], axis=0
            )

    @pl.when(turning)
    def _():
        for slot in range(2):
            col_stat[slot, 1 + z] = col_part[slot * rows:(slot + 1) * rows, :].T

    def remote(src, dst, send, recv, device):
        return pltpu.make_async_remote_copy(
            src_ref=src, dst_ref=dst, send_sem=send, recv_sem=recv,
            device_id=device, device_id_type=MESH,
        )

    outer_pb = y_outer * batches + seq
    inner_pb = y_inner * batches + seq
    other_inner = last - z
    my_slot = jnp.where(z * 2 < levels, 0, 1)

    def inner_sends():
        copies = [
            remote(row_stat.at[place], row_stat.at[place], row_send.at[step], row_recv.at[place], planes[step - 1])
            for step in range(1, 2 * groups)
        ]
        for xb in range(2):
            copies.append(remote(
                row_stat.at[place, xb], col_stat.at[my_slot, place], col_send.at[xb, 0],
                col_recv.at[my_slot, place], (inner_pb, other_inner * 2 + xb),
            ))
        return copies

    def turning_sends():
        copies = []
        for slot, end in ((0, 0), (1, last)):
            src = col_stat.at[slot, 1 + z]
            for xb in range(2):
                copies.append(remote(
                    src, row_stat.at[1 + z, x], end_send.at[slot, xb], end_recv.at[z - 1, x],
                    (pb, end * 2 + xb),
                ))
            for i, level in enumerate((other_inner, last - end)):
                copies.append(remote(
                    src, col_stat.at[slot, 1 + z], end_send.at[slot, 2 + i], col_recv.at[slot, 1 + z],
                    (pb, level * 2 + x),
                ))
        return copies

    def end_sends():
        copies = [remote(row_stat.at[x], row_stat.at[x], row_send.at[0], row_recv.at[x], x_device)]
        for xb in range(2):
            for i, level in enumerate((1, last - 1, last - z)):
                copies.append(remote(
                    row_stat.at[x, xb], col_stat.at[my_slot, x], col_send.at[xb, 1 + i],
                    col_recv.at[my_slot, x], (pb, level * 2 + xb),
                ))
        return copies

    kinds = ((turning, turning_sends), (inner_level, inner_sends), (outer_end, end_sends))
    for case, sends in kinds:
        @pl.when(case)
        def _():
            for copy in sends():
                copy.start()

    @pl.when(active)
    def _():
        for slot in range(2):
            high_part, low_part = split((col_s[slot] * (1.0 / math.sqrt(DS))).T)
            q_tr[0:DS, slot * rows:(slot + 1) * rows] = high_part
            q_tr[DS:2 * DS, slot * rows:(slot + 1) * rows] = low_part

    def landed(ref, sem):
        remote(ref, ref, row_send.at[0], sem, x_device).wait_recv()

    @pl.when(inner_level)
    def _():
        for step in range(1, 2 * groups):
            other = (place + step) % (2 * groups)
            landed(row_stat.at[other], row_recv.at[other])

    @pl.when(outer_end)
    def _():
        landed(row_stat.at[1 - x], row_recv.at[1 - x])
        for xb in range(2):
            for level in range(2):
                landed(row_stat.at[2 + level, xb], end_recv.at[level, xb])

    def combine(stats):
        t_max = functools.reduce(jnp.maximum, [stat[0:1] for stat in stats])
        s_max = functools.reduce(jnp.maximum, [stat[3:4] for stat in stats])
        t_sum = cross = s_sum = jnp.zeros((1, rows), jnp.float32)
        for stat in stats:
            t_scale = jnp.exp2(stat[0:1] - t_max)
            t_sum = t_sum + stat[1:2] * t_scale
            cross = cross + stat[2:3] * t_scale
            s_sum = s_sum + stat[4:5] * jnp.exp2(stat[3:4] - s_max)
        t_level = t_max + jnp.log2(t_sum)
        s_level = s_max + jnp.log2(s_sum)
        return t_level, s_level, LN2 * (cross / t_sum - t_level + s_level)

    @pl.when(active)
    def _():
        divergence = jnp.zeros((1, rows), jnp.float32)
        for xb in range(2):
            t_level, s_level, share = combine([row_stat[other, xb] for other in range(2 * groups)])
            wide[xb] = jnp.concatenate([t_level, s_level], axis=0)
            divergence = divergence + share
        div_in[z] = jnp.broadcast_to(divergence, (8, rows))

    def div_copy(step, slot):
        return pltpu.make_async_remote_copy(
            src_ref=div_in.at[slot], dst_ref=div_in.at[slot],
            send_sem=div_send.at[step], recv_sem=div_recv.at[step],
            device_id=line[step - 1], device_id_type=MESH,
        )

    @pl.when(outer)
    def _():
        for step in range(1, levels):
            div_copy(step, z).start()

    tiles = 2 * rows // WIDE

    def row_weights(xb):
        rows_t = wide[xb, 0:1, :]
        rows_s = wide[xb, 1:2, :]

        def tile(j, carry):
            at = pl.ds(pl.multiple_of(j * WIDE, WIDE), WIDE)
            w_row[xb, at, :] = jnp.exp2(s_sc[xb, at, :] - rows_s) - jnp.exp2(t_sc[xb, at, :] - rows_t)
            return carry

        lax.fori_loop(0, tiles, tile, 0)

    def both_weights(xb, carry):
        row_weights(xb)
        return carry

    passes = jnp.where(active, 2, 0)
    lax.fori_loop(0, passes, both_weights, 0)
    for slot in range(2):
        @pl.when(jnp.logical_and(active, z == sources[slot]))
        def _():
            for other in range(2 * groups):
                col_stat[slot, other] = row_stat[other, x]

        @pl.when(jnp.logical_and(active, z != sources[slot]))
        def _():
            for other in range(2 * groups):
                @pl.when(jnp.logical_not(jnp.logical_and(turning, other == 1 + z)))
                def _():
                    landed(col_stat.at[slot, other], col_recv.at[slot, other])

    @pl.when(active)
    def _():
        for slot in range(2):
            t_level, s_level, _ = combine([col_stat[slot, other] for other in range(2 * groups)])
            both = jnp.concatenate([t_level, s_level, jnp.zeros((6, rows), jnp.float32)], axis=0)
            col_level[slot * rows:(slot + 1) * rows, :] = both.T

    blocks = rows // LANES

    def px_copy(b):
        return pltpu.make_async_remote_copy(
            src_ref=part.at[1 - x, b], dst_ref=x_in.at[b],
            send_sem=px_send.at[b], recv_sem=px_recv.at[b],
            device_id=x_device, device_id_type=MESH,
        )

    def py_copy(step, b):
        return pltpu.make_async_remote_copy(
            src_ref=x_sum.at[b], dst_ref=y_in.at[step, b],
            send_sem=py_send.at[step, b], recv_sem=py_recv.at[step, b],
            device_id=(((y + step) % groups) * batches + seq, ka), device_id_type=MESH,
        )

    def out_copy(which, b, to):
        span = pl.ds(b * LANES, LANES)
        return pltpu.make_async_remote_copy(
            src_ref=out_ref.at[which, span, :], dst_ref=out_ref.at[which, span, :],
            send_sem=out_send.at[to, b], recv_sem=out_recv.at[which, b],
            device_id=totals[to], device_id_type=MESH,
        )

    totals = [(((1 - y) * batches + seq), ka), (mate, ka), (diagonal, ka)]

    def total_copy(i):
        return remote(total_in.at[seq], total_in.at[seq], total_send.at[i], total_recv.at[seq], totals[i])

    def turned_copy(slot, b):
        end = 0 if slot == 0 else last
        return remote(
            turned.at[slot, b], turned_in.at[z - 1, b], pz_send.at[slot, b], pz_recv.at[z - 1, b],
            (pb, end * 2 + x),
        )

    def gradient(xb):
        product = jnp.zeros((DS, rows), jnp.float32)
        for start in range(0, 2 * rows, STEP):
            at = slice(start, start + STEP)
            col = col_level[at, :]
            weight = (
                w_row[xb, at, :]
                + jnp.exp2(s_sc[xb, at, :] - col[:, 1:2])
                - jnp.exp2(t_sc[xb, at, :] - col[:, 0:1])
            )
            high_part, low_part = split(weight)
            w_high[at, :] = high_part
            w_low[at, :] = low_part
            first = nn(q_tr[:, at], high_part)
            product = product + (first[:DS] + first[DS:] + nn(q_tr[0:DS, at], low_part))
        for b in range(blocks):
            part[xb, b] = product[:, b * LANES:(b + 1) * LANES]

    def turn_back(xb):
        back = nn(w_high[...], row_n[xb])
        back = back[:, :DS] + back[:, DS:] + nn(w_low[...], row_n[xb, :, 0:DS])
        for slot in range(2):
            for b in range(blocks):
                start = slot * rows + b * LANES
                piece = back[start:start + LANES]
                turned[slot, b] = jnp.where(xb == x, turned[slot, b] + piece, piece)

    def both_gradients(step, carry):
        xb = jnp.where(step == 0, 1 - x, x)
        gradient(xb)

        @pl.when(step == 0)
        def _():
            for b in range(blocks):
                px_copy(b).start()

        @pl.when(turning)
        def _():
            turn_back(xb)
        return carry

    lax.fori_loop(0, passes, both_gradients, 0)

    @pl.when(turning)
    def _():
        for b in range(blocks):
            for slot in range(2):
                turned_copy(slot, b).start()

    for b in range(blocks):
        @pl.when(active)
        def _():
            px_copy(b).wait_recv()
            x_sum[b] = part[x, b] + x_in[b]

        @pl.when(outer_end)
        def _():
            for level in range(2):
                landed(turned_in.at[level, b], pz_recv.at[level, b])
            x_sum[b] = x_sum[b] + (turned_in[0, b] + turned_in[1, b]).T

        @pl.when(inner_level)
        def _():
            py_copy(1, b).start()

    @pl.when(outer)
    def _():
        for step in range(1, levels):
            div_copy(step, (z - step + levels) % levels).wait_recv()
        total = div_in[0, 0:1, :]
        for level in range(1, levels):
            total = total + div_in[level, 0:1, :]
        total_in[seq] = jnp.broadcast_to(total, (8, rows))
        for i in range(3):
            total_copy(i).start()

    for b in range(blocks):
        span = slice(b * LANES, (b + 1) * LANES)

        @pl.when(inner_level)
        def _():
            py_copy(1, b).wait_recv()
            out_ref[seq, span, :] = (x_sum[b] + y_in[1, b]).T
            out_copy(seq, b, 1).start()

        @pl.when(outer_end)
        def _():
            out_ref[seq, span, :] = x_sum[b].T
            for to in range(3):
                out_copy(seq, b, to).start()

    landed(total_in.at[1 - seq], total_recv.at[1 - seq])

    @pl.when(jnp.logical_not(outer))
    def _():
        landed(total_in.at[seq], total_recv.at[seq])
    loss_ref[0, 0] = jnp.sum(total_in[0, 0:1, :] + total_in[1, 0:1, :]) / (
        batches * HEADS * rows * 2 * levels
    )

    @pl.when(outer)
    def _():
        for i in range(3):
            total_copy(i).wait_send()

    @pl.when(active)
    def _():
        for q in range(chunks):
            @pl.when(jnp.logical_or(end_level, q // half == y))
            def _():
                for copy in piece_copies(q, True):
                    copy.wait_send()

            @pl.when(jnp.logical_and(inner_level, q // half == y))
            def _():
                for copy in piece_copies(q, False):
                    copy.wait_send()

    def sent(j, carry):
        for slot in range(2):
            for to in range(levels):
                goes = source_sends(slot, to) if 0 < to < last else forwards(slot, to)

                @pl.when(goes)
                def _():
                    for copy in z_copies(slot, j, to):
                        copy.wait_send()
        return carry

    lax.fori_loop(0, chunks, sent, 0)
    for case, sends in kinds:
        @pl.when(case)
        def _():
            for copy in sends():
                copy.wait_send()

    @pl.when(outer)
    def _():
        for step in range(1, levels):
            div_copy(step, z).wait_send()

    for b in range(blocks):
        @pl.when(active)
        def _():
            px_copy(b).wait_send()

        @pl.when(turning)
        def _():
            for slot in range(2):
                turned_copy(slot, b).wait_send()

        @pl.when(inner_level)
        def _():
            py_copy(1, b).wait_send()

        @pl.when(active)
        def _():
            out_copy(seq, b, 1).wait_send()

        @pl.when(outer_end)
        def _():
            out_copy(seq, b, 0).wait_send()
            out_copy(seq, b, 2).wait_send()

        @pl.when(jnp.logical_not(active))
        def _():
            out_copy(seq, b, 1).wait_recv()
        out_copy(1 - seq, b, 1).wait_recv()


def solution(mesh):
    def shards(teacher_q, student_q):
        batches, rows = teacher_q.shape[0], teacher_q.shape[1]
        groups = mesh.shape["pb"] // batches
        levels = mesh.shape["ka"] // 2
        chunks = rows // CHUNK
        blocks = rows // LANES
        f32, bf16 = jnp.float32, jnp.bfloat16
        dma = pltpu.SemaphoreType.DMA
        folds = groups == 2 and levels == 4
        chosen = folded_kernel if folds else kernel
        scratch = [
            pltpu.VMEM((2, rows, DT), f32),
            pltpu.VMEM((2, rows, DS), f32),
            pltpu.VMEM((2, rows, DT), f32),
            pltpu.VMEM((2, rows, DS), f32),
            pltpu.VMEM((2, 3 * DT, rows), bf16),
            pltpu.VMEM((2, 3 * DS, rows), bf16),
            pltpu.VMEM((2, 2 * rows, rows), f32),
            pltpu.VMEM((2, 2 * rows, rows), f32),
            pltpu.VMEM((2, 5, 8, rows), f32),
        ]
        if folds:
            scratch.insert(2, pltpu.VMEM((2, rows, 2 * DS), bf16))
        scratch += [
            pltpu.VMEM((4, 2, 8, rows), f32),
            pltpu.VMEM((2, 4, 8, rows), f32),
            pltpu.VMEM((2 * rows, 8), f32),
            pltpu.VMEM((levels, 8, rows), f32),
            pltpu.VMEM((2, 2, rows), f32),
            pltpu.VMEM((2 * rows, 8), f32),
            pltpu.VMEM((2, 2 * rows, rows), f32),
            pltpu.VMEM((2 * DS, 2 * rows), bf16),
            pltpu.VMEM((2 * rows, rows), bf16),
            pltpu.VMEM((2 * rows, rows), bf16),
            pltpu.VMEM((2, blocks, DS, LANES), f32),
            pltpu.VMEM((blocks, DS, LANES), f32),
            pltpu.VMEM((blocks, DS, LANES), f32),
            pltpu.VMEM((groups, blocks, DS, LANES), f32),
            pltpu.VMEM((2, blocks, LANES, DS), f32),
            pltpu.VMEM((2, blocks, LANES, DS), f32),
            pltpu.VMEM((batches, 8, rows), f32),
            dma((2,)),
            dma((2, 2)),
            dma((2, chunks, 2)),
            dma((chunks, 2)),
            dma((levels, 2, chunks, 2)),
            dma((2, chunks, 2)),
            dma((4,)),
            dma((4,)),
            dma((2, 4)),
            dma((2, 2)),
            dma((2, 4)),
            dma((2, 4)),
            dma((levels,)),
            dma((levels,)),
            dma((blocks,)),
            dma((blocks,)),
            dma((groups, blocks)),
            dma((groups, blocks)),
            dma((2, blocks)),
            dma((2, blocks)),
            dma((3, blocks)),
            dma((2, blocks)),
            dma((3,)),
            dma((2,)),
        ] if folds else [
            pltpu.VMEM((2 * groups, 2, 8, rows), f32),
            pltpu.VMEM((2, 2 * groups, 8, rows), f32),
            pltpu.VMEM((levels, 8, rows), f32),
            pltpu.VMEM((2, 2, rows), f32),
            pltpu.VMEM((2 * rows, 8), f32),
            pltpu.VMEM((2, 2 * rows, rows), f32),
            pltpu.VMEM((2 * DS, 2 * rows), bf16),
            pltpu.VMEM((2 * rows, rows), bf16),
            pltpu.VMEM((2 * rows, rows), bf16),
            pltpu.VMEM((2, blocks, DS, LANES), f32),
            pltpu.VMEM((blocks, DS, LANES), f32),
            pltpu.VMEM((blocks, DS, LANES), f32),
            pltpu.VMEM((groups, blocks, DS, LANES), f32),
            pltpu.VMEM((batches, 8, rows), f32),
            dma((2,)),
            dma((2, 2)),
            dma((2,)),
            dma((2,)),
            dma((levels, 2, chunks, 2)),
            dma((2, chunks, 2)),
            dma((2 * groups,)),
            dma((2 * groups,)),
            dma((2, levels)),
            dma((2, 2 * groups)),
            dma((levels,)),
            dma((levels,)),
            dma((blocks,)),
            dma((blocks,)),
            dma((groups, blocks)),
            dma((groups, blocks)),
            dma((blocks,)),
            dma((blocks,)),
            dma,
            dma,
        ]
        grad, loss = pl.pallas_call(
            functools.partial(chosen, groups, levels, rows, batches),
            out_shape=(
                jax.ShapeDtypeStruct((batches, rows, DS), f32),
                jax.ShapeDtypeStruct((1, 1), f32),
            ),
            in_specs=[pl.BlockSpec(memory_space=pl.ANY)] * 2,
            out_specs=(
                pl.BlockSpec(memory_space=pltpu.VMEM),
                pl.BlockSpec(memory_space=pltpu.SMEM),
            ),
            scratch_shapes=scratch,
            compiler_params=pltpu.CompilerParams(
                collective_id=1 if folds else 0, has_side_effects=True, vmem_limit_bytes=40 * 1024 * 1024
            ),
        )(pltpu.with_memory_space_constraint(teacher_q, pltpu.HBM), pltpu.with_memory_space_constraint(student_q, pltpu.HBM))
        return grad, loss.reshape(())

    in_specs = (P(None, "ka", None), P(None, "ka", None))
    out_specs = (P(None, "ka", None), P())
    return jax.shard_map(shards, mesh=mesh, in_specs=in_specs, out_specs=out_specs, check_vma=False)
```
